128 devices in a mesh: row: 8 (over z, y_hi), col: 16 (over y_lo, x, core).
Axes of the slice: x: 4, y: 4 (y_hi: 2, y_lo: 2; y = y_hi * 2 + y_lo), z: 4, core: 2. Of those that a mesh axis runs over, the one named last changes fastest.
Arguments:
- features: bfloat16 [131072, 128], P(('row', 'col')), may hold values from -6 to 6
- weight_self: bfloat16 [128, 256], replicated, may hold values from -0.5 to 0.5
- weight_neigh: bfloat16 [128, 256], replicated, may hold values from -0.5 to 0.5
- bias_term: float32 [256], replicated, may hold values from -3 to 3
- upstream: bfloat16 [131072, 256], P(('row', 'col')), may hold values from -6 to 6
- tile_values: bfloat16 [8, 16, 128, 256, 256], P('row', 'col'), may hold values from -0.1875 to 0.1875
- block_pairs: int32 [8, 16, 128, 2], P('row', 'col'), may hold values from 0 to 63, as said below
- tile_counts: int32 [8, 16], P('row', 'col'), may hold values from 16 to 128, as said below
Outputs:
- hidden_out: bfloat16 [131072, 256], P(('row', 'col'))
- grad_features: bfloat16 [131072, 128], P(('row', 'col'))
- grad_self_weight: float32 [128, 256], replicated
- grad_neigh_weight: float32 [128, 256], replicated
The draws below stay inside these ranges and needn't reach their ends.
Inputs may be any that keep to these rules, and one draw needn't show every extreme that they name: `block_pairs`: within one grid cell all 128 slots name distinct block pairs; destination indices are below 8 * 4 and source indices below 16 * 4. Slots from tile_counts on are ignored. `tile_counts`: some grid cell uses all 128 slots in every draw.
All inputs are finite; a program needn't handle non-finite values.
Results may differ from the reference program's by a relative error of at most 0.0061.
Values may be sent and summed in bfloat16 or wider, within the bound.
No kernel may reach another device: no remote copies, remote signals or barrier semaphores. Data moves between devices by JAX's collectives and lax.ppermute only.
A program may use at most 192 MiB of HBM per device.

```python
import jax
import jax.numpy as jnp
from jax import lax

F = 128
H = 256
TILE = 256
NB_DEV = 4
MAXB = 128
NODES = 131072
N_ROW = 8
N_COL = 16


def draw_block_pairs(key, part):
    key = jax.random.fold_in(key, 11)
    cells = N_ROW * N_COL
    positions = N_ROW * NB_DEV * N_COL * NB_DEV
    keys = jax.random.split(key, cells)

    def pick_one(cell_key):
        return jax.random.permutation(cell_key, positions)[:MAXB].astype(jnp.int32)
    picks = jax.vmap(pick_one)(keys)
    target = picks // (N_COL * NB_DEV)
    source = picks % (N_COL * NB_DEV)
    return jnp.stack([target, source], axis=-1).reshape(N_ROW, N_COL, MAXB, 2).astype(jnp.int32)


def draw_tile_counts(key, part):
    key = jax.random.fold_in(key, 12)
    first_key, second_key = jax.random.split(key)
    cells = N_ROW * N_COL
    lowest = max(MAXB // 8, 1)
    values = jax.random.randint(first_key, (cells,), lowest, MAXB + 1, dtype=jnp.int32)
    fullest = jax.random.randint(second_key, (), 0, cells, dtype=jnp.int32)
    values = values.at[fullest].set(MAXB)
    return values.reshape(N_ROW, N_COL).astype(jnp.int32)


def block_levels(rng, shape, shards, least, top_value):
    def one(dim, shards_of):
        draws = jax.random.uniform(jax.random.fold_in(jax.random.fold_in(rng, 6), dim), (shards_of,), jnp.float32, least / len(shards), top_value / len(shards))
        return jnp.repeat(jnp.exp(draws), shape[dim] // shards_of).reshape((-1,) + (1,) * (len(shape) - dim - 1))

    loudness = one(*shards[0])
    for cut in shards[1:]:
        loudness = loudness * one(*cut)
    return loudness


def centred(own_key, dims, width, bound, pieces=(), held_as=jnp.bfloat16):
    level = block_levels(own_key, dims, pieces, -0.22, 0.18) if pieces else 1.0
    entries = jax.random.normal(own_key, dims, jnp.float32) * width * level
    return jnp.minimum(jnp.maximum(entries, -bound), bound).astype(held_as)


def setup_inputs(seed: int = 0) -> dict:
    seeds = jax.random.split(jax.random.key(seed), 9)
    features = centred(seeds[0], (NODES, F), 1.0, 6.0, ((0, 128),))
    weight_self = centred(seeds[1], (F, H), F ** -0.5, 0.5)
    weight_neigh = centred(seeds[2], (F, H), F ** -0.5, 0.5)
    bias_term = centred(seeds[3], (H,), 0.5, 3.0, (), jnp.float32)
    upstream = centred(seeds[4], (NODES, H), 1.0, 6.0, ((0, 128),))
    tile_values = centred(seeds[5], (N_ROW, N_COL, MAXB, TILE, TILE), (max(TILE * MAXB // (NB_DEV * N_ROW), TILE)) ** -0.5, 0.1875, ((0, 8), (1, 16)))
    block_pairs = draw_block_pairs(jax.random.fold_in(seeds[8], 71), 0)
    tile_counts = draw_tile_counts(jax.random.fold_in(seeds[8], 71), 0)
    return dict(features=features, weight_self=weight_self, weight_neigh=weight_neigh, bias_term=bias_term, upstream=upstream, tile_values=tile_values, block_pairs=block_pairs, tile_counts=tile_counts)


def locate(device, pairs):
    grid_row = device // N_COL
    grid_col = device % N_COL
    source = (grid_row * N_COL * NB_DEV + pairs[:, 1]).astype(jnp.int32)
    target = (((pairs[:, 0] // NB_DEV) * N_COL + grid_col) * NB_DEV + pairs[:, 0] % NB_DEV).astype(jnp.int32)
    return source, target


def reference(features, weight_self, weight_neigh, bias_term, upstream, tile_values, block_pairs, tile_counts):
    block_total = NODES // TILE
    cells = N_ROW * N_COL
    tiles_flat = tile_values.reshape(cells, MAXB, TILE, TILE)
    pairs_flat = block_pairs.reshape(cells, MAXB, 2)
    counts_flat = tile_counts.reshape(cells)
    devices = jnp.arange(cells, dtype=jnp.int32)
    slots = jnp.arange(MAXB, dtype=jnp.int32)
    feat_blocks = features.reshape(block_total, TILE, F)

    def forward_step(total, item):
        device, tiles, pairs, count = item
        source, target = locate(device, pairs)
        valid = (slots < count).astype(jnp.float32)
        terms = jnp.einsum("stu,suf->stf", tiles.astype(jnp.float32), feat_blocks[source].astype(jnp.float32))
        return total.at[target].add(terms * valid[:, None, None]), None

    zero_agg = jnp.zeros((block_total, TILE, F), jnp.float32)
    summed, _ = lax.scan(forward_step, zero_agg, (devices, tiles_flat, pairs_flat, counts_flat))
    aggregated = summed.reshape(NODES, F).astype(jnp.bfloat16)
    pre_act = (jnp.dot(features, weight_self, preferred_element_type=jnp.float32)
               + jnp.dot(aggregated, weight_neigh, preferred_element_type=jnp.float32) + bias_term)
    hidden_out = jax.nn.silu(pre_act).astype(jnp.bfloat16)
    sig_value = jax.nn.sigmoid(pre_act)
    slope = sig_value * (1.0 + pre_act * (1.0 - sig_value))
    dpre = (upstream.astype(jnp.float32) * slope).astype(jnp.bfloat16)
    grad_scale = float(NODES) ** -0.5
    grad_self_weight = jnp.dot(features.T, dpre, preferred_element_type=jnp.float32) * grad_scale
    grad_neigh_weight = jnp.dot(aggregated.T, dpre, preferred_element_type=jnp.float32) * grad_scale
    dz_value = jnp.dot(dpre, weight_neigh.T, preferred_element_type=jnp.float32).astype(jnp.bfloat16)
    dz_blocks = dz_value.reshape(block_total, TILE, F)

    def backward_step(total, item):
        device, tiles, pairs, count = item
        source, target = locate(device, pairs)
        valid = (slots < count).astype(jnp.float32)
        terms = jnp.einsum("stu,stf->suf", tiles.astype(jnp.float32), dz_blocks[target].astype(jnp.float32))
        return total.at[source].add(terms * valid[:, None, None]), None

    back_sum, _ = lax.scan(backward_step, zero_agg, (devices, tiles_flat, pairs_flat, counts_flat))
    grad_features = (jnp.dot(dpre, weight_self.T, preferred_element_type=jnp.float32)
                     + back_sum.reshape(NODES, F)).astype(jnp.bfloat16)
    return hidden_out, grad_features, grad_self_weight, grad_neigh_weight
```

```python
import functools

import jax
import jax.numpy as jnp
from jax import lax
from jax.experimental import pallas as pl
from jax.experimental.pallas import tpu as pltpu
from jax.sharding import PartitionSpec as P

TILE = 256
VMEM = pltpu.VMEM
BF16 = jnp.bfloat16
F32 = jnp.float32
LIMIT = 28 * 1024 * 1024


def hop_col(value, dy, dx, dc=0):
    pairs = []
    for y in range(2):
        for x in range(4):
            for c in range(2):
                to = (((y + dy) % 2) * 4 + (x + dx) % 4) * 2 + (c + dc) % 2
                pairs.append(((y * 4 + x) * 2 + c, to))
    return lax.ppermute(value, "col", pairs)


def hop_row(value, dy, dz):
    pairs = []
    for z in range(4):
        for y in range(2):
            pairs.append((z * 2 + y, ((z + dz) % 4) * 2 + (y + dy) % 2))
    return lax.ppermute(value, "row", pairs)


def hop_diag(value):
    pairs = []
    for r in range(8):
        for c in range(16):
            pairs.append((r * 16 + c, (r ^ 1) * 16 + (c ^ 8)))
    return lax.ppermute(value, ("row", "col"), pairs)


def in_vmem(*values):
    return [pltpu.with_memory_space_constraint(v, VMEM) for v in values]


def vmem_specs(n):
    return [pl.BlockSpec(memory_space=VMEM)] * n


def call(body, outs, vmem_args, smem_args=(), scratch=(), flops=0, nbytes=0, limit=LIMIT):
    single = not isinstance(outs, (list, tuple))
    specs = [pl.BlockSpec(memory_space=pltpu.SMEM)] * len(smem_args) + vmem_specs(len(vmem_args))
    return pl.pallas_call(
        body,
        out_shape=outs,
        in_specs=specs,
        out_specs=pl.BlockSpec(memory_space=VMEM) if single else vmem_specs(len(outs)),
        scratch_shapes=list(scratch),
        compiler_params=pltpu.CompilerParams(vmem_limit_bytes=limit),
        cost_estimate=pl.CostEstimate(flops=flops, bytes_accessed=nbytes, transcendentals=0),
    )(*smem_args, *in_vmem(*vmem_args))


def gather_halves(lo, hi, whole, step, swap):
    l_lo = step(lo, 1)
    r_hi = step(hi, -1)
    other = swap(whole)
    l_hi = step(hi, 1)
    r_lo = step(lo, -1)
    o_lo = step(l_lo, 1)
    o_hi = step(r_hi, -1)
    y_l = step(other, 1)
    y_r = step(other, -1)
    yo_lo = swap(o_lo)
    yo_hi = swap(o_hi)
    return {
        (0, 0): [whole],
        (0, 3): [l_lo, l_hi],
        (0, 1): [r_lo, r_hi],
        (0, 2): [o_lo, o_hi],
        (1, 0): [other],
        (1, 3): [y_l],
        (1, 1): [y_r],
        (1, 2): [yo_lo, yo_hi],
    }


def places():
    col = lax.axis_index("col")
    row = lax.axis_index("row")
    return col, row


def source_slot(s, col):
    c = s >> 2
    away = (c ^ col) & 9
    dx = ((c >> 1) - (col >> 1)) & 3
    return ((away & 1) << 5) | ((away >> 3) << 4) | (dx << 2) | (s & 3)


def target_slot(d, row):
    q = d >> 2
    dz = ((q >> 1) - (row >> 1)) & 3
    return (((q ^ row) & 1) << 4) | (dz << 2) | (d & 3)


def over_slots(count, step):
    group = 4

    def many(i, carry):
        step([i * group + k for k in range(group)])
        return carry

    def one(i, carry):
        step([i])
        return carry

    full = count // group
    lax.fori_loop(0, full, many, 0)
    lax.fori_loop(full * group, count, one, 0)


def forward_body(places_in, pairs, count, tiles, *rest):
    parts = rest[: len(places_in)]
    outs = rest[len(places_in) : len(places_in) + 8]
    held, total = rest[len(places_in) + 8 :]
    col, row = places()
    for ref, (start, size) in zip(parts, places_in):
        held[start : start + size] = ref[...].reshape(size, TILE, 128)
    total[...] = jnp.zeros_like(total)

    def step(slots):
        news = []
        for i in slots:
            d = target_slot(pairs[2 * i], row)
            s = source_slot(pairs[2 * i + 1], col)
            news.append((d, jnp.dot(tiles[i], held[s], preferred_element_type=F32)))
        for d, new in news:
            total[d] += new

    over_slots(count[0], step)
    for k in range(8):
        outs[k][...] = total[4 * k : 4 * k + 4].reshape(1024, 128).astype(BF16)


def backward_body(widths, pairs, count, tiles, *rest):
    n = len(widths)
    parts = rest[:n]
    sib = rest[n]
    outs = rest[n + 1 : n + 9]
    held, total = rest[n + 9 :]
    col, row = places()
    at = 0
    for ref, blocks in zip(parts, widths):
        for b in range(blocks):
            held[at] = ref[:, b * TILE : (b + 1) * TILE]
            at += 1
    total[...] = jnp.zeros_like(total)

    def step(slots):
        news = []
        for i in slots:
            d = target_slot(pairs[2 * i], row)
            s = source_slot(pairs[2 * i + 1], col)
            news.append((s, jnp.dot(held[d], tiles[i], preferred_element_type=F32)))
        for s, new in news:
            total[s] += new

    over_slots(count[0], step)
    for k in range(8):
        for b in range(4):
            outs[k][:, b * TILE : (b + 1) * TILE] = total[4 * k + b].astype(BF16)
            sib[k, :, b * TILE : (b + 1) * TILE] = total[32 + 4 * k + b].astype(BF16)


def add_body(sib, *rest):
    for k in range(8):
        rest[8 + k][...] = (rest[k][...].astype(F32) + sib[k].astype(F32)).astype(BF16)


def dense_body(bias, feats, upstream, w_self, w_neigh, *rest):
    sums = rest[:8]
    hidden, dpre_out, agg_out, dz_whole, dz_lo, dz_hi = rest[8:]
    for b in range(4):
        rows = slice(b * TILE, (b + 1) * TILE)
        agg = sums[0][rows].astype(F32)
        for k in range(1, 8):
            agg = agg + sums[k][rows].astype(F32)
        agg = agg.astype(BF16)
        agg_out[rows] = agg
        pre = jnp.dot(feats[rows], w_self[...], preferred_element_type=F32)
        pre = pre + jnp.dot(agg, w_neigh[...], preferred_element_type=F32) + bias[...]
        sig = jax.nn.sigmoid(pre)
        hidden[rows] = (pre * sig).astype(BF16)
        slope = sig * (1.0 + pre * (1.0 - sig))
        dpre = (upstream[rows].astype(F32) * slope).astype(BF16)
        dpre_out[rows] = dpre
        dz = lax.dot_general(
            w_neigh[...], dpre, (((1,), (1,)), ((), ())), preferred_element_type=F32
        ).astype(BF16)
        dz_whole[:, rows] = dz
        half = slice((b % 2) * TILE, (b % 2 + 1) * TILE)
        if b < 2:
            dz_lo[:, half] = dz
        else:
            dz_hi[:, half] = dz


def weights_body(feats, agg, dpre, w_self, keep, send, own_grad):
    over_nodes = (((0,), (0,)), ((), ()))
    grad_self = lax.dot_general(feats[...], dpre[...], over_nodes, preferred_element_type=F32)
    grad_neigh = lax.dot_general(agg[...], dpre[...], over_nodes, preferred_element_type=F32)
    first = lax.axis_index("col") % 2 == 0

    @pl.when(first)
    def _():
        keep[...] = grad_self
        send[...] = grad_neigh

    @pl.when(jnp.logical_not(first))
    def _():
        keep[...] = grad_neigh
        send[...] = grad_self

    own_grad[...] = lax.dot_general(
        w_self[...], dpre[...], (((1,), (1,)), ((), ())), preferred_element_type=F32
    )


def finish_body(own_grad, *rest):
    out = rest[-1]
    for b in range(4):
        nodes = slice(b * TILE, (b + 1) * TILE)
        total = own_grad[:, nodes]
        for k in range(8):
            total = total + rest[k][:, nodes].astype(F32)
        out[nodes] = total.T.astype(BF16)


def ring_place(axis):
    col, row = places()
    return (col >> 1) & 3 if axis == "x" else row >> 1


def sum_split_body(axis, n_in, *rest):
    ins, outs = rest[:n_in], rest[n_in : n_in + 4]
    held = rest[n_in + 4]
    total = ins[0][...]
    for ref in ins[1:]:
        total = total + ref[...]
    held[...] = total
    me = ring_place(axis)
    size = outs[0].shape[0]
    for k in range(4):
        at = pl.multiple_of(((me + k) & 3) * size, size)
        outs[k][...] = held[pl.ds(at, size), :]


def sum_body(*rest):
    total = rest[0][...]
    for ref in rest[1:-1]:
        total = total + ref[...]
    rest[-1][...] = total


def pair_sum_body(a, b, c, d, out):
    out[...] = (a[...] + b[...]) + (c[...] + d[...])


def join_body(axis, *rest):
    me = ring_place(axis)
    out = rest[4]
    size = rest[0].shape[0]
    for k in range(4):
        at = pl.multiple_of(((me + k) & 3) * size, size)
        out[pl.ds(at, size), :] = rest[k][...]


def place_body(scale, mine, other, grad_self, grad_neigh):
    first = lax.axis_index("col") % 2 == 0
    a = mine[...] * scale
    b = other[...] * scale
    grad_self[...] = jnp.where(first, a, b)
    grad_neigh[...] = jnp.where(first, b, a)


def sum_weights(keep, send, scale):
    def f32(rows):
        return VMEM((rows, 256), F32)

    got = hop_col(send, 0, 0, 1)
    pieces = call(
        functools.partial(sum_split_body, "x", 2), [f32(32)] * 4, [keep, got], scratch=[f32(128)]
    )
    got = [pieces[0]] + [hop_col(pieces[k], 0, k) for k in (1, 2, 3)]
    pieces = call(
        functools.partial(sum_split_body, "z", 4), [f32(8)] * 4, got, scratch=[f32(32)]
    )
    got = [pieces[0]] + [hop_row(pieces[k], 0, k) for k in (1, 2, 3)]
    part = call(sum_body, f32(8), got)
    whole = call(
        pair_sum_body, f32(8), [part, hop_col(part, 1, 0), hop_row(part, 1, 0), hop_diag(part)]
    )
    got = [whole] + [hop_row(whole, 0, -k) for k in (1, 2, 3)]
    quarter = call(functools.partial(join_body, "z"), f32(32), got)
    got = [quarter] + [hop_col(quarter, 0, -k) for k in (1, 2, 3)]
    half = call(functools.partial(join_body, "x"), f32(128), got)
    other = hop_col(half, 0, 0, 1)
    shape = jax.ShapeDtypeStruct((128, 256), F32)
    return call(functools.partial(place_body, scale), [shape, shape], [half, other])


def shards(
    features, weight_self, weight_neigh, bias_term, upstream, tile_values, block_pairs, tile_counts
):
    tiles = tile_values.reshape(tile_values.shape[2:])
    pairs = block_pairs.reshape(-1)
    count = tile_counts.reshape(-1)
    nodes = 131072

    with jax.named_scope("gather_features"):
        got = gather_halves(
            features[:512],
            features[512:],
            features,
            lambda v, d: hop_col(v, 0, d),
            lambda v: hop_col(v, 1, 0),
        )
        parts, where = [], []
        for core in range(2):
            for (y, x), pieces in got.items():
                at = (core * 8 + y * 4 + x) * 4
                for piece in pieces:
                    size = piece.shape[0] // TILE
                    parts.append(hop_col(piece, 0, 0, 1) if core else piece)
                    where.append((at, size))
                    at += size
    with jax.named_scope("forward_tiles"):
        partial = call(
            functools.partial(forward_body, where),
            [VMEM((1024, 128), BF16)] * 8,
            [tiles, *parts],
            [pairs, count],
            [VMEM((64, TILE, 128), BF16), VMEM((32, TILE, 128), F32)],
            flops=128 * 2 * TILE * TILE * 128,
            nbytes=24 << 20,
        )
    with jax.named_scope("sum_aggregates"):
        sums = [partial[0]]
        for y in range(2):
            for z in range(4):
                if y or z:
                    sums.append(hop_row(partial[y * 4 + z], y, z))
    with jax.named_scope("dense"):
        bias = bias_term.reshape(1, 256)
        hidden, dpre, agg, dz_whole, dz_lo, dz_hi = call(
            dense_body,
            [
                jax.ShapeDtypeStruct((1024, 256), BF16),
                VMEM((1024, 256), BF16),
                VMEM((1024, 128), BF16),
                VMEM((128, 1024), BF16),
                VMEM((128, 512), BF16),
                VMEM((128, 512), BF16),
            ],
            [bias, features, upstream, weight_self, weight_neigh, *sums],
            flops=3 * 2 * 1024 * 128 * 256,
            nbytes=6 << 20,
        )
    with jax.named_scope("gather_dz"):
        got = gather_halves(
            dz_lo, dz_hi, dz_whole, lambda v, d: hop_row(v, 0, d), lambda v: hop_row(v, 1, 0)
        )
        parts, widths = [], []
        for y in range(2):
            for z in range(4):
                for piece in got[y, z]:
                    parts.append(piece)
                    widths.append(piece.shape[1] // TILE)
    with jax.named_scope("weights"):
        keep, send, own_grad = call(
            weights_body,
            [VMEM((128, 256), F32), VMEM((128, 256), F32), VMEM((128, 1024), F32)],
            [features, agg, dpre, weight_self],
            flops=3 * 2 * 1024 * 128 * 256,
            nbytes=2 << 20,
        )
        grad_self, grad_neigh = sum_weights(keep, send, float(nodes) ** -0.5)
    with jax.named_scope("backward_tiles"):
        sib, *mine = call(
            functools.partial(backward_body, widths),
            [VMEM((8, 128, 1024), BF16)] + [VMEM((128, 1024), BF16)] * 8,
            [tiles, *parts],
            [pairs, count],
            [VMEM((32, 128, TILE), BF16), VMEM((64, 128, TILE), F32)],
            flops=128 * 2 * TILE * TILE * 128,
            nbytes=24 << 20,
        )
    with jax.named_scope("sum_grads"):
        sib = hop_col(sib, 0, 0, 1)
        mine = call(add_body, [VMEM((128, 1024), BF16)] * 8, [sib, *mine], nbytes=6 << 20)
        sums = [mine[0]]
        for y in range(2):
            for x in range(4):
                if y or x:
                    sums.append(hop_col(mine[y * 4 + x], y, x))
    with jax.named_scope("finish"):
        grad_features = call(
            finish_body,
            jax.ShapeDtypeStruct((1024, 128), BF16),
            [own_grad, *sums],
            nbytes=4 << 20,
        )
    return hidden, grad_features, grad_self, grad_neigh


def solution(mesh):
    placed = (
        P(("row", "col"), None),
        P(),
        P(),
        P(),
        P(("row", "col"), None),
        P("row", "col", None, None, None),
        P("row", "col", None, None),
        P("row", "col"),
    )
    return jax.shard_map(
        shards,
        mesh=mesh,
        in_specs=placed,
        out_specs=(P(("row", "col"), None), P(("row", "col"), None), P(), P()),
        check_vma=False,
    )
```

```python
import functools

import jax
import jax.numpy as jnp
from jax import lax
from jax.experimental import pallas as pl
from jax.experimental.pallas import tpu as pltpu
from jax.sharding import PartitionSpec as P

TILE = 256
VMEM = pltpu.VMEM
BF16 = jnp.bfloat16
F32 = jnp.float32
LIMIT = 12 * 1024 * 1024
GROUP = 16
ROOM = 144

ORDER = [(0, 0), (0, 3), (0, 1), (1, 0), (0, 2), (1, 3), (1, 1), (1, 2)]
OWN, LEFT, RIGHT, PAIR, OPPOSITE, PAIR_LEFT, PAIR_RIGHT, PAIR_OPPOSITE = range(8)
PLACE = sum(ORDER.index((k // 4, k % 4)) << (4 * k) for k in range(8))


def hop_col(value, dy, dx, dc=0):
    pairs = []
    for y in range(2):
        for x in range(4):
            for c in range(2):
                to = (((y + dy) % 2) * 4 + (x + dx) % 4) * 2 + (c + dc) % 2
                pairs.append(((y * 4 + x) * 2 + c, to))
    return lax.ppermute(value, "col", pairs)


def hop_row(value, dy, dz):
    pairs = []
    for z in range(4):
        for y in range(2):
            pairs.append((z * 2 + y, ((z + dz) % 4) * 2 + (y + dy) % 2))
    return lax.ppermute(value, "row", pairs)


def hop_diag(value):
    pairs = []
    for r in range(8):
        for c in range(16):
            pairs.append((r * 16 + c, (r ^ 1) * 16 + (c ^ 8)))
    return lax.ppermute(value, ("row", "col"), pairs)


def in_vmem(*values):
    return [pltpu.with_memory_space_constraint(v, VMEM) for v in values]


def vmem_specs(n):
    return [pl.BlockSpec(memory_space=VMEM)] * n


def call(body, outs, vmem_args, smem_args=(), after=(), scratch=(), alias=None, flops=0, nbytes=0):
    single = not isinstance(outs, (list, tuple))
    skip = len(smem_args) + len(vmem_args)

    def run(*refs):
        body(*refs[:skip], *refs[skip + len(after) :])

    return pl.pallas_call(
        run,
        out_shape=outs,
        in_specs=[pl.BlockSpec(memory_space=pltpu.SMEM)] * len(smem_args)
        + vmem_specs(len(vmem_args))
        + [pl.BlockSpec(memory_space=pl.ANY)] * len(after),
        out_specs=pl.BlockSpec(memory_space=VMEM) if single else vmem_specs(len(outs)),
        scratch_shapes=list(scratch),
        input_output_aliases=alias or {},
        compiler_params=pltpu.CompilerParams(vmem_limit_bytes=LIMIT),
        cost_estimate=pl.CostEstimate(flops=flops, bytes_accessed=nbytes, transcendentals=0),
    )(*smem_args, *in_vmem(*vmem_args), *after)


def places():
    return lax.axis_index("col"), lax.axis_index("row")


def first_round(value, step, swap):
    return [value, step(value, 1), step(value, -1), swap(value), step(value, 2)]


def second_round(near, step, swap):
    return [step(near[PAIR], 1), step(near[PAIR], -1), swap(near[OPPOSITE])]


def place_of(index, me, other_bit, ring_shift):
    other = ((index ^ me) >> other_bit) & 1
    offset = ((index >> ring_shift) - (me >> ring_shift)) & 3
    return (PLACE >> ((other * 4 + offset) * 4)) & 15


def plan_body(pairs, count, tiles, held, lists, sizes, sems):
    copies = []
    for k in range(8):
        part = pl.ds(16 * k, 16)
        copies.append(pltpu.make_async_copy(tiles.at[part], held.at[part], sems.at[k]))
        copies[-1].start()
    col, row = places()
    for k in range(8):
        sizes[k] = 0

    def put(which, entry):
        at = sizes[which]
        lists[which * ROOM + at] = entry
        sizes[which] = at + 1

    def sort(i, carry):
        d = pairs[2 * i]
        s = pairs[2 * i + 1]
        c = s >> 2
        q = d >> 2
        sib = (c ^ col) & 1
        source = place_of(c, col, 3, 1) * 4 + (s & 3)
        target = place_of(q, row, 0, 1) * 4 + (d & 3)
        put((source >> 4) * 2 + sib, i | (target << 8) | ((source & 15) << 16))
        put(4 + (target >> 4) * 2 + sib, i | ((target & 15) << 8) | (source << 16))
        return carry

    lax.fori_loop(0, count[0], sort, 0)
    for k in range(8):
        at = sizes[k]
        for j in range(GROUP - 1):
            lists[k * ROOM + at + j] = 32 << 8 if k < 4 else 32 << 16
    for copy in copies:
        copy.wait()


def over_list(which, lists, sizes, product, total, to_target):
    def step(g, carry):
        news = []
        for j in range(GROUP):
            entry = lists[which * ROOM + g * GROUP + j]
            i = entry & 255
            d = (entry >> 8) & 255
            s = entry >> 16
            news.append((d if to_target else s, product(i, d, s)))
        for at, new in news:
            total[at] += new
        return carry

    lax.fori_loop(0, (sizes[which] + GROUP - 1) // GROUP, step, 0)


def pack_body(*rest):
    for k in range(4):
        rest[4][4 * k : 4 * k + 4] = rest[k][...].reshape(4, TILE, 128)
    for out in rest[5:]:
        out[...] = rest[PAIR][...]


def forward_step(lists, sizes, tiles, which, blocks, total):
    def product(i, d, s):
        return jnp.dot(tiles[i], blocks[s], preferred_element_type=F32)

    over_list(which, lists, sizes, product, total, True)


def forward_near_body(lists, sizes, tiles, mine, sib, total):
    total[...] = jnp.zeros_like(total)
    forward_step(lists, sizes, tiles, 0, mine, total)
    forward_step(lists, sizes, tiles, 1, sib, total)


def forward_far_body(lists, sizes, tiles, mine, before, total):
    forward_step(lists, sizes, tiles, 2, mine, total)


def forward_last_body(lists, sizes, tiles, sib, before, total, *outs):
    forward_step(lists, sizes, tiles, 3, sib, total)
    for k in range(8):
        outs[k][...] = total[4 * k : 4 * k + 4].reshape(1024, 128).astype(outs[k].dtype)


def hold_dz(parts, held):
    for k, ref in enumerate(parts):
        for b in range(4):
            held[4 * k + b] = ref[:, b * TILE : (b + 1) * TILE]


def backward_step(lists, sizes, tiles, which, held, total):
    def product(i, d, s):
        return jnp.dot(held[d], tiles[i], preferred_element_type=F32)

    over_list(which, lists, sizes, product, total, False)


def backward_near_body(lists, sizes, tiles, *rest):
    parts, (mine, sib, held) = rest[:4], rest[4:]
    hold_dz(parts, held)
    mine[...] = jnp.zeros_like(mine)
    sib[...] = jnp.zeros_like(sib)
    backward_step(lists, sizes, tiles, 5, held, sib)
    backward_step(lists, sizes, tiles, 4, held, mine)


def write_places(total, first, outs):
    for k, ref in enumerate(outs):
        for b in range(4):
            ref[:, b * TILE : (b + 1) * TILE] = total[4 * (first + k) + b].astype(ref.dtype)


def backward_sib_body(lists, sizes, tiles, *rest):
    parts, (before, sib, far, near, held) = rest[:4], rest[4:]
    hold_dz(parts, held)
    backward_step(lists, sizes, tiles, 7, held, sib)
    write_places(sib, PAIR_LEFT, [far.at[k] for k in range(3)])
    write_places(sib, OWN, [near.at[k] for k in range(5)])


def backward_mine_body(lists, sizes, tiles, *rest):
    parts, (before, mine, held) = rest[:4], rest[4:]
    hold_dz(parts, held)
    backward_step(lists, sizes, tiles, 6, held, mine)


def add_sib_body(first, mine, got, *outs):
    for k, ref in enumerate(outs):
        for b in range(4):
            nodes = slice(b * TILE, (b + 1) * TILE)
            new = mine[4 * (first + k) + b] + got[k, :, nodes].astype(F32)
            ref[:, nodes] = new.astype(ref.dtype)


def add_round_body(pair, opposite, a, b, c, pair_out, opposite_out):
    new = pair[...] + (a[...].astype(F32) + b[...].astype(F32))
    pair_out[...] = new.astype(BF16)
    opposite_out[...] = (opposite[...] + c[...].astype(F32)).astype(BF16)


def reduce_places(parts, step, swap, after=()):
    shape = parts[OWN].shape
    for_pair = [step(parts[PAIR_LEFT], -1), step(parts[PAIR_RIGHT], 1)]
    for_opposite = swap(parts[PAIR_OPPOSITE])
    left = step(parts[LEFT], -1)
    right = step(parts[RIGHT], 1)
    pair, opposite = call(
        add_round_body,
        [VMEM(shape, BF16)] * 2,
        [parts[PAIR], parts[OPPOSITE], *for_pair, for_opposite],
        after=after,
        nbytes=4 << 20,
    )
    return [parts[OWN], left, right, step(opposite, 2), swap(pair)]


def dense_body(bias, feats, upstream, w_self, w_neigh, *rest):
    sums = rest[:5]
    hidden, dpre_out, agg_out, dz_out = rest[5:]
    for b in range(4):
        rows = slice(b * TILE, (b + 1) * TILE)
        agg = sums[0][rows]
        for ref in sums[1:]:
            agg = agg + ref[rows].astype(F32)
        agg = agg.astype(BF16)
        agg_out[rows] = agg
        pre = jnp.dot(feats[rows], w_self[...], preferred_element_type=F32)
        pre = pre + jnp.dot(agg, w_neigh[...], preferred_element_type=F32) + bias[...]
        sig = jax.nn.sigmoid(pre)
        hidden[rows] = (pre * sig).astype(BF16)
        slope = sig * (1.0 + pre * (1.0 - sig))
        dpre = (upstream[rows].astype(F32) * slope).astype(BF16)
        dpre_out[rows] = dpre
        dz = lax.dot_general(
            w_neigh[...], dpre, (((1,), (1,)), ((), ())), preferred_element_type=F32
        ).astype(BF16)
        dz_out[:, rows] = dz


def weights_body(feats, agg, dpre, w_self, keep, send, own_grad):
    over_nodes = (((0,), (0,)), ((), ()))
    grad_self = lax.dot_general(feats[...], dpre[...], over_nodes, preferred_element_type=F32)
    grad_neigh = lax.dot_general(agg[...], dpre[...], over_nodes, preferred_element_type=F32)
    first = lax.axis_index("col") % 2 == 0

    @pl.when(first)
    def _():
        keep[...] = grad_self
        send[...] = grad_neigh

    @pl.when(jnp.logical_not(first))
    def _():
        keep[...] = grad_neigh
        send[...] = grad_self

    own_grad[...] = lax.dot_general(
        w_self[...], dpre[...], (((1,), (1,)), ((), ())), preferred_element_type=F32
    )


def finish_body(own_grad, *rest):
    out = rest[-1]
    for b in range(4):
        nodes = slice(b * TILE, (b + 1) * TILE)
        total = own_grad[:, nodes]
        for ref in rest[:-1]:
            total = total + ref[:, nodes].astype(F32)
        out[nodes] = total.T.astype(BF16)


def ring_place(axis):
    col, row = places()
    return (col >> 1) & 3 if axis == "x" else row >> 1


def sum_split_body(axis, n_in, *rest):
    ins, outs = rest[:n_in], rest[n_in : n_in + 4]
    held = rest[n_in + 4]
    total = ins[0][...]
    for ref in ins[1:]:
        total = total + ref[...]
    held[...] = total
    me = ring_place(axis)
    size = outs[0].shape[0]
    for k in range(4):
        at = pl.multiple_of(((me + k) & 3) * size, size)
        outs[k][...] = held[pl.ds(at, size), :]


def sum_body(*rest):
    total = rest[0][...]
    for ref in rest[1:-1]:
        total = total + ref[...]
    rest[-1][...] = total


def pair_sum_body(a, b, c, d, out):
    out[...] = (a[...] + b[...]) + (c[...] + d[...])


def join_body(axis, *rest):
    me = ring_place(axis)
    out = rest[4]
    size = rest[0].shape[0]
    for k in range(4):
        at = pl.multiple_of(((me + k) & 3) * size, size)
        out[pl.ds(at, size), :] = rest[k][...]


def place_body(scale, mine, other, grad_self, grad_neigh):
    first = lax.axis_index("col") % 2 == 0
    a = mine[...] * scale
    b = other[...] * scale
    grad_self[...] = jnp.where(first, a, b)
    grad_neigh[...] = jnp.where(first, b, a)


def sum_weights_down(keep, send, first):
    def f32(rows):
        return VMEM((rows, 256), F32)

    got = hop_col(send, 0, 0, 1)
    pieces = call(
        functools.partial(sum_split_body, "x", 2), [f32(32)] * 4, [keep, got], scratch=[f32(128)]
    )
    got = [pieces[0]] + [hop_col(pieces[k], 0, k) for k in (1, 2, 3)]
    pieces = call(
        functools.partial(sum_split_body, "z", 4),
        [f32(8)] * 4,
        got,
        after=[first],
        scratch=[f32(32)],
    )
    got = [pieces[0]] + [hop_row(pieces[k], 0, k) for k in (1, 2, 3)]
    part = call(sum_body, f32(8), got)
    whole = call(
        pair_sum_body, f32(8), [part, hop_col(part, 1, 0), hop_row(part, 1, 0), hop_diag(part)]
    )
    return pieces[0], whole


def gather_weights_rings(whole):
    def f32(rows):
        return VMEM((rows, 256), F32)

    got = [whole] + [hop_row(whole, 0, -k) for k in (1, 2, 3)]
    quarter = call(functools.partial(join_body, "z"), f32(32), got)
    got = [quarter] + [hop_col(quarter, 0, -k) for k in (1, 2, 3)]
    return quarter, call(functools.partial(join_body, "x"), f32(128), got)


def gather_weights_cores(half, scale):
    other = hop_col(half, 0, 0, 1)
    shape = jax.ShapeDtypeStruct((128, 256), F32)
    return call(functools.partial(place_body, scale), [shape, shape], [half, other])


def shards(
    features, weight_self, weight_neigh, bias_term, upstream, tile_values, block_pairs, tile_counts
):
    nodes = 131072
    tile_bytes = 128 * TILE * TILE * 2
    share = 32 * 2 * TILE * TILE * 128
    in_hbm = pltpu.with_memory_space_constraint(tile_values.reshape(128, TILE, TILE), pltpu.HBM)
    with jax.named_scope("plan"):
        tiles, lists, sizes = pl.pallas_call(
            plan_body,
            out_shape=[
                VMEM((128, TILE, TILE), BF16),
                pltpu.SMEM((8 * ROOM,), jnp.int32),
                pltpu.SMEM((8,), jnp.int32),
            ],
            in_specs=[pl.BlockSpec(memory_space=pltpu.SMEM)] * 2
            + [pl.BlockSpec(memory_space=pl.ANY)],
            out_specs=[pl.BlockSpec(memory_space=VMEM)]
            + [pl.BlockSpec(memory_space=pltpu.SMEM)] * 2,
            scratch_shapes=[pltpu.SemaphoreType.DMA((8,))],
            compiler_params=pltpu.CompilerParams(vmem_limit_bytes=LIMIT),
            cost_estimate=pl.CostEstimate(flops=0, bytes_accessed=tile_bytes, transcendentals=0),
        )(block_pairs.reshape(-1), tile_counts.reshape(-1), in_hbm)
    by_list = [lists, sizes]

    with jax.named_scope("gather_features"):
        step, swap = (lambda v, d: hop_col(v, 0, d)), (lambda v: hop_col(v, 1, 0))
        packed = VMEM((16, TILE, 128), BF16)
        near = first_round(features, step, swap)
        near_mine, near[PAIR] = call(
            pack_body, [packed, VMEM((1024, 128), BF16)], near[:4], after=[sizes], nbytes=2 << 20
        )
        far = [near[OPPOSITE], *second_round(near, step, swap)]
        near_sib = hop_col(near_mine, 0, 0, 1)
        far_mine = call(pack_body, packed, far, nbytes=2 << 20)
        far_sib = hop_col(far_mine, 0, 0, 1)
    with jax.named_scope("forward_tiles"):
        total = VMEM((33, TILE, 128), F32)
        sums = call(
            forward_near_body,
            total,
            [tiles, near_mine, near_sib],
            by_list,
            flops=2 * share,
            nbytes=tile_bytes // 2,
        )
        sums = call(
            forward_far_body,
            total,
            [tiles, far_mine, sums],
            by_list,
            alias={4: 0},
            flops=share,
            nbytes=tile_bytes // 4,
        )
        f32, bf16 = VMEM((1024, 128), F32), VMEM((1024, 128), BF16)
        _, *partial = call(
            forward_last_body,
            [total, f32, bf16, bf16, f32, f32, bf16, bf16, bf16],
            [tiles, far_sib, sums],
            by_list,
            alias={4: 0},
            flops=share,
            nbytes=tile_bytes // 4,
        )
    with jax.named_scope("sum_aggregates"):
        step, swap = (lambda v, d: hop_row(v, 0, d)), (lambda v: hop_row(v, 1, 0))
        sums = reduce_places(partial, step, swap)
    with jax.named_scope("dense"):
        hidden, dpre, agg, dz = call(
            dense_body,
            [
                jax.ShapeDtypeStruct((1024, 256), BF16),
                VMEM((1024, 256), BF16),
                VMEM((1024, 128), BF16),
                VMEM((128, 1024), BF16),
            ],
            [bias_term.reshape(1, 256), features, upstream, weight_self, weight_neigh, *sums],
            flops=3 * 2 * 1024 * 128 * 256,
            nbytes=6 << 20,
        )
    with jax.named_scope("gather_dz"):
        near = first_round(dz, step, swap)
        far = [near[OPPOSITE], *second_round(near, step, swap)]
    with jax.named_scope("weights"):
        keep, send, own_grad = call(
            weights_body,
            [VMEM((128, 256), F32), VMEM((128, 256), F32), VMEM((128, 1024), F32)],
            [features, agg, dpre, weight_self],
            flops=3 * 2 * 1024 * 128 * 256,
            nbytes=2 << 20,
        )
        early, whole = sum_weights_down(keep, send, near[PAIR])
    with jax.named_scope("backward_tiles"):
        total = VMEM((33, 128, TILE), F32)
        held = [VMEM((16, 128, TILE), BF16)]
        mine, sib = call(
            backward_near_body,
            [total, total],
            [tiles, *near[:4]],
            by_list,
            after=[early],
            scratch=held,
            flops=2 * share,
            nbytes=tile_bytes // 2,
        )
        _, sib_far, sib_near = call(
            backward_sib_body,
            [total, VMEM((3, 128, 1024), BF16), VMEM((5, 128, 1024), BF16)],
            [tiles, *far, sib],
            by_list,
            after=[whole],
            alias={7: 0},
            scratch=held,
            flops=share,
            nbytes=tile_bytes // 4,
        )
        mine = call(
            backward_mine_body,
            total,
            [tiles, *far, mine],
            by_list,
            scratch=held,
            alias={7: 0},
            flops=share,
            nbytes=tile_bytes // 4,
        )
    with jax.named_scope("gather_weights"):
        quarter, half = gather_weights_rings(whole)
        grad_self, grad_neigh = gather_weights_cores(half, float(nodes) ** -0.5)
    with jax.named_scope("sum_grads"):
        step, swap = (lambda v, d: hop_col(v, 0, d)), (lambda v: hop_col(v, 1, 0))
        f32, bf16 = VMEM((128, 1024), F32), VMEM((128, 1024), BF16)
        far = call(
            functools.partial(add_sib_body, PAIR_LEFT),
            [bf16] * 3,
            [mine, hop_col(sib_far, 0, 0, 1)],
            nbytes=3 << 20,
        )
        near = call(
            functools.partial(add_sib_body, OWN),
            [f32, bf16, bf16, f32, f32],
            [mine, hop_col(sib_near, 0, 0, 1)],
            after=[quarter],
            nbytes=5 << 20,
        )
        sums = reduce_places([*near, *far], step, swap, [half])
    with jax.named_scope("finish"):
        grad_features = call(
            finish_body,
            jax.ShapeDtypeStruct((1024, 128), BF16),
            [own_grad, *sums],
            nbytes=4 << 20,
        )
    return hidden, grad_features, grad_self, grad_neigh


def solution(mesh):
    placed = (
        P(("row", "col"), None),
        P(),
        P(),
        P(),
        P(("row", "col"), None),
        P("row", "col", None, None, None),
        P("row", "col", None, None),
        P("row", "col"),
    )
    return jax.shard_map(
        shards,
        mesh=mesh,
        in_specs=placed,
        out_specs=(P(("row", "col"), None), P(("row", "col"), None), P(), P()),
        check_vma=False,
    )
```

```python
import functools

import jax
import jax.numpy as jnp
from jax import lax
from jax.experimental import pallas as pl
from jax.experimental.pallas import tpu as pltpu
from jax.sharding import PartitionSpec as P

TILE = 256
VMEM = pltpu.VMEM
BF16 = jnp.bfloat16
F32 = jnp.float32
LIMIT = 12 * 1024 * 1024
GROUP = 16
ROOM = 144

NEAR = 5
ORDER = [(0, 0), (0, 3), (0, 1), (1, 0), (0, 2), (1, 3), (1, 1), (1, 2)]
OWN, LEFT, RIGHT, PAIR, OPPOSITE, PAIR_LEFT, PAIR_RIGHT, PAIR_OPPOSITE = range(8)
PLACE = sum(ORDER.index((k // 4, k % 4)) << (4 * k) for k in range(8))


def hop_col(value, dy, dx, dc=0):
    pairs = []
    for y in range(2):
        for x in range(4):
            for c in range(2):
                to = (((y + dy) % 2) * 4 + (x + dx) % 4) * 2 + (c + dc) % 2
                pairs.append(((y * 4 + x) * 2 + c, to))
    return lax.ppermute(value, "col", pairs)


def hop_row(value, dy, dz):
    pairs = []
    for z in range(4):
        for y in range(2):
            pairs.append((z * 2 + y, ((z + dz) % 4) * 2 + (y + dy) % 2))
    return lax.ppermute(value, "row", pairs)


def in_vmem(*values):
    return [pltpu.with_memory_space_constraint(v, VMEM) for v in values]


def vmem_specs(n):
    return [pl.BlockSpec(memory_space=VMEM)] * n


def call(
    body,
    outs,
    vmem_args,
    smem_args=(),
    after=(),
    scratch=(),
    alias=None,
    flops=0,
    nbytes=0,
):
    single = not isinstance(outs, (list, tuple))
    skip = len(smem_args) + len(vmem_args)

    def run(*refs):
        body(*refs[:skip], *refs[skip + len(after) :])

    return pl.pallas_call(
        run,
        out_shape=outs,
        in_specs=[pl.BlockSpec(memory_space=pltpu.SMEM)] * len(smem_args)
        + vmem_specs(len(vmem_args))
        + [pl.BlockSpec(memory_space=pl.ANY)] * len(after),
        out_specs=pl.BlockSpec(memory_space=VMEM) if single else vmem_specs(len(outs)),
        scratch_shapes=list(scratch),
        input_output_aliases=alias or {},
        compiler_params=pltpu.CompilerParams(vmem_limit_bytes=LIMIT),
        cost_estimate=pl.CostEstimate(flops=flops, bytes_accessed=nbytes, transcendentals=0),
    )(*smem_args, *in_vmem(*vmem_args), *after)


def write_extra(ref, row, value):
    for j in range(4):
        ref[row : row + 16, j * 256 : (j + 1) * 256] = value[16 * j : 16 * j + 16].astype(BF16)


def read_extra(ref, row):
    return jnp.concatenate(
        [ref[row : row + 16, j * 256 : (j + 1) * 256].astype(F32) for j in range(4)], axis=0
    )


def rounded(value):
    return value.astype(BF16).astype(F32)


def write_fine(ref, row, value):
    write_extra(ref, row, value)
    write_extra(ref, row + 16, value - rounded(value))


def read_fine(ref, row):
    return read_extra(ref, row) + read_extra(ref, row + 16)


def fine(value):
    high = rounded(value)
    return high + rounded(value - high)


def places():
    return lax.axis_index("col"), lax.axis_index("row")


def first_round(value, step, swap, to=None):
    to = to or [value] * 3
    return [value, step(to[0], 1), step(to[1], -1), swap(value), step(to[2], 2)]


def second_round(near, step, swap):
    return [step(near[PAIR], 1), step(near[PAIR], -1), swap(near[OPPOSITE])]


def place_of(index, me, other_bit, ring_shift):
    other = ((index ^ me) >> other_bit) & 1
    offset = ((index >> ring_shift) - (me >> ring_shift)) & 3
    return (PLACE >> ((other * 4 + offset) * 4)) & 15


def bring(first, last, stored, tiles, sems):
    copies = []
    for k, at in enumerate(range(first, last, 8)):
        part = pl.ds(at, 8)
        copies.append(pltpu.make_async_copy(stored.at[part], tiles.at[part], sems.at[k]))
        copies[-1].start()
    return copies


def plan_body(pairs, count, stored, tiles, lists, sizes, sems):
    copies = bring(0, 128, stored, tiles, sems)
    col, row = places()

    def put(base, which, entry, counts):
        at = (counts >> (which * 8)) & 255
        lists[(base + which) * ROOM + at] = entry
        return counts + (jnp.int32(1) << (which * 8))

    def sort(i, carry):
        d = pairs[0, i]
        s = pairs[1, i]
        c = s >> 2
        q = d >> 2
        sib = (c ^ col) & 1
        source = place_of(c, col, 3, 1) * 4 + (s & 3)
        target = place_of(q, row, 0, 1) * 4 + (d & 3)
        far = (source >= 4 * NEAR).astype(jnp.int32)
        entry = i | (target << 8) | ((source - far * 4 * NEAR) << 16)
        ahead = put(0, far * 2 + sib, entry, carry[0])
        far = (target >= 4 * NEAR).astype(jnp.int32)
        entry = i | ((target - far * 4 * NEAR) << 8) | (source << 16)
        back = put(4, far * 2 + sib, entry, carry[1])
        return ahead, back

    counts = lax.fori_loop(0, count[0], sort, (jnp.int32(0), jnp.int32(0)))
    for k in range(8):
        at = (counts[k // 4] >> (8 * (k % 4))) & 255
        sizes[k] = at
        for j in range(GROUP - 1):
            lists[k * ROOM + at + j] = 32 << 8 if k < 4 else 32 << 16
    for copy in copies:
        copy.wait()


def over_list(which, lists, sizes, product, total, to_target):
    def step(g, carry):
        news = []
        for j in range(GROUP):
            entry = lists[which * ROOM + g * GROUP + j]
            i = entry & 255
            d = (entry >> 8) & 255
            s = entry >> 16
            news.append((d if to_target else s, product(i, d, s)))
        for at, new in news:
            total[at] += new
        return carry

    lax.fori_loop(0, (sizes[which] + GROUP - 1) // GROUP, step, 0)


def pack_body(n, *rest):
    for k in range(n):
        rest[n][4 * k : 4 * k + 4] = rest[k][...].reshape(4, TILE, 128)
    for out in rest[n + 1 :]:
        out[...] = rest[PAIR][...]


def forward_step(lists, sizes, tiles, which, blocks, total):
    def product(i, d, s):
        return jnp.dot(tiles[i], blocks[s], preferred_element_type=F32)

    over_list(which, lists, sizes, product, total, True)


def forward_near_body(lists, sizes, tiles, mine, sib, total):
    total[...] = jnp.zeros_like(total)
    forward_step(lists, sizes, tiles, 0, mine, total)
    forward_step(lists, sizes, tiles, 1, sib, total)


def forward_far_body(lists, sizes, tiles, mine, before, total):
    forward_step(lists, sizes, tiles, 2, mine, total)


def forward_last_body(lists, sizes, tiles, sib, before, total, *outs):
    forward_step(lists, sizes, tiles, 3, sib, total)
    for k in range(8):
        outs[k][...] = total[4 * k : 4 * k + 4].reshape(1024, 128).astype(outs[k].dtype)


def hold_dz(parts, held):
    for k, ref in enumerate(parts):
        for b in range(4):
            held[4 * k + b] = ref[0:128, b * TILE : (b + 1) * TILE]


def backward_step(lists, sizes, tiles, which, held, total):
    def product(i, d, s):
        return jnp.dot(held[d], tiles[i], preferred_element_type=F32)

    over_list(which, lists, sizes, product, total, False)


def backward_near_body(lists, sizes, tiles, *rest):
    parts, (mine, sib, held) = rest[:NEAR], rest[NEAR:]
    hold_dz(parts, held)
    mine[...] = jnp.zeros_like(mine)
    sib[...] = jnp.zeros_like(sib)
    backward_step(lists, sizes, tiles, 5, held, sib)
    backward_step(lists, sizes, tiles, 4, held, mine)


def write_places(total, first, outs):
    for k, ref in enumerate(outs):
        for b in range(4):
            new = total[4 * (first + k) + b].astype(ref.dtype)
            ref[0:128, b * TILE : (b + 1) * TILE] = new


def backward_sib_body(lists, sizes, tiles, *rest):
    parts, (quarter, other, before, sib, far, near, quarter_out, held) = rest[:3], rest[3:]
    hold_dz(parts, held)
    backward_step(lists, sizes, tiles, 7, held, sib)
    write_places(sib, PAIR_LEFT, [far.at[pl.ds(128 * k, 128)] for k in range(3)])
    write_places(sib, OWN, [near.at[k] for k in range(5)])
    total = read_fine(quarter, 0) + read_fine(other, 0)
    quarter_out[...] = fine(total)
    write_fine(far, 384, total)


def backward_mine_body(lists, sizes, tiles, *rest):
    parts, (before, mine, held) = rest[:3], rest[3:]
    hold_dz(parts, held)
    backward_step(lists, sizes, tiles, 6, held, mine)


def add_sib_near_body(mine, got, *outs):
    for k, ref in enumerate(outs):
        for b in range(4):
            nodes = slice(b * TILE, (b + 1) * TILE)
            new = mine[4 * k + b] + got[k, :, nodes].astype(F32)
            ref[:, nodes] = new.astype(ref.dtype)


def add_sib_far_body(mine, got, quarter, *rest):
    outs, quarter_out = rest[:3], rest[3]
    total = quarter[...] + read_fine(got, 384)
    quarter_out[...] = rounded(total)
    for k, ref in enumerate(outs):
        for b in range(4):
            nodes = slice(b * TILE, (b + 1) * TILE)
            new = mine[4 * (PAIR_LEFT + k) + b] + got[128 * k : 128 * k + 128, nodes].astype(F32)
            ref[0:128, nodes] = new.astype(BF16)
        write_extra(ref, 128, total)


def add_round_body(n, own_extra, pair, opposite, a, b, c, *rest):
    pair_out, opposite_out = rest[-2:]
    new = pair[...] + (a[0:n].astype(F32) + b[0:n].astype(F32))
    pair_out[0:n] = new.astype(BF16)
    opposite_out[0:n] = (opposite[...] + c[0:n].astype(F32)).astype(BF16)
    if own_extra:
        own = rest[0]
        write_extra(opposite_out, n, own[...])
        opposite_out[n + 16 : n + 32] = c[n : n + 16]
        pair_out[n : n + 16] = b[n : n + 16]
        pair_out[n + 16 : n + 32] = a[n : n + 16]


def reduce_places(parts, step, swap, own_extra=()):
    n, lanes = parts[OWN].shape
    from_right = step(parts[PAIR_LEFT], -1)
    from_left = step(parts[PAIR_RIGHT], 1)
    from_pair = swap(parts[PAIR_OPPOSITE])
    sent = VMEM((n + 32 * len(own_extra), lanes), BF16)
    left = step(parts[LEFT], -1)
    right = step(parts[RIGHT], 1)
    pair, opposite = call(
        functools.partial(add_round_body, n, bool(own_extra)),
        [sent, sent],
        [parts[PAIR], parts[OPPOSITE], from_right, from_left, from_pair, *own_extra],
        nbytes=4 << 20,
    )
    opposite = step(opposite, 2)
    pair = swap(pair)
    return [parts[OWN], left, right, opposite, pair], [from_left, from_right, from_pair]


def dense_body(bias, feats, upstream, w_self, w_neigh, *rest):
    sums = rest[:5]
    hidden, dpre_out, dz_out, *dz_to, quarter, agg_out, grads = rest[5:]
    for b in range(4):
        rows = slice(b * TILE, (b + 1) * TILE)
        agg = sums[0][rows]
        for ref in sums[1:]:
            agg = agg + ref[rows].astype(F32)
        agg = agg.astype(BF16)
        agg_out[rows] = agg
        pre = jnp.dot(feats[rows], w_self[...], preferred_element_type=F32)
        pre = pre + jnp.dot(agg, w_neigh[...], preferred_element_type=F32) + bias[...]
        sig = jax.nn.sigmoid(pre)
        hidden[rows] = (pre * sig).astype(BF16)
        slope = sig * (1.0 + pre * (1.0 - sig))
        dpre = (upstream[rows].astype(F32) * slope).astype(BF16)
        dpre_out[rows] = dpre
        dz = lax.dot_general(
            w_neigh[...], dpre, (((1,), (1,)), ((), ())), preferred_element_type=F32
        ).astype(BF16)
        for ref in [dz_out, *dz_to]:
            ref[0:128, rows] = dz
    over_nodes = (((0,), (0,)), ((), ()))
    grads[0:128] = lax.dot_general(
        feats[...], dpre_out[...], over_nodes, preferred_element_type=F32
    )
    grads[128:256] = lax.dot_general(
        agg_out[...], dpre_out[...], over_nodes, preferred_element_type=F32
    )
    z = lax.axis_index("row") >> 1

    def piece(k):
        return grads[pl.ds(pl.multiple_of(((z + k) & 3) * 64, 64), 64), :]

    quarter[...] = piece(0)
    for ref, k in zip(dz_to, (1, 3, 2)):
        write_extra(ref, 128, piece(k))


def ring_sum_body(quarter, opposite, left, right, out):
    total = quarter[...] + read_extra(left, 128)
    write_fine(out, 0, total + (read_extra(right, 128) + read_extra(opposite, 128)))


def own_grad_body(dpre, w_self, own_grad):
    own_grad[...] = lax.dot_general(
        w_self[...], dpre[...], (((1,), (1,)), ((), ())), preferred_element_type=F32
    )


def finish_body(own_grad, *rest):
    out = rest[-1]
    for b in range(4):
        nodes = slice(b * TILE, (b + 1) * TILE)
        total = own_grad[:, nodes]
        for ref in rest[:-1]:
            total = total + ref[0:128, nodes].astype(F32)
        out[nodes] = total.T.astype(BF16)


def weight_sum_body(own, left, right, pair, from_opposite, from_pair, out, parts):
    col, _ = places()
    y, x = col >> 3, (col >> 1) & 3
    parts[y * 4 + x] = own[...]
    parts[y * 4 + ((x + 3) & 3)] = read_extra(left, 128)
    parts[y * 4 + ((x + 1) & 3)] = read_extra(right, 128)
    parts[(1 - y) * 4 + x] = read_extra(pair, 128)
    parts[y * 4 + ((x + 2) & 3)] = read_extra(from_opposite, 128)
    parts[(1 - y) * 4 + ((x + 2) & 3)] = read_extra(from_opposite, 144)
    parts[(1 - y) * 4 + ((x + 3) & 3)] = read_extra(from_pair, 128)
    parts[(1 - y) * 4 + ((x + 1) & 3)] = read_extra(from_pair, 144)
    total = parts[0]
    for k in range(1, 8):
        total = total + parts[k]
    out[...] = total


def weight_join_body(scale, own, *rest):
    others, (grad_self, grad_neigh, held) = rest[:3], rest[3:]
    z = lax.axis_index("row") >> 1
    for k, ref in enumerate([own, *others]):
        at = pl.multiple_of(((z + k) & 3) * 64, 64)
        held[pl.ds(at, 64), :] = ref[...] * scale
    grad_self[...] = held[0:128]
    grad_neigh[...] = held[128:256]


def shards(
    features, weight_self, weight_neigh, bias_term, upstream, tile_values, block_pairs, tile_counts
):
    nodes = 131072
    tile_bytes = 128 * TILE * TILE * 2
    share = 32 * 2 * TILE * TILE * 128
    in_hbm = pltpu.with_memory_space_constraint(tile_values.reshape(128, TILE, TILE), pltpu.HBM)
    with jax.named_scope("plan"):
        tiles, lists, sizes = pl.pallas_call(
            plan_body,
            out_shape=[
                VMEM((128, TILE, TILE), BF16),
                pltpu.SMEM((8 * ROOM,), jnp.int32),
                pltpu.SMEM((8,), jnp.int32),
            ],
            in_specs=[pl.BlockSpec(memory_space=pltpu.SMEM)] * 2
            + [pl.BlockSpec(memory_space=pl.ANY)],
            out_specs=[pl.BlockSpec(memory_space=VMEM)]
            + [pl.BlockSpec(memory_space=pltpu.SMEM)] * 2,
            scratch_shapes=[pltpu.SemaphoreType.DMA((16,))],
            compiler_params=pltpu.CompilerParams(vmem_limit_bytes=LIMIT),
            cost_estimate=pl.CostEstimate(flops=0, bytes_accessed=tile_bytes, transcendentals=0),
        )(block_pairs[0, 0].T, tile_counts.reshape(-1), in_hbm)
    by_list = [lists, sizes]

    with jax.named_scope("gather_features"):
        step, swap = (lambda v, d: hop_col(v, 0, d)), (lambda v: hop_col(v, 1, 0))
        near_blocks, far_blocks = VMEM((4 * NEAR, TILE, 128), BF16), VMEM((12, TILE, 128), BF16)
        near = first_round(features, step, swap)
        near_mine, near[PAIR] = call(
            functools.partial(pack_body, NEAR),
            [near_blocks, VMEM((1024, 128), BF16)],
            near,
            after=[sizes],
        )
        far = second_round(near, step, swap)
        near_sib = hop_col(near_mine, 0, 0, 1)
    with jax.named_scope("forward_tiles"):
        total = VMEM((33, TILE, 128), F32)
        sums = call(
            forward_near_body,
            total,
            [tiles, near_mine, near_sib],
            by_list,
        )
        far_mine = call(functools.partial(pack_body, 3), far_blocks, far, after=[sums])
        far_sib = hop_col(far_mine, 0, 0, 1)
        sums = call(
            forward_far_body,
            total,
            [tiles, far_mine, sums],
            by_list,
            alias={4: 0},
            flops=share,
            nbytes=tile_bytes // 4,
        )
        f32, bf16 = VMEM((1024, 128), F32), VMEM((1024, 128), BF16)
        _, *partial = call(
            forward_last_body,
            [total, f32, bf16, bf16, f32, f32, bf16, bf16, bf16],
            [tiles, far_sib, sums],
            by_list,
            alias={4: 0},
            flops=share,
            nbytes=tile_bytes // 4,
        )
    with jax.named_scope("sum_aggregates"):
        step, swap = (lambda v, d: hop_row(v, 0, d)), (lambda v: hop_row(v, 1, 0))
        sums, _ = reduce_places(partial, step, swap)
    with jax.named_scope("dense"):
        longer = VMEM((144, 1024), BF16)
        block = VMEM((64, 256), F32)
        hidden, dpre, dz, *dz_to, quarter = call(
            dense_body,
            [
                jax.ShapeDtypeStruct((1024, 256), BF16),
                VMEM((1024, 256), BF16),
                VMEM((128, 1024), BF16),
                longer,
                longer,
                longer,
                block,
            ],
            [bias_term.reshape(1, 256), features, upstream, weight_self, weight_neigh, *sums],
            scratch=[VMEM((1024, 128), BF16), VMEM((256, 256), F32)],
            flops=5 * 2 * 1024 * 128 * 256,
            nbytes=6 << 20,
        )
    with jax.named_scope("gather_dz"):
        near = first_round(dz, step, swap, dz_to)
        quarter = call(
            ring_sum_body,
            VMEM((32, 1024), BF16),
            [quarter, near[OPPOSITE], near[LEFT], near[RIGHT]],
        )
        quarter_pair = swap(quarter)
        far = second_round(near, step, swap)
    with jax.named_scope("own_grad"):
        own_grad = call(
            own_grad_body,
            VMEM((128, 1024), F32),
            [dpre, weight_self],
            flops=2 * 1024 * 128 * 256,
            nbytes=2 << 20,
        )
    with jax.named_scope("backward_tiles"):
        total = VMEM((33, 128, TILE), F32)
        held = [VMEM((4 * NEAR, 128, TILE), BF16)]
        mine, sib = call(
            backward_near_body,
            [total, total],
            [tiles, *near],
            by_list,
            after=[own_grad],
            scratch=held,
            flops=2 * share,
            nbytes=tile_bytes // 2,
        )
        _, sib_far, sib_near, quarter = call(
            backward_sib_body,
            [total, VMEM((416, 1024), BF16), VMEM((5, 128, 1024), BF16), block],
            [tiles, *far, quarter, quarter_pair, sib],
            by_list,
            alias={8: 0},
            scratch=held,
            flops=share,
            nbytes=tile_bytes // 4,
        )
        mine = call(
            backward_mine_body,
            total,
            [tiles, *far, mine],
            by_list,
            scratch=held,
            alias={6: 0},
            flops=share,
            nbytes=tile_bytes // 4,
        )
    with jax.named_scope("sum_grads"):
        step, swap = (lambda v, d: hop_col(v, 0, d)), (lambda v: hop_col(v, 1, 0))
        f32, bf16 = VMEM((128, 1024), F32), VMEM((128, 1024), BF16)
        *far, quarter = call(
            add_sib_far_body,
            [longer, longer, longer, block],
            [mine, hop_col(sib_far, 0, 0, 1), quarter],
            nbytes=3 << 20,
        )
        near = call(
            add_sib_near_body,
            [f32, bf16, bf16, f32, f32],
            [mine, hop_col(sib_near, 0, 0, 1)],
            nbytes=5 << 20,
        )
        sums, came = reduce_places([*near, *far], step, swap, [quarter])
    with jax.named_scope("sum_weights"):
        quarter = call(
            weight_sum_body,
            block,
            [quarter, *came, sums[3], sums[4]],
            scratch=[VMEM((8, 64, 256), F32)],
            nbytes=1 << 20,
        )
        shape = jax.ShapeDtypeStruct((128, 256), F32)
        grad_self, grad_neigh = call(
            functools.partial(weight_join_body, float(nodes) ** -0.5),
            [shape, shape],
            [quarter, *[hop_row(quarter, 0, -k) for k in (1, 2, 3)]],
            scratch=[VMEM((256, 256), F32)],
            nbytes=1 << 20,
        )
    with jax.named_scope("finish"):
        grad_features = call(
            finish_body,
            jax.ShapeDtypeStruct((1024, 128), BF16),
            [own_grad, *sums],
            nbytes=4 << 20,
        )
    return hidden, grad_features, grad_self, grad_neigh


def solution(mesh):
    placed = (
        P(("row", "col"), None),
        P(),
        P(),
        P(),
        P(("row", "col"), None),
        P("row", "col", None, None, None),
        P("row", "col", None, None),
        P("row", "col"),
    )
    return jax.shard_map(
        shards,
        mesh=mesh,
        in_specs=placed,
        out_specs=(P(("row", "col"), None), P(("row", "col"), None), P(), P()),
        check_vma=False,
    )
```

```python
import functools

import jax
import jax.numpy as jnp
from jax import lax
from jax.experimental import pallas as pl
from jax.experimental.pallas import tpu as pltpu
from jax.sharding import PartitionSpec as P

TILE = 256
VMEM = pltpu.VMEM
BF16 = jnp.bfloat16
F32 = jnp.float32
LIMIT = 12 * 1024 * 1024
GROUP = 16
ROOM = 144

NEAR = 5
ORDER = [(0, 0), (0, 3), (0, 1), (1, 0), (0, 2), (1, 3), (1, 1), (1, 2)]
OWN, LEFT, RIGHT, PAIR, OPPOSITE, PAIR_LEFT, PAIR_RIGHT, PAIR_OPPOSITE = range(8)
PLACE = sum(ORDER.index((k // 4, k % 4)) << (4 * k) for k in range(8))


def hop_col(value, dy, dx, dc=0):
    pairs = []
    for y in range(2):
        for x in range(4):
            for c in range(2):
                to = (((y + dy) % 2) * 4 + (x + dx) % 4) * 2 + (c + dc) % 2
                pairs.append(((y * 4 + x) * 2 + c, to))
    return lax.ppermute(value, "col", pairs)


def hop_row(value, dy, dz):
    pairs = []
    for z in range(4):
        for y in range(2):
            pairs.append((z * 2 + y, ((z + dz) % 4) * 2 + (y + dy) % 2))
    return lax.ppermute(value, "row", pairs)


def in_vmem(*values):
    return [pltpu.with_memory_space_constraint(v, VMEM) for v in values]


def vmem_specs(n):
    return [pl.BlockSpec(memory_space=VMEM)] * n


def call(
    body,
    outs,
    vmem_args,
    smem_args=(),
    after=(),
    scratch=(),
    alias=None,
    flops=0,
    nbytes=0,
):
    single = not isinstance(outs, (list, tuple))
    skip = len(smem_args) + len(vmem_args)

    def run(*refs):
        body(*refs[:skip], *refs[skip + len(after) :])

    return pl.pallas_call(
        run,
        out_shape=outs,
        in_specs=[pl.BlockSpec(memory_space=pltpu.SMEM)] * len(smem_args)
        + vmem_specs(len(vmem_args))
        + [pl.BlockSpec(memory_space=pl.ANY)] * len(after),
        out_specs=pl.BlockSpec(memory_space=VMEM) if single else vmem_specs(len(outs)),
        scratch_shapes=list(scratch),
        input_output_aliases=alias or {},
        compiler_params=pltpu.CompilerParams(vmem_limit_bytes=LIMIT),
        cost_estimate=pl.CostEstimate(flops=flops, bytes_accessed=nbytes, transcendentals=0),
    )(*smem_args, *in_vmem(*vmem_args), *after)


def write_extra(ref, row, value):
    for j in range(4):
        ref[row : row + 16, j * 256 : (j + 1) * 256] = value[16 * j : 16 * j + 16].astype(BF16)


def read_extra(ref, row):
    return jnp.concatenate(
        [ref[row : row + 16, j * 256 : (j + 1) * 256].astype(F32) for j in range(4)], axis=0
    )


def rounded(value):
    return value.astype(BF16).astype(F32)


def write_fine(ref, row, value):
    write_extra(ref, row, value)
    write_extra(ref, row + 16, value - rounded(value))


def read_fine(ref, row):
    return read_extra(ref, row) + read_extra(ref, row + 16)


def fine(value):
    high = rounded(value)
    return high + rounded(value - high)


def places():
    return lax.axis_index("col"), lax.axis_index("row")


def first_round(value, step, swap, to=None):
    to = to or [value] * 3
    return [value, step(to[0], 1), step(to[1], -1), swap(value), step(to[2], 2)]


def second_round(near, step, swap):
    return [step(near[PAIR], 1), step(near[PAIR], -1), swap(near[OPPOSITE])]


def place_of(index, me, other_bit, ring_shift):
    other = ((index ^ me) >> other_bit) & 1
    offset = ((index >> ring_shift) - (me >> ring_shift)) & 3
    return (PLACE >> ((other * 4 + offset) * 4)) & 15


def bring(first, last, stored, tiles, sems):
    copies = []
    for k, at in enumerate(range(first, last, 8)):
        part = pl.ds(at, 8)
        copies.append(pltpu.make_async_copy(stored.at[part], tiles.at[part], sems.at[k]))
        copies[-1].start()
    return copies


def plan_body(pairs, count, stored, tiles, lists, sizes, sems):
    copies = bring(0, 128, stored, tiles, sems)
    col, row = places()

    def put(base, which, entry, counts):
        at = (counts >> (which * 8)) & 255
        lists[(base + which) * ROOM + at] = entry
        return counts + (jnp.int32(1) << (which * 8))

    def sort(i, carry):
        d = pairs[0, i]
        s = pairs[1, i]
        c = s >> 2
        q = d >> 2
        sib = (c ^ col) & 1
        source = place_of(c, col, 3, 1) * 4 + (s & 3)
        target = place_of(q, row, 0, 1) * 4 + (d & 3)
        far = (source >= 4 * NEAR).astype(jnp.int32)
        entry = i | (target << 8) | ((source - far * 4 * NEAR) << 16)
        ahead = put(0, far * 2 + sib, entry, carry[0])
        far = (target >= 4 * NEAR).astype(jnp.int32)
        entry = i | ((target - far * 4 * NEAR) << 8) | (source << 16)
        back = put(4, far * 2 + sib, entry, carry[1])
        return ahead, back

    counts = lax.fori_loop(0, count[0], sort, (jnp.int32(0), jnp.int32(0)))
    for k in range(8):
        at = (counts[k // 4] >> (8 * (k % 4))) & 255
        sizes[k] = at
        for j in range(GROUP - 1):
            lists[k * ROOM + at + j] = 32 << 8 if k < 4 else 32 << 16
    for copy in copies:
        copy.wait()


def over_list(which, lists, sizes, product, total, to_target):
    def step(g, carry):
        news = []
        for j in range(GROUP):
            entry = lists[which * ROOM + g * GROUP + j]
            i = entry & 255
            d = (entry >> 8) & 255
            s = entry >> 16
            news.append((d if to_target else s, product(i, d, s)))
        for at, new in news:
            total[at] += new
        return carry

    lax.fori_loop(0, (sizes[which] + GROUP - 1) // GROUP, step, 0)


def pack_body(n, *rest):
    for k in range(n):
        rest[n][4 * k : 4 * k + 4] = rest[k][...].reshape(4, TILE, 128)
    for out in rest[n + 1 :]:
        out[...] = rest[PAIR][...]


def forward_step(lists, sizes, tiles, which, blocks, total):
    def product(i, d, s):
        return jnp.dot(tiles[i], blocks[s], preferred_element_type=F32)

    over_list(which, lists, sizes, product, total, True)


def forward_near_body(lists, sizes, tiles, mine, sib, total):
    total[...] = jnp.zeros_like(total)
    forward_step(lists, sizes, tiles, 0, mine, total)
    forward_step(lists, sizes, tiles, 1, sib, total)


def forward_far_body(lists, sizes, tiles, mine, before, total):
    forward_step(lists, sizes, tiles, 2, mine, total)


def forward_last_body(lists, sizes, tiles, sib, before, total, *outs):
    forward_step(lists, sizes, tiles, 3, sib, total)
    for k in range(8):
        outs[k][...] = total[4 * k : 4 * k + 4].reshape(1024, 128).astype(outs[k].dtype)


def hold_dz(parts, held):
    for k, ref in enumerate(parts):
        for b in range(4):
            held[4 * k + b] = ref[0:128, b * TILE : (b + 1) * TILE]


def backward_step(lists, sizes, tiles, which, held, total):
    def product(i, d, s):
        return jnp.dot(held[d], tiles[i], preferred_element_type=F32)

    over_list(which, lists, sizes, product, total, False)


def backward_near_body(lists, sizes, tiles, *rest):
    parts, (mine, sib, held) = rest[:NEAR], rest[NEAR:]
    hold_dz(parts, held)
    mine[...] = jnp.zeros_like(mine)
    sib[...] = jnp.zeros_like(sib)
    backward_step(lists, sizes, tiles, 5, held, sib)
    backward_step(lists, sizes, tiles, 4, held, mine)


def write_places(total, first, outs):
    for k, ref in enumerate(outs):
        for b in range(4):
            new = total[4 * (first + k) + b].astype(ref.dtype)
            ref[0:128, b * TILE : (b + 1) * TILE] = new


def backward_sib_body(lists, sizes, tiles, *rest):
    parts, (quarter, other, before, sib, far, quarter_out, held) = rest[:3], rest[3:]
    hold_dz(parts, held)
    backward_step(lists, sizes, tiles, 7, held, sib)
    write_places(sib, PAIR_LEFT, [far.at[pl.ds(128 * k, 128)] for k in range(3)])
    total = read_fine(quarter, 0) + read_fine(other, 0)
    quarter_out[...] = fine(total)
    write_fine(far, 384, total)


def backward_mine_body(lists, sizes, tiles, *rest):
    parts, (before, mine, held) = rest[:3], rest[3:]
    hold_dz(parts, held)
    backward_step(lists, sizes, tiles, 6, held, mine)


def add_sib_far_body(mine, sib, got, quarter, *rest):
    outs, quarter_out, near = rest[:3], rest[3], rest[4]
    total = quarter[...] + read_fine(got, 384)
    quarter_out[...] = rounded(total)
    for k, ref in enumerate(outs):
        for b in range(4):
            nodes = slice(b * TILE, (b + 1) * TILE)
            new = mine[4 * (PAIR_LEFT + k) + b] + got[128 * k : 128 * k + 128, nodes].astype(F32)
            ref[0:128, nodes] = new.astype(BF16)
        write_extra(ref, 128, total)
    write_places(sib, OWN, [near.at[k] for k in range(5)])


def add_round_body(pair, opposite, from_right, from_left, from_pair, pair_out, opposite_out):
    new = pair[...] + (from_right[...].astype(F32) + from_left[...].astype(F32))
    pair_out[...] = new.astype(BF16)
    opposite_out[...] = (opposite[...] + from_pair[...].astype(F32)).astype(BF16)


def add_near_body(mine, got, from_right, from_left, from_pair, quarter, *outs):
    more = {PAIR: [from_right, from_left], OPPOSITE: [from_pair]}
    for place, ref in enumerate(outs):
        for b in range(4):
            nodes = slice(b * TILE, (b + 1) * TILE)
            new = mine[4 * place + b] + got[place, :, nodes].astype(F32)
            for came in more.get(place, []):
                new = new + came[0:128, nodes].astype(F32)
            ref[0:128, nodes] = new.astype(ref.dtype)
    pair, opposite = outs[PAIR], outs[OPPOSITE]
    write_extra(opposite, 128, quarter[...])
    opposite[144:160] = from_pair[128:144]
    pair[128:144] = from_left[128:144]
    pair[144:160] = from_right[128:144]


def first_sums(parts, step, swap):
    return step(parts[0], -1), step(parts[1], 1), swap(parts[2])


def second_sums(own, left, right, pair, opposite, step, swap):
    return [own, step(left, -1), step(right, 1), step(opposite, 2), swap(pair)]


def dense_body(bias, feats, upstream, w_self, w_neigh, *rest):
    sums = rest[:5]
    hidden, dpre_out, dz_out, *dz_to, quarter, agg_out, grads = rest[5:]
    for b in range(4):
        rows = slice(b * TILE, (b + 1) * TILE)
        agg = sums[0][rows]
        for ref in sums[1:]:
            agg = agg + ref[rows].astype(F32)
        agg = agg.astype(BF16)
        agg_out[rows] = agg
        pre = jnp.dot(feats[rows], w_self[...], preferred_element_type=F32)
        pre = pre + jnp.dot(agg, w_neigh[...], preferred_element_type=F32) + bias[...]
        sig = jax.nn.sigmoid(pre)
        hidden[rows] = (pre * sig).astype(BF16)
        slope = sig * (1.0 + pre * (1.0 - sig))
        dpre = (upstream[rows].astype(F32) * slope).astype(BF16)
        dpre_out[rows] = dpre
        dz = lax.dot_general(
            w_neigh[...], dpre, (((1,), (1,)), ((), ())), preferred_element_type=F32
        ).astype(BF16)
        for ref in [dz_out, *dz_to]:
            ref[0:128, rows] = dz
    over_nodes = (((0,), (0,)), ((), ()))
    grads[0:128] = lax.dot_general(
        feats[...], dpre_out[...], over_nodes, preferred_element_type=F32
    )
    grads[128:256] = lax.dot_general(
        agg_out[...], dpre_out[...], over_nodes, preferred_element_type=F32
    )
    z = lax.axis_index("row") >> 1

    def piece(k):
        return grads[pl.ds(pl.multiple_of(((z + k) & 3) * 64, 64), 64), :]

    quarter[...] = piece(0)
    for ref, k in zip(dz_to, (1, 3, 2)):
        write_extra(ref, 128, piece(k))


def ring_sum_body(quarter, opposite, left, right, out):
    total = quarter[...] + read_extra(left, 128)
    write_fine(out, 0, total + (read_extra(right, 128) + read_extra(opposite, 128)))


def own_grad_body(dpre, w_self, own_grad):
    own_grad[...] = lax.dot_general(
        w_self[...], dpre[...], (((1,), (1,)), ((), ())), preferred_element_type=F32
    )


def finish_body(own_grad, *rest):
    out = rest[-1]
    for b in range(4):
        nodes = slice(b * TILE, (b + 1) * TILE)
        total = own_grad[:, nodes]
        for ref in rest[:-1]:
            total = total + ref[0:128, nodes].astype(F32)
        out[nodes] = total.T.astype(BF16)


def weight_sum_body(own, left, right, pair, from_opposite, from_pair, out, parts):
    col, _ = places()
    y, x = col >> 3, (col >> 1) & 3
    parts[y * 4 + x] = own[...]
    parts[y * 4 + ((x + 3) & 3)] = read_extra(left, 128)
    parts[y * 4 + ((x + 1) & 3)] = read_extra(right, 128)
    parts[(1 - y) * 4 + x] = read_extra(pair, 128)
    parts[y * 4 + ((x + 2) & 3)] = read_extra(from_opposite, 128)
    parts[(1 - y) * 4 + ((x + 2) & 3)] = read_extra(from_opposite, 144)
    parts[(1 - y) * 4 + ((x + 3) & 3)] = read_extra(from_pair, 128)
    parts[(1 - y) * 4 + ((x + 1) & 3)] = read_extra(from_pair, 144)
    total = parts[0]
    for k in range(1, 8):
        total = total + parts[k]
    out[...] = total


def weight_join_body(scale, own, *rest):
    others, (grad_self, grad_neigh, held) = rest[:3], rest[3:]
    z = lax.axis_index("row") >> 1
    for k, ref in enumerate([own, *others]):
        at = pl.multiple_of(((z + k) & 3) * 64, 64)
        held[pl.ds(at, 64), :] = ref[...] * scale
    grad_self[...] = held[0:128]
    grad_neigh[...] = held[128:256]


def shards(
    features, weight_self, weight_neigh, bias_term, upstream, tile_values, block_pairs, tile_counts
):
    nodes = 131072
    tile_bytes = 128 * TILE * TILE * 2
    share = 32 * 2 * TILE * TILE * 128
    in_hbm = pltpu.with_memory_space_constraint(tile_values.reshape(128, TILE, TILE), pltpu.HBM)
    with jax.named_scope("plan"):
        tiles, lists, sizes = pl.pallas_call(
            plan_body,
            out_shape=[
                VMEM((128, TILE, TILE), BF16),
                pltpu.SMEM((8 * ROOM,), jnp.int32),
                pltpu.SMEM((8,), jnp.int32),
            ],
            in_specs=[pl.BlockSpec(memory_space=pltpu.SMEM)] * 2
            + [pl.BlockSpec(memory_space=pl.ANY)],
            out_specs=[pl.BlockSpec(memory_space=VMEM)]
            + [pl.BlockSpec(memory_space=pltpu.SMEM)] * 2,
            scratch_shapes=[pltpu.SemaphoreType.DMA((16,))],
            compiler_params=pltpu.CompilerParams(vmem_limit_bytes=LIMIT),
            cost_estimate=pl.CostEstimate(flops=0, bytes_accessed=tile_bytes, transcendentals=0),
        )(block_pairs[0, 0].T, tile_counts.reshape(-1), in_hbm)
    by_list = [lists, sizes]

    with jax.named_scope("gather_features"):
        step, swap = (lambda v, d: hop_col(v, 0, d)), (lambda v: hop_col(v, 1, 0))
        near_blocks, far_blocks = VMEM((4 * NEAR, TILE, 128), BF16), VMEM((12, TILE, 128), BF16)
        near = first_round(features, step, swap)
        near_mine, near[PAIR] = call(
            functools.partial(pack_body, NEAR),
            [near_blocks, VMEM((1024, 128), BF16)],
            near,
            after=[sizes],
        )
        far = second_round(near, step, swap)
        near_sib = hop_col(near_mine, 0, 0, 1)
    with jax.named_scope("forward_tiles"):
        total = VMEM((33, TILE, 128), F32)
        sums = call(
            forward_near_body,
            total,
            [tiles, near_mine, near_sib],
            by_list,
        )
        far_mine = call(functools.partial(pack_body, 3), far_blocks, far, after=[sums])
        far_sib = hop_col(far_mine, 0, 0, 1)
        sums = call(
            forward_far_body,
            total,
            [tiles, far_mine, sums],
            by_list,
            alias={4: 0},
            flops=share,
            nbytes=tile_bytes // 4,
        )
        f32, bf16 = VMEM((1024, 128), F32), VMEM((1024, 128), BF16)
        _, *partial = call(
            forward_last_body,
            [total, f32, bf16, bf16, f32, f32, bf16, bf16, bf16],
            [tiles, far_sib, sums],
            by_list,
            alias={4: 0},
            flops=share,
            nbytes=tile_bytes // 4,
        )
    with jax.named_scope("sum_aggregates"):
        step, swap = (lambda v, d: hop_row(v, 0, d)), (lambda v: hop_row(v, 1, 0))
        own, left, right, pair, opposite, *far = partial
        pair, opposite = call(
            add_round_body,
            [bf16, bf16],
            [pair, opposite, *first_sums(far, step, swap)],
            nbytes=4 << 20,
        )
        sums = second_sums(own, left, right, pair, opposite, step, swap)
    with jax.named_scope("dense"):
        longer = VMEM((144, 1024), BF16)
        block = VMEM((64, 256), F32)
        hidden, dpre, dz, *dz_to, quarter = call(
            dense_body,
            [
                jax.ShapeDtypeStruct((1024, 256), BF16),
                VMEM((1024, 256), BF16),
                VMEM((128, 1024), BF16),
                longer,
                longer,
                longer,
                block,
            ],
            [bias_term.reshape(1, 256), features, upstream, weight_self, weight_neigh, *sums],
            scratch=[VMEM((1024, 128), BF16), VMEM((256, 256), F32)],
            flops=5 * 2 * 1024 * 128 * 256,
            nbytes=6 << 20,
        )
    with jax.named_scope("gather_dz"):
        near = first_round(dz, step, swap, dz_to)
        quarter = call(
            ring_sum_body,
            VMEM((32, 1024), BF16),
            [quarter, near[OPPOSITE], near[LEFT], near[RIGHT]],
        )
        quarter_pair = swap(quarter)
        far = second_round(near, step, swap)
    with jax.named_scope("own_grad"):
        own_grad = call(
            own_grad_body,
            VMEM((128, 1024), F32),
            [dpre, weight_self],
            flops=2 * 1024 * 128 * 256,
            nbytes=2 << 20,
        )
    with jax.named_scope("backward_tiles"):
        total = VMEM((33, 128, TILE), F32)
        held = [VMEM((4 * NEAR, 128, TILE), BF16)]
        mine, sib = call(
            backward_near_body,
            [total, total],
            [tiles, *near],
            by_list,
            after=[own_grad],
            scratch=held,
            flops=2 * share,
            nbytes=tile_bytes // 2,
        )
        sib, sib_far, quarter = call(
            backward_sib_body,
            [total, VMEM((416, 1024), BF16), block],
            [tiles, *far, quarter, quarter_pair, sib],
            by_list,
            alias={8: 0},
            scratch=held,
            flops=share,
            nbytes=tile_bytes // 4,
        )
        mine = call(
            backward_mine_body,
            total,
            [tiles, *far, mine],
            by_list,
            scratch=held,
            alias={6: 0},
            flops=share,
            nbytes=tile_bytes // 4,
        )
    with jax.named_scope("sum_grads"):
        step, swap = (lambda v, d: hop_col(v, 0, d)), (lambda v: hop_col(v, 1, 0))
        f32, bf16 = VMEM((128, 1024), F32), VMEM((128, 1024), BF16)
        *far, quarter, sib_near = call(
            add_sib_far_body,
            [longer, longer, longer, block, VMEM((5, 128, 1024), BF16)],
            [mine, sib, hop_col(sib_far, 0, 0, 1), quarter],
            nbytes=3 << 20,
        )
        from_right, from_left, from_pair = first_sums(far, step, swap)
        longest = VMEM((160, 1024), BF16)
        near = call(
            add_near_body,
            [f32, bf16, bf16, longest, longest],
            [mine, hop_col(sib_near, 0, 0, 1), from_right, from_left, from_pair, quarter],
            nbytes=5 << 20,
        )
        sums = second_sums(*near, step, swap)
        came = [from_left, from_right, from_pair]
    with jax.named_scope("sum_weights"):
        quarter = call(
            weight_sum_body,
            block,
            [quarter, *came, sums[3], sums[4]],
            scratch=[VMEM((8, 64, 256), F32)],
            nbytes=1 << 20,
        )
        shape = jax.ShapeDtypeStruct((128, 256), F32)
        grad_self, grad_neigh = call(
            functools.partial(weight_join_body, float(nodes) ** -0.5),
            [shape, shape],
            [quarter, *[hop_row(quarter, 0, -k) for k in (1, 2, 3)]],
            scratch=[VMEM((256, 256), F32)],
            nbytes=1 << 20,
        )
    with jax.named_scope("finish"):
        grad_features = call(
            finish_body,
            jax.ShapeDtypeStruct((1024, 128), BF16),
            [own_grad, *sums],
            nbytes=4 << 20,
        )
    return hidden, grad_features, grad_self, grad_neigh


def solution(mesh):
    placed = (
        P(("row", "col"), None),
        P(),
        P(),
        P(),
        P(("row", "col"), None),
        P("row", "col", None, None, None),
        P("row", "col", None, None),
        P("row", "col"),
    )
    return jax.shard_map(
        shards,
        mesh=mesh,
        in_specs=placed,
        out_specs=(P(("row", "col"), None), P(("row", "col"), None), P(), P()),
        check_vma=False,
    )
```

```python
import functools

import jax
import jax.numpy as jnp
from jax import lax
from jax.experimental import pallas as pl
from jax.experimental.pallas import tpu as pltpu
from jax.sharding import PartitionSpec as P

TILE = 256
VMEM = pltpu.VMEM
BF16 = jnp.bfloat16
F32 = jnp.float32
LIMIT = 12 * 1024 * 1024
GROUP = 16
ROOM = 144

NEAR = 5
ORDER = [(0, 0), (0, 3), (0, 1), (1, 0), (0, 2), (1, 3), (1, 1), (1, 2)]
OWN, LEFT, RIGHT, PAIR, OPPOSITE, PAIR_LEFT, PAIR_RIGHT, PAIR_OPPOSITE = range(8)
PLACE = sum(ORDER.index((k // 4, k % 4)) << (4 * k) for k in range(8))


def hop_col(value, dy, dx, dc=0):
    pairs = []
    for y in range(2):
        for x in range(4):
            for c in range(2):
                to = (((y + dy) % 2) * 4 + (x + dx) % 4) * 2 + (c + dc) % 2
                pairs.append(((y * 4 + x) * 2 + c, to))
    return lax.ppermute(value, "col", pairs)


def hop_row(value, dy, dz):
    pairs = []
    for z in range(4):
        for y in range(2):
            pairs.append((z * 2 + y, ((z + dz) % 4) * 2 + (y + dy) % 2))
    return lax.ppermute(value, "row", pairs)


def in_vmem(*values):
    return [pltpu.with_memory_space_constraint(v, VMEM) for v in values]


def vmem_specs(n):
    return [pl.BlockSpec(memory_space=VMEM)] * n


def call(
    body,
    outs,
    vmem_args,
    smem_args=(),
    after=(),
    scratch=(),
    alias=None,
    flops=0,
    nbytes=0,
):
    single = not isinstance(outs, (list, tuple))
    skip = len(smem_args) + len(vmem_args)

    def run(*refs):
        body(*refs[:skip], *refs[skip + len(after) :])

    return pl.pallas_call(
        run,
        out_shape=outs,
        in_specs=[pl.BlockSpec(memory_space=pltpu.SMEM)] * len(smem_args)
        + vmem_specs(len(vmem_args))
        + [pl.BlockSpec(memory_space=pl.ANY)] * len(after),
        out_specs=pl.BlockSpec(memory_space=VMEM) if single else vmem_specs(len(outs)),
        scratch_shapes=list(scratch),
        input_output_aliases=alias or {},
        compiler_params=pltpu.CompilerParams(vmem_limit_bytes=LIMIT),
        cost_estimate=pl.CostEstimate(flops=flops, bytes_accessed=nbytes, transcendentals=0),
    )(*smem_args, *in_vmem(*vmem_args), *after)


def write_extra(ref, row, value):
    for j in range(4):
        ref[row : row + 16, j * 256 : (j + 1) * 256] = value[16 * j : 16 * j + 16].astype(BF16)


def read_extra(ref, row):
    return jnp.concatenate(
        [ref[row : row + 16, j * 256 : (j + 1) * 256].astype(F32) for j in range(4)], axis=0
    )


def rounded(value):
    return value.astype(BF16).astype(F32)


def write_fine(ref, row, value):
    write_extra(ref, row, value)
    write_extra(ref, row + 16, value - rounded(value))


def read_fine(ref, row):
    return read_extra(ref, row) + read_extra(ref, row + 16)


def fine(value):
    high = rounded(value)
    return high + rounded(value - high)


def places():
    return lax.axis_index("col"), lax.axis_index("row")


def first_round(value, step, swap, to=None):
    to = to or [value] * 3
    return [value, step(to[0], 1), step(to[1], -1), swap(value), step(to[2], 2)]


def second_round(near, step, swap):
    return [step(near[PAIR], 1), step(near[PAIR], -1), swap(near[OPPOSITE])]


def place_of(index, me, other_bit, ring_shift):
    other = ((index ^ me) >> other_bit) & 1
    offset = ((index >> ring_shift) - (me >> ring_shift)) & 3
    return (PLACE >> ((other * 4 + offset) * 4)) & 15


def bring(first, last, stored, tiles, sems):
    copies = []
    for k, at in enumerate(range(first, last, 8)):
        part = pl.ds(at, 8)
        copies.append(pltpu.make_async_copy(stored.at[part], tiles.at[part], sems.at[k]))
        copies[-1].start()
    return copies


def plan_body(pairs, count, stored, tiles, lists, sizes, sems):
    copies = bring(0, 128, stored, tiles, sems)
    col, row = places()

    def put(base, which, entry, counts):
        at = (counts >> (which * 8)) & 255
        lists[(base + which) * ROOM + at] = entry
        return counts + (jnp.int32(1) << (which * 8))

    def sort(i, carry):
        d = pairs[0, i]
        s = pairs[1, i]
        c = s >> 2
        q = d >> 2
        sib = (c ^ col) & 1
        source = place_of(c, col, 3, 1) * 4 + (s & 3)
        target = place_of(q, row, 0, 1) * 4 + (d & 3)
        far = (source >= 4 * NEAR).astype(jnp.int32)
        entry = i | (target << 8) | ((source - far * 4 * NEAR) << 16)
        ahead = put(0, far * 2 + sib, entry, carry[0])
        far = (target >= 4 * NEAR).astype(jnp.int32)
        entry = i | ((target - far * 4 * NEAR) << 8) | (source << 16)
        back = put(4, far * 2 + sib, entry, carry[1])
        return ahead, back

    counts = lax.fori_loop(0, count[0], sort, (jnp.int32(0), jnp.int32(0)))
    for k in range(8):
        at = (counts[k // 4] >> (8 * (k % 4))) & 255
        sizes[k] = at
        for j in range(GROUP - 1):
            lists[k * ROOM + at + j] = 32 << 8 if k < 4 else 32 << 16
    for copy in copies:
        copy.wait()


def over_list(which, lists, sizes, product, total, to_target):
    def step(g, carry):
        news = []
        for j in range(GROUP):
            entry = lists[which * ROOM + g * GROUP + j]
            i = entry & 255
            d = (entry >> 8) & 255
            s = entry >> 16
            news.append((d if to_target else s, product(i, d, s)))
        for at, new in news:
            total[at] += new
        return carry

    lax.fori_loop(0, (sizes[which] + GROUP - 1) // GROUP, step, 0)


def pack_body(n, *rest):
    for k in range(n):
        rest[n][4 * k : 4 * k + 4] = rest[k][...].reshape(4, TILE, 128)
    for out in rest[n + 1 :]:
        out[...] = rest[PAIR][...]


def forward_step(lists, sizes, tiles, which, blocks, total):
    def product(i, d, s):
        return jnp.dot(tiles[i], blocks[s], preferred_element_type=F32)

    over_list(which, lists, sizes, product, total, True)


def forward_near_body(lists, sizes, tiles, mine, sib, total):
    total[...] = jnp.zeros_like(total)
    forward_step(lists, sizes, tiles, 0, mine, total)
    forward_step(lists, sizes, tiles, 1, sib, total)


def forward_far_body(lists, sizes, tiles, mine, before, total):
    forward_step(lists, sizes, tiles, 2, mine, total)


def forward_last_body(lists, sizes, tiles, sib, before, total, *outs):
    forward_step(lists, sizes, tiles, 3, sib, total)
    for k in range(8):
        outs[k][...] = total[4 * k : 4 * k + 4].reshape(1024, 128).astype(outs[k].dtype)


def hold_dz(parts, held):
    for k, ref in enumerate(parts):
        for b in range(4):
            held[4 * k + b] = ref[0:128, b * TILE : (b + 1) * TILE]


def backward_step(lists, sizes, tiles, which, held, total):
    def product(i, d, s):
        return jnp.dot(held[d], tiles[i], preferred_element_type=F32)

    over_list(which, lists, sizes, product, total, False)


def backward_near_body(lists, sizes, tiles, *rest):
    parts, (mine, sib, held) = rest[:NEAR], rest[NEAR:]
    hold_dz(parts, held)
    mine[...] = jnp.zeros_like(mine)
    sib[...] = jnp.zeros_like(sib)
    backward_step(lists, sizes, tiles, 5, held, sib)
    backward_step(lists, sizes, tiles, 4, held, mine)


def write_places(total, first, outs):
    for k, ref in enumerate(outs):
        for b in range(4):
            new = total[4 * (first + k) + b].astype(ref.dtype)
            ref[0:128, b * TILE : (b + 1) * TILE] = new


def backward_sib_body(lists, sizes, tiles, *rest):
    parts, (quarter, other, before, sib, far, quarter_out, held) = rest[:3], rest[3:]
    hold_dz(parts, held)
    backward_step(lists, sizes, tiles, 7, held, sib)
    write_places(sib, PAIR_LEFT, [far.at[pl.ds(128 * k, 128)] for k in range(3)])
    total = read_fine(quarter, 0) + read_fine(other, 0)
    quarter_out[...] = fine(total)
    write_fine(far, 384, total)


def backward_mine_body(lists, sizes, tiles, *rest):
    parts, (before, mine, held) = rest[:3], rest[3:]
    hold_dz(parts, held)
    backward_step(lists, sizes, tiles, 6, held, mine)


def add_sib_far_body(mine, sib, got, quarter, *rest):
    outs, (quarter_out, near, extra) = rest[:3], rest[3:]
    total = quarter[...] + read_fine(got, 384)
    quarter_out[...] = rounded(total)
    for k, ref in enumerate(outs):
        for b in range(4):
            nodes = slice(b * TILE, (b + 1) * TILE)
            new = mine[4 * (PAIR_LEFT + k) + b] + got[128 * k : 128 * k + 128, nodes].astype(F32)
            ref[0:128, nodes] = new.astype(BF16)
        write_extra(ref, 128, total)
    write_extra(extra, 0, total)
    write_places(sib, OWN, [near.at[k] for k in range(5)])


def add_round_body(pair, opposite, from_right, from_left, from_pair, pair_out, opposite_out):
    new = pair[...] + (from_right[...].astype(F32) + from_left[...].astype(F32))
    pair_out[...] = new.astype(BF16)
    opposite_out[...] = (opposite[...] + from_pair[...].astype(F32)).astype(BF16)


def add_sides_body(mine, got, left, right):
    for place, ref in ((LEFT, left), (RIGHT, right)):
        for b in range(4):
            nodes = slice(b * TILE, (b + 1) * TILE)
            new = mine[4 * place + b] + got[place, :, nodes].astype(F32)
            ref[:, nodes] = new.astype(BF16)


def add_near_body(mine, got, from_right, from_left, from_pair, *outs):
    more = {PAIR: [from_right, from_left], OPPOSITE: [from_pair]}
    for place, ref in zip((OWN, PAIR, OPPOSITE), outs):
        for b in range(4):
            nodes = slice(b * TILE, (b + 1) * TILE)
            new = mine[4 * place + b] + got[place, :, nodes].astype(F32)
            for came in more.get(place, []):
                new = new + came[0:128, nodes].astype(F32)
            ref[:, nodes] = new.astype(ref.dtype)


def extras_body(from_right, from_left, from_opposite, pair):
    pair[0:16] = from_left[128:144]
    pair[16:32] = from_right[128:144]
    pair[32:48] = from_opposite[...]


def first_sums(parts, step, swap):
    return step(parts[0], -1), step(parts[1], 1), swap(parts[2])


def second_sums(own, left, right, pair, opposite, step, swap):
    return [own, step(left, -1), step(right, 1), step(opposite, 2), swap(pair)]


def dense_body(bias, feats, upstream, w_self, w_neigh, *rest):
    sums = rest[:5]
    hidden, dpre_out, dz_out, *dz_to, quarter, agg_out, grads = rest[5:]
    for b in range(4):
        rows = slice(b * TILE, (b + 1) * TILE)
        agg = sums[0][rows]
        for ref in sums[1:]:
            agg = agg + ref[rows].astype(F32)
        agg = agg.astype(BF16)
        agg_out[rows] = agg
        pre = jnp.dot(feats[rows], w_self[...], preferred_element_type=F32)
        pre = pre + jnp.dot(agg, w_neigh[...], preferred_element_type=F32) + bias[...]
        sig = jax.nn.sigmoid(pre)
        hidden[rows] = (pre * sig).astype(BF16)
        slope = sig * (1.0 + pre * (1.0 - sig))
        dpre = (upstream[rows].astype(F32) * slope).astype(BF16)
        dpre_out[rows] = dpre
        dz = lax.dot_general(
            w_neigh[...], dpre, (((1,), (1,)), ((), ())), preferred_element_type=F32
        ).astype(BF16)
        for ref in [dz_out, *dz_to]:
            ref[0:128, rows] = dz
    over_nodes = (((0,), (0,)), ((), ()))
    grads[0:128] = lax.dot_general(
        feats[...], dpre_out[...], over_nodes, preferred_element_type=F32
    )
    grads[128:256] = lax.dot_general(
        agg_out[...], dpre_out[...], over_nodes, preferred_element_type=F32
    )
    z = lax.axis_index("row") >> 1

    def piece(k):
        return grads[pl.ds(pl.multiple_of(((z + k) & 3) * 64, 64), 64), :]

    quarter[...] = piece(0)
    for ref, k in zip(dz_to, (1, 3, 2)):
        write_extra(ref, 128, piece(k))


def ring_sum_body(quarter, opposite, left, right, out):
    total = quarter[...] + read_extra(left, 128)
    write_fine(out, 0, total + (read_extra(right, 128) + read_extra(opposite, 128)))


def own_grad_body(dpre, w_self, own_grad):
    own_grad[...] = lax.dot_general(
        w_self[...], dpre[...], (((1,), (1,)), ((), ())), preferred_element_type=F32
    )


def finish_body(own_grad, *rest):
    out = rest[-1]
    for b in range(4):
        nodes = slice(b * TILE, (b + 1) * TILE)
        total = own_grad[:, nodes]
        for ref in rest[:-1]:
            total = total + ref[0:128, nodes].astype(F32)
        out[nodes] = total.T.astype(BF16)


def weight_sum_body(own, left, right, pair, opposite, pair_ring, out, parts):
    col, _ = places()
    y, x = col >> 3, (col >> 1) & 3
    ring, other = y * 4, (1 - y) * 4
    parts[ring + x] = own[...]
    parts[ring + ((x + 3) & 3)] = read_extra(left, 128)
    parts[ring + ((x + 1) & 3)] = read_extra(right, 128)
    parts[ring + ((x + 2) & 3)] = read_extra(opposite, 0)
    parts[other + x] = read_extra(pair, 128)
    parts[other + ((x + 3) & 3)] = read_extra(pair_ring, 0)
    parts[other + ((x + 1) & 3)] = read_extra(pair_ring, 16)
    parts[other + ((x + 2) & 3)] = read_extra(pair_ring, 32)
    total = parts[0]
    for k in range(1, 8):
        total = total + parts[k]
    out[...] = total


def weight_join_body(scale, own, *rest):
    others, (grad_self, grad_neigh, held) = rest[:3], rest[3:]
    z = lax.axis_index("row") >> 1
    for k, ref in enumerate([own, *others]):
        at = pl.multiple_of(((z + k) & 3) * 64, 64)
        held[pl.ds(at, 64), :] = ref[...] * scale
    grad_self[...] = held[0:128]
    grad_neigh[...] = held[128:256]


def shards(
    features, weight_self, weight_neigh, bias_term, upstream, tile_values, block_pairs, tile_counts
):
    nodes = 131072
    tile_bytes = 128 * TILE * TILE * 2
    share = 32 * 2 * TILE * TILE * 128
    in_hbm = pltpu.with_memory_space_constraint(tile_values.reshape(128, TILE, TILE), pltpu.HBM)
    with jax.named_scope("plan"):
        tiles, lists, sizes = pl.pallas_call(
            plan_body,
            out_shape=[
                VMEM((128, TILE, TILE), BF16),
                pltpu.SMEM((8 * ROOM,), jnp.int32),
                pltpu.SMEM((8,), jnp.int32),
            ],
            in_specs=[pl.BlockSpec(memory_space=pltpu.SMEM)] * 2
            + [pl.BlockSpec(memory_space=pl.ANY)],
            out_specs=[pl.BlockSpec(memory_space=VMEM)]
            + [pl.BlockSpec(memory_space=pltpu.SMEM)] * 2,
            scratch_shapes=[pltpu.SemaphoreType.DMA((16,))],
            compiler_params=pltpu.CompilerParams(vmem_limit_bytes=LIMIT),
            cost_estimate=pl.CostEstimate(flops=0, bytes_accessed=tile_bytes, transcendentals=0),
        )(block_pairs[0, 0].T, tile_counts.reshape(-1), in_hbm)
    by_list = [lists, sizes]

    with jax.named_scope("gather_features"):
        step, swap = (lambda v, d: hop_col(v, 0, d)), (lambda v: hop_col(v, 1, 0))
        near_blocks, far_blocks = VMEM((4 * NEAR, TILE, 128), BF16), VMEM((12, TILE, 128), BF16)
        near = first_round(features, step, swap)
        near_mine, near[PAIR] = call(
            functools.partial(pack_body, NEAR),
            [near_blocks, VMEM((1024, 128), BF16)],
            near,
            after=[sizes],
        )
        far = second_round(near, step, swap)
        near_sib = hop_col(near_mine, 0, 0, 1)
    with jax.named_scope("forward_tiles"):
        total = VMEM((33, TILE, 128), F32)
        sums = call(
            forward_near_body,
            total,
            [tiles, near_mine, near_sib],
            by_list,
        )
        far_mine = call(functools.partial(pack_body, 3), far_blocks, far, after=[sums])
        far_sib = hop_col(far_mine, 0, 0, 1)
        sums = call(
            forward_far_body,
            total,
            [tiles, far_mine, sums],
            by_list,
            alias={4: 0},
            flops=share,
            nbytes=tile_bytes // 4,
        )
        f32, bf16 = VMEM((1024, 128), F32), VMEM((1024, 128), BF16)
        _, *partial = call(
            forward_last_body,
            [total, f32, bf16, bf16, f32, f32, bf16, bf16, bf16],
            [tiles, far_sib, sums],
            by_list,
            alias={4: 0},
            flops=share,
            nbytes=tile_bytes // 4,
        )
    with jax.named_scope("sum_aggregates"):
        step, swap = (lambda v, d: hop_row(v, 0, d)), (lambda v: hop_row(v, 1, 0))
        own, left, right, pair, opposite, *far = partial
        pair, opposite = call(
            add_round_body,
            [bf16, bf16],
            [pair, opposite, *first_sums(far, step, swap)],
            nbytes=4 << 20,
        )
        sums = second_sums(own, left, right, pair, opposite, step, swap)
    with jax.named_scope("dense"):
        longer = VMEM((144, 1024), BF16)
        block = VMEM((64, 256), F32)
        hidden, dpre, dz, *dz_to, quarter = call(
            dense_body,
            [
                jax.ShapeDtypeStruct((1024, 256), BF16),
                VMEM((1024, 256), BF16),
                VMEM((128, 1024), BF16),
                longer,
                longer,
                longer,
                block,
            ],
            [bias_term.reshape(1, 256), features, upstream, weight_self, weight_neigh, *sums],
            scratch=[VMEM((1024, 128), BF16), VMEM((256, 256), F32)],
            flops=5 * 2 * 1024 * 128 * 256,
            nbytes=6 << 20,
        )
    with jax.named_scope("gather_dz"):
        near = first_round(dz, step, swap, dz_to)
        quarter = call(
            ring_sum_body,
            VMEM((32, 1024), BF16),
            [quarter, near[OPPOSITE], near[LEFT], near[RIGHT]],
        )
        quarter_pair = swap(quarter)
        far = second_round(near, step, swap)
    with jax.named_scope("own_grad"):
        own_grad = call(
            own_grad_body,
            VMEM((128, 1024), F32),
            [dpre, weight_self],
            flops=2 * 1024 * 128 * 256,
            nbytes=2 << 20,
        )
    with jax.named_scope("backward_tiles"):
        total = VMEM((33, 128, TILE), F32)
        held = [VMEM((4 * NEAR, 128, TILE), BF16)]
        mine, sib = call(
            backward_near_body,
            [total, total],
            [tiles, *near],
            by_list,
            after=[own_grad],
            scratch=held,
            flops=2 * share,
            nbytes=tile_bytes // 2,
        )
        sib, sib_far, quarter = call(
            backward_sib_body,
            [total, VMEM((416, 1024), BF16), block],
            [tiles, *far, quarter, quarter_pair, sib],
            by_list,
            alias={8: 0},
            scratch=held,
            flops=share,
            nbytes=tile_bytes // 4,
        )
        mine = call(
            backward_mine_body,
            total,
            [tiles, *far, mine],
            by_list,
            scratch=held,
            alias={6: 0},
            flops=share,
            nbytes=tile_bytes // 4,
        )
    with jax.named_scope("sum_grads"):
        step, swap = (lambda v, d: hop_col(v, 0, d)), (lambda v: hop_col(v, 1, 0))
        f32, bf16 = VMEM((128, 1024), F32), VMEM((128, 1024), BF16)
        *far, quarter, sib_near, extra = call(
            add_sib_far_body,
            [longer, longer, longer, block, VMEM((5, 128, 1024), BF16), VMEM((16, 1024), BF16)],
            [mine, sib, hop_col(sib_far, 0, 0, 1), quarter],
            nbytes=3 << 20,
        )
        from_right, from_left, from_pair = first_sums(far, step, swap)
        sib_near = hop_col(sib_near, 0, 0, 1)
        left, right = call(add_sides_body, [bf16, bf16], [mine, sib_near], nbytes=2 << 20)
        left, right = step(left, -1), step(right, 1)
        from_opposite = step(extra, 2)
        extras = call(extras_body, VMEM((48, 1024), BF16), [from_right, from_left, from_opposite])
        came = [from_left, from_right, from_pair, from_opposite, swap(extras)]
        own, pair, opposite = call(
            add_near_body,
            [f32, bf16, bf16],
            [mine, sib_near, from_right, from_left, from_pair],
            after=[came[4], left, right],
            nbytes=5 << 20,
        )
        sums = [own, left, right, step(opposite, 2), swap(pair)]
    with jax.named_scope("sum_weights"):
        quarter = call(
            weight_sum_body,
            block,
            [quarter, *came],
            scratch=[VMEM((8, 64, 256), F32)],
            nbytes=1 << 20,
        )
        shape = jax.ShapeDtypeStruct((128, 256), F32)
        grad_self, grad_neigh = call(
            functools.partial(weight_join_body, float(nodes) ** -0.5),
            [shape, shape],
            [quarter, *[hop_row(quarter, 0, -k) for k in (1, 2, 3)]],
            scratch=[VMEM((256, 256), F32)],
            nbytes=1 << 20,
        )
    with jax.named_scope("finish"):
        grad_features = call(
            finish_body,
            jax.ShapeDtypeStruct((1024, 128), BF16),
            [own_grad, *sums],
            nbytes=4 << 20,
        )
    return hidden, grad_features, grad_self, grad_neigh


def solution(mesh):
    placed = (
        P(("row", "col"), None),
        P(),
        P(),
        P(),
        P(("row", "col"), None),
        P("row", "col", None, None, None),
        P("row", "col", None, None),
        P("row", "col"),
    )
    return jax.shard_map(
        shards,
        mesh=mesh,
        in_specs=placed,
        out_specs=(P(("row", "col"), None), P(("row", "col"), None), P(), P()),
        check_vma=False,
    )
```

```python
import functools

import jax
import jax.numpy as jnp
from jax import lax
from jax.experimental import pallas as pl
from jax.experimental.pallas import tpu as pltpu
from jax.sharding import PartitionSpec as P

TILE = 256
VMEM = pltpu.VMEM
BF16 = jnp.bfloat16
F32 = jnp.float32
LIMIT = 12 * 1024 * 1024
GROUP = 16
ROOM = 144

NEAR = 5
ORDER = [(0, 0), (0, 3), (0, 1), (1, 0), (0, 2), (1, 3), (1, 1), (1, 2)]
OWN, LEFT, RIGHT, PAIR, OPPOSITE, PAIR_LEFT, PAIR_RIGHT, PAIR_OPPOSITE = range(8)
PLACE = sum(ORDER.index((k // 4, k % 4)) << (4 * k) for k in range(8))


def hop_col(value, dy, dx, dc=0):
    pairs = []
    for y in range(2):
        for x in range(4):
            for c in range(2):
                to = (((y + dy) % 2) * 4 + (x + dx) % 4) * 2 + (c + dc) % 2
                pairs.append(((y * 4 + x) * 2 + c, to))
    return lax.ppermute(value, "col", pairs)


def hop_row(value, dy, dz):
    pairs = []
    for z in range(4):
        for y in range(2):
            pairs.append((z * 2 + y, ((z + dz) % 4) * 2 + (y + dy) % 2))
    return lax.ppermute(value, "row", pairs)


def in_vmem(*values):
    return [pltpu.with_memory_space_constraint(v, VMEM) for v in values]


def vmem_specs(n):
    return [pl.BlockSpec(memory_space=VMEM)] * n


def call(
    body,
    outs,
    vmem_args,
    smem_args=(),
    after=(),
    scratch=(),
    alias=None,
    flops=0,
    nbytes=0,
):
    single = not isinstance(outs, (list, tuple))
    skip = len(smem_args) + len(vmem_args)

    def run(*refs):
        body(*refs[:skip], *refs[skip + len(after) :])

    return pl.pallas_call(
        run,
        out_shape=outs,
        in_specs=[pl.BlockSpec(memory_space=pltpu.SMEM)] * len(smem_args)
        + vmem_specs(len(vmem_args))
        + [pl.BlockSpec(memory_space=pl.ANY)] * len(after),
        out_specs=pl.BlockSpec(memory_space=VMEM) if single else vmem_specs(len(outs)),
        scratch_shapes=list(scratch),
        input_output_aliases=alias or {},
        compiler_params=pltpu.CompilerParams(vmem_limit_bytes=LIMIT),
        cost_estimate=pl.CostEstimate(flops=flops, bytes_accessed=nbytes, transcendentals=0),
    )(*smem_args, *in_vmem(*vmem_args), *after)


def write_extra(ref, row, value):
    for j in range(4):
        ref[row : row + 16, j * 256 : (j + 1) * 256] = value[16 * j : 16 * j + 16].astype(BF16)


def read_extra(ref, row):
    return jnp.concatenate(
        [ref[row : row + 16, j * 256 : (j + 1) * 256].astype(F32) for j in range(4)], axis=0
    )


def rounded(value):
    return value.astype(BF16).astype(F32)


def write_fine(ref, row, value):
    write_extra(ref, row, value)
    write_extra(ref, row + 16, value - rounded(value))


def read_fine(ref, row):
    return read_extra(ref, row) + read_extra(ref, row + 16)


def fine(value):
    high = rounded(value)
    return high + rounded(value - high)


def places():
    return lax.axis_index("col"), lax.axis_index("row")


def first_round(value, step, swap, to=None):
    to = to or [value] * 3
    return [value, step(to[0], 1), step(to[1], -1), swap(value), step(to[2], 2)]


def second_round(near, step, swap):
    return [step(near[PAIR], 1), step(near[PAIR], -1), swap(near[OPPOSITE])]


def place_of(index, me, other_bit, ring_shift):
    other = ((index ^ me) >> other_bit) & 1
    offset = ((index >> ring_shift) - (me >> ring_shift)) & 3
    return (PLACE >> ((other * 4 + offset) * 4)) & 15


def bring(first, last, stored, tiles, sems):
    copies = []
    for k, at in enumerate(range(first, last, 8)):
        part = pl.ds(at, 8)
        copies.append(pltpu.make_async_copy(stored.at[part], tiles.at[part], sems.at[k]))
        copies[-1].start()
    return copies


def plan_body(pairs, count, stored, tiles, lists, sizes, sems):
    copies = bring(0, 128, stored, tiles, sems)
    col, row = places()

    def put(base, which, entry, counts):
        at = (counts >> (which * 8)) & 255
        lists[(base + which) * ROOM + at] = entry
        return counts + (jnp.int32(1) << (which * 8))

    def sort(i, carry):
        d = pairs[0, i]
        s = pairs[1, i]
        c = s >> 2
        q = d >> 2
        sib = (c ^ col) & 1
        source = place_of(c, col, 3, 1) * 4 + (s & 3)
        target = place_of(q, row, 0, 1) * 4 + (d & 3)
        far = (source >= 4 * NEAR).astype(jnp.int32)
        entry = i | (target << 8) | ((source - far * 4 * NEAR) << 16)
        ahead = put(0, far * 2 + sib, entry, carry[0])
        far = (target >= 4 * NEAR).astype(jnp.int32)
        entry = i | ((target - far * 4 * NEAR) << 8) | (source << 16)
        back = put(4, far * 2 + sib, entry, carry[1])
        return ahead, back

    counts = lax.fori_loop(0, count[0], sort, (jnp.int32(0), jnp.int32(0)))
    for k in range(8):
        at = (counts[k // 4] >> (8 * (k % 4))) & 255
        sizes[k] = at
        for j in range(GROUP - 1):
            lists[k * ROOM + at + j] = 32 << 8 if k < 4 else 32 << 16
    for copy in copies:
        copy.wait()


def over_list(which, lists, sizes, product, total, to_target):
    def step(g, carry):
        news = []
        for j in range(GROUP):
            entry = lists[which * ROOM + g * GROUP + j]
            i = entry & 255
            d = (entry >> 8) & 255
            s = entry >> 16
            news.append((d if to_target else s, product(i, d, s)))
        for at, new in news:
            total[at] += new
        return carry

    lax.fori_loop(0, (sizes[which] + GROUP - 1) // GROUP, step, 0)


def pack_body(n, *rest):
    for k in range(n):
        rest[n][4 * k : 4 * k + 4] = rest[k][...].reshape(4, TILE, 128)
    for out in rest[n + 1 :]:
        out[...] = rest[PAIR][...]


def forward_step(lists, sizes, tiles, which, blocks, total):
    def product(i, d, s):
        return jnp.dot(tiles[i], blocks[s], preferred_element_type=F32)

    over_list(which, lists, sizes, product, total, True)


def forward_near_body(lists, sizes, tiles, mine, sib, total):
    total[...] = jnp.zeros_like(total)
    forward_step(lists, sizes, tiles, 0, mine, total)
    forward_step(lists, sizes, tiles, 1, sib, total)


def forward_far_body(lists, sizes, tiles, mine, before, total):
    forward_step(lists, sizes, tiles, 2, mine, total)


def forward_last_body(lists, sizes, tiles, sib, before, total, *outs):
    forward_step(lists, sizes, tiles, 3, sib, total)
    for k in range(8):
        outs[k][...] = total[4 * k : 4 * k + 4].reshape(1024, 128).astype(outs[k].dtype)


def hold_dz(parts, held):
    for k, ref in enumerate(parts):
        for b in range(4):
            held[4 * k + b] = ref[0:128, b * TILE : (b + 1) * TILE]


def backward_step(lists, sizes, tiles, which, held, total):
    def product(i, d, s):
        return jnp.dot(held[d], tiles[i], preferred_element_type=F32)

    over_list(which, lists, sizes, product, total, False)


def backward_near_body(lists, sizes, tiles, *rest):
    parts, (mine, sib, held) = rest[:NEAR], rest[NEAR:]
    hold_dz(parts, held)
    mine[...] = jnp.zeros_like(mine)
    sib[...] = jnp.zeros_like(sib)
    backward_step(lists, sizes, tiles, 5, held, sib)
    backward_step(lists, sizes, tiles, 4, held, mine)


def write_places(total, first, outs):
    for k, ref in enumerate(outs):
        for b in range(4):
            new = total[4 * (first + k) + b].astype(ref.dtype)
            ref[0:128, b * TILE : (b + 1) * TILE] = new


def backward_sib_body(lists, sizes, tiles, *rest):
    parts, (quarter, other, before, sib, far, quarter_out, held) = rest[:3], rest[3:]
    hold_dz(parts, held)
    backward_step(lists, sizes, tiles, 7, held, sib)
    write_places(sib, PAIR_LEFT, [far.at[pl.ds(128 * k, 128)] for k in range(3)])
    total = read_fine(quarter, 0) + read_fine(other, 0)
    quarter_out[...] = fine(total)
    write_fine(far, 384, total)


def backward_mine_body(lists, sizes, tiles, *rest):
    parts, (before, mine, held) = rest[:3], rest[3:]
    hold_dz(parts, held)
    backward_step(lists, sizes, tiles, 6, held, mine)


def add_sib_far_body(mine, sib, got, quarter, to_left, to_right, to_pair, quarter_out, near):
    for k, ref in enumerate((to_left, to_right, to_pair)):
        for b in range(4):
            nodes = slice(b * TILE, (b + 1) * TILE)
            new = mine[4 * (PAIR_LEFT + k) + b] + got[128 * k : 128 * k + 128, nodes].astype(F32)
            ref[0:128, nodes] = new.astype(BF16)
    total = quarter[...] + read_fine(got, 384)
    quarter_out[...] = fine(total)
    write_fine(to_pair, 128, total)
    write_places(sib, OWN, [near.at[k] for k in range(5)])


def add_body(own, *rest):
    new = own[...]
    for ref in rest[:-1]:
        new = new + ref[...].astype(F32)
    rest[-1][...] = new.astype(rest[-1].dtype)


def add_cores(mine, place, got, b):
    return mine[4 * place + b] + got[place, :, b * TILE : (b + 1) * TILE].astype(F32)


def add_ring_body(mine, got, from_pair, quarter, left, right, opposite, quarter_out):
    total = quarter[...] + read_fine(from_pair, 128)
    quarter_out[...] = rounded(total)
    for place, ref in ((LEFT, left), (RIGHT, right), (OPPOSITE, opposite)):
        for b in range(4):
            nodes = slice(b * TILE, (b + 1) * TILE)
            new = add_cores(mine, place, got, b)
            if place == OPPOSITE:
                new = new + from_pair[0:128, nodes].astype(F32)
            ref[0:128, nodes] = new.astype(BF16)
        write_extra(ref, 128, total)


def add_pair_body(mine, got, from_right, from_left, out):
    for b in range(4):
        nodes = slice(b * TILE, (b + 1) * TILE)
        came = from_right[:, nodes].astype(F32) + from_left[:, nodes].astype(F32)
        out[:, nodes] = (add_cores(mine, PAIR, got, b) + came).astype(BF16)


def dense_body(bias, feats, upstream, w_self, w_neigh, *rest):
    sums = rest[:5]
    hidden, dpre_out, dz_out, *dz_to, quarter, agg_out, grads = rest[5:]
    for b in range(4):
        rows = slice(b * TILE, (b + 1) * TILE)
        agg = sums[0][rows]
        for ref in sums[1:]:
            agg = agg + ref[rows].astype(F32)
        agg = agg.astype(BF16)
        agg_out[rows] = agg
        pre = jnp.dot(feats[rows], w_self[...], preferred_element_type=F32)
        pre = pre + jnp.dot(agg, w_neigh[...], preferred_element_type=F32) + bias[...]
        sig = jax.nn.sigmoid(pre)
        hidden[rows] = (pre * sig).astype(BF16)
        slope = sig * (1.0 + pre * (1.0 - sig))
        dpre = (upstream[rows].astype(F32) * slope).astype(BF16)
        dpre_out[rows] = dpre
        dz = lax.dot_general(
            w_neigh[...], dpre, (((1,), (1,)), ((), ())), preferred_element_type=F32
        ).astype(BF16)
        for ref in [dz_out, *dz_to]:
            ref[0:128, rows] = dz
    over_nodes = (((0,), (0,)), ((), ()))
    grads[0:128] = lax.dot_general(
        feats[...], dpre_out[...], over_nodes, preferred_element_type=F32
    )
    grads[128:256] = lax.dot_general(
        agg_out[...], dpre_out[...], over_nodes, preferred_element_type=F32
    )
    z = lax.axis_index("row") >> 1

    def piece(k):
        return grads[pl.ds(pl.multiple_of(((z + k) & 3) * 64, 64), 64), :]

    quarter[...] = piece(0)
    for ref, k in zip(dz_to, (1, 3, 2)):
        write_extra(ref, 128, piece(k))


def ring_sum_body(quarter, opposite, left, right, out):
    total = quarter[...] + read_extra(left, 128)
    write_fine(out, 0, total + (read_extra(right, 128) + read_extra(opposite, 128)))


def own_grad_body(dpre, w_self, own_grad):
    own_grad[...] = lax.dot_general(
        w_self[...], dpre[...], (((1,), (1,)), ((), ())), preferred_element_type=F32
    )


def finish_body(own_grad, mine, got, *rest):
    out = rest[-1]
    for b in range(4):
        nodes = slice(b * TILE, (b + 1) * TILE)
        total = own_grad[:, nodes] + add_cores(mine, OWN, got, b)
        for ref in rest[:-1]:
            total = total + ref[0:128, nodes].astype(F32)
        out[nodes] = total.T.astype(BF16)


def weight_sum_body(own, left, right, opposite, out, parts):
    x = (lax.axis_index("col") >> 1) & 3
    parts[x] = own[...]
    for k, ref in ((3, left), (1, right), (2, opposite)):
        parts[(x + k) & 3] = read_extra(ref, 128)
    out[...] = ((parts[0] + parts[1]) + parts[2]) + parts[3]


def weight_join_body(scale, own, *rest):
    others, (grad_self, grad_neigh, held) = rest[:3], rest[3:]
    z = lax.axis_index("row") >> 1
    for k, ref in enumerate([own, *others]):
        at = pl.multiple_of(((z + k) & 3) * 64, 64)
        held[pl.ds(at, 64), :] = ref[...] * scale
    grad_self[...] = held[0:128]
    grad_neigh[...] = held[128:256]


def shards(
    features, weight_self, weight_neigh, bias_term, upstream, tile_values, block_pairs, tile_counts
):
    nodes = 131072
    tile_bytes = 128 * TILE * TILE * 2
    share = 32 * 2 * TILE * TILE * 128
    in_hbm = pltpu.with_memory_space_constraint(tile_values.reshape(128, TILE, TILE), pltpu.HBM)
    with jax.named_scope("plan"):
        tiles, lists, sizes = pl.pallas_call(
            plan_body,
            out_shape=[
                VMEM((128, TILE, TILE), BF16),
                pltpu.SMEM((8 * ROOM,), jnp.int32),
                pltpu.SMEM((8,), jnp.int32),
            ],
            in_specs=[pl.BlockSpec(memory_space=pltpu.SMEM)] * 2
            + [pl.BlockSpec(memory_space=pl.ANY)],
            out_specs=[pl.BlockSpec(memory_space=VMEM)]
            + [pl.BlockSpec(memory_space=pltpu.SMEM)] * 2,
            scratch_shapes=[pltpu.SemaphoreType.DMA((16,))],
            compiler_params=pltpu.CompilerParams(vmem_limit_bytes=LIMIT),
            cost_estimate=pl.CostEstimate(flops=0, bytes_accessed=tile_bytes, transcendentals=0),
        )(block_pairs[0, 0].T, tile_counts.reshape(-1), in_hbm)
    by_list = [lists, sizes]

    with jax.named_scope("gather_features"):
        step, swap = (lambda v, d: hop_col(v, 0, d)), (lambda v: hop_col(v, 1, 0))
        near_blocks, far_blocks = VMEM((4 * NEAR, TILE, 128), BF16), VMEM((12, TILE, 128), BF16)
        near = first_round(features, step, swap)
        near_mine, near[PAIR] = call(
            functools.partial(pack_body, NEAR),
            [near_blocks, VMEM((1024, 128), BF16)],
            near,
            after=[sizes],
        )
        far = second_round(near, step, swap)
        near_sib = hop_col(near_mine, 0, 0, 1)
    with jax.named_scope("forward_tiles"):
        total = VMEM((33, TILE, 128), F32)
        sums = call(
            forward_near_body,
            total,
            [tiles, near_mine, near_sib],
            by_list,
        )
        far_mine = call(functools.partial(pack_body, 3), far_blocks, far, after=[sums])
        far_sib = hop_col(far_mine, 0, 0, 1)
        sums = call(
            forward_far_body,
            total,
            [tiles, far_mine, sums],
            by_list,
            alias={4: 0},
            flops=share,
            nbytes=tile_bytes // 4,
        )
        f32, bf16 = VMEM((1024, 128), F32), VMEM((1024, 128), BF16)
        _, *partial = call(
            forward_last_body,
            [total, f32, bf16, bf16, f32, f32, bf16, bf16, bf16],
            [tiles, far_sib, sums],
            by_list,
            alias={4: 0},
            flops=share,
            nbytes=tile_bytes // 4,
        )
    with jax.named_scope("sum_aggregates"):
        step, swap = (lambda v, d: hop_row(v, 0, d)), (lambda v: hop_row(v, 1, 0))
        own, left, right, pair, opposite, *far = partial
        from_right, from_left, from_pair = step(far[0], -1), step(far[1], 1), swap(far[2])
        opposite = call(add_body, bf16, [opposite, from_pair], nbytes=1 << 20)
        pair = call(add_body, bf16, [pair, from_right, from_left], nbytes=1 << 20)
        sums = [own, step(left, -1), step(right, 1), step(opposite, 2), swap(pair)]
    with jax.named_scope("dense"):
        longer = VMEM((144, 1024), BF16)
        block = VMEM((64, 256), F32)
        hidden, dpre, dz, *dz_to, quarter = call(
            dense_body,
            [
                jax.ShapeDtypeStruct((1024, 256), BF16),
                VMEM((1024, 256), BF16),
                VMEM((128, 1024), BF16),
                longer,
                longer,
                longer,
                block,
            ],
            [bias_term.reshape(1, 256), features, upstream, weight_self, weight_neigh, *sums],
            scratch=[VMEM((1024, 128), BF16), VMEM((256, 256), F32)],
            flops=5 * 2 * 1024 * 128 * 256,
            nbytes=6 << 20,
        )
    with jax.named_scope("gather_dz"):
        near = first_round(dz, step, swap, dz_to)
        quarter = call(
            ring_sum_body,
            VMEM((32, 1024), BF16),
            [quarter, near[OPPOSITE], near[LEFT], near[RIGHT]],
        )
        quarter_pair = swap(quarter)
        far = second_round(near, step, swap)
    with jax.named_scope("own_grad"):
        own_grad = call(
            own_grad_body,
            VMEM((128, 1024), F32),
            [dpre, weight_self],
            flops=2 * 1024 * 128 * 256,
            nbytes=2 << 20,
        )
    with jax.named_scope("backward_tiles"):
        total = VMEM((33, 128, TILE), F32)
        held = [VMEM((4 * NEAR, 128, TILE), BF16)]
        mine, sib = call(
            backward_near_body,
            [total, total],
            [tiles, *near],
            by_list,
            after=[own_grad],
            scratch=held,
            flops=2 * share,
            nbytes=tile_bytes // 2,
        )
        sib, sib_far, quarter = call(
            backward_sib_body,
            [total, VMEM((416, 1024), BF16), block],
            [tiles, *far, quarter, quarter_pair, sib],
            by_list,
            alias={8: 0},
            scratch=held,
            flops=share,
            nbytes=tile_bytes // 4,
        )
        mine = call(
            backward_mine_body,
            total,
            [tiles, *far, mine],
            by_list,
            scratch=held,
            alias={6: 0},
            flops=share,
            nbytes=tile_bytes // 4,
        )
    with jax.named_scope("sum_grads"):
        step, swap = (lambda v, d: hop_col(v, 0, d)), (lambda v: hop_col(v, 1, 0))
        f32, bf16 = VMEM((128, 1024), F32), VMEM((128, 1024), BF16)
        *far, quarter, sib_near = call(
            add_sib_far_body,
            [bf16, bf16, VMEM((160, 1024), BF16), block, VMEM((5, 128, 1024), BF16)],
            [mine, sib, hop_col(sib_far, 0, 0, 1), quarter],
            nbytes=3 << 20,
        )
        from_right, from_left, from_pair = step(far[0], -1), step(far[1], 1), swap(far[2])
        sib_near = hop_col(sib_near, 0, 0, 1)
        left, right, opposite, quarter = call(
            add_ring_body,
            [longer, longer, longer, block],
            [mine, sib_near, from_pair, quarter],
            nbytes=2 << 20,
        )
        pair = call(add_pair_body, bf16, [mine, sib_near, from_right, from_left], nbytes=1 << 20)
        ring = [step(right, 1), step(left, -1), step(opposite, 2)]
        sums = [*ring, swap(pair)]
    with jax.named_scope("sum_weights"):
        quarter = call(
            weight_sum_body, block, [quarter, *ring], scratch=[VMEM((4, 64, 256), F32)]
        )
        shape = jax.ShapeDtypeStruct((128, 256), F32)
        grad_self, grad_neigh = call(
            functools.partial(weight_join_body, float(nodes) ** -0.5),
            [shape, shape],
            [quarter, *[hop_row(quarter, 0, -k) for k in (1, 2, 3)]],
            scratch=[VMEM((256, 256), F32)],
            nbytes=1 << 20,
        )
    with jax.named_scope("finish"):
        grad_features = call(
            finish_body,
            jax.ShapeDtypeStruct((1024, 128), BF16),
            [own_grad, mine, sib_near, *sums],
            nbytes=4 << 20,
        )
    return hidden, grad_features, grad_self, grad_neigh


def solution(mesh):
    placed = (
        P(("row", "col"), None),
        P(),
        P(),
        P(),
        P(("row", "col"), None),
        P("row", "col", None, None, None),
        P("row", "col", None, None),
        P("row", "col"),
    )
    return jax.shard_map(
        shards,
        mesh=mesh,
        in_specs=placed,
        out_specs=(P(("row", "col"), None), P(("row", "col"), None), P(), P()),
        check_vma=False,
    )
```

```python
import functools

import jax
import jax.numpy as jnp
from jax import lax
from jax.experimental import pallas as pl
from jax.experimental.pallas import tpu as pltpu
from jax.sharding import PartitionSpec as P

TILE = 256
VMEM = pltpu.VMEM
BF16 = jnp.bfloat16
F32 = jnp.float32
LIMIT = 12 * 1024 * 1024
GROUP = 16
ROOM = 144

NEAR = 5
ORDER = [(0, 0), (0, 3), (0, 1), (1, 0), (0, 2), (1, 3), (1, 1), (1, 2)]
OWN, LEFT, RIGHT, PAIR, OPPOSITE, PAIR_LEFT, PAIR_RIGHT, PAIR_OPPOSITE = range(8)
PLACE = sum(ORDER.index((k // 4, k % 4)) << (4 * k) for k in range(8))


def hop_col(value, dy, dx, dc=0):
    pairs = []
    for y in range(2):
        for x in range(4):
            for c in range(2):
                to = (((y + dy) % 2) * 4 + (x + dx) % 4) * 2 + (c + dc) % 2
                pairs.append(((y * 4 + x) * 2 + c, to))
    return lax.ppermute(value, "col", pairs)


def hop_row(value, dy, dz):
    pairs = []
    for z in range(4):
        for y in range(2):
            pairs.append((z * 2 + y, ((z + dz) % 4) * 2 + (y + dy) % 2))
    return lax.ppermute(value, "row", pairs)


def in_vmem(*values):
    return [pltpu.with_memory_space_constraint(v, VMEM) for v in values]


def vmem_specs(n):
    return [pl.BlockSpec(memory_space=VMEM)] * n


def call(
    body,
    outs,
    vmem_args,
    smem_args=(),
    after=(),
    scratch=(),
    alias=None,
    flops=0,
    nbytes=0,
):
    single = not isinstance(outs, (list, tuple))
    skip = len(smem_args) + len(vmem_args)

    def run(*refs):
        body(*refs[:skip], *refs[skip + len(after) :])

    return pl.pallas_call(
        run,
        out_shape=outs,
        in_specs=[pl.BlockSpec(memory_space=pltpu.SMEM)] * len(smem_args)
        + vmem_specs(len(vmem_args))
        + [pl.BlockSpec(memory_space=pl.ANY)] * len(after),
        out_specs=pl.BlockSpec(memory_space=VMEM) if single else vmem_specs(len(outs)),
        scratch_shapes=list(scratch),
        input_output_aliases=alias or {},
        compiler_params=pltpu.CompilerParams(vmem_limit_bytes=LIMIT),
        cost_estimate=pl.CostEstimate(flops=flops, bytes_accessed=nbytes, transcendentals=0),
    )(*smem_args, *in_vmem(*vmem_args), *after)


def write_extra(ref, row, value):
    for j in range(4):
        ref[row : row + 16, j * 256 : (j + 1) * 256] = value[16 * j : 16 * j + 16].astype(BF16)


def read_extra(ref, row):
    return jnp.concatenate(
        [ref[row : row + 16, j * 256 : (j + 1) * 256].astype(F32) for j in range(4)], axis=0
    )


def rounded(value):
    return value.astype(BF16).astype(F32)


def write_fine(ref, row, value):
    write_extra(ref, row, value)
    write_extra(ref, row + 16, value - rounded(value))


def read_fine(ref, row):
    return read_extra(ref, row) + read_extra(ref, row + 16)


def fine(value):
    high = rounded(value)
    return high + rounded(value - high)


def places():
    return lax.axis_index("col"), lax.axis_index("row")


def first_round(value, step, swap, to=None):
    to = to or [value] * 3
    return [value, step(to[0], 1), step(to[1], -1), swap(value), step(to[2], 2)]


def second_round(near, step, swap):
    return [step(near[PAIR], 1), step(near[PAIR], -1), swap(near[OPPOSITE])]


def place_of(index, me, other_bit, ring_shift):
    other = ((index ^ me) >> other_bit) & 1
    offset = ((index >> ring_shift) - (me >> ring_shift)) & 3
    return (PLACE >> ((other * 4 + offset) * 4)) & 15


def bring(first, last, stored, tiles, sems):
    copies = []
    for k, at in enumerate(range(first, last, 8)):
        part = pl.ds(at, 8)
        copies.append(pltpu.make_async_copy(stored.at[part], tiles.at[part], sems.at[k]))
        copies[-1].start()
    return copies


def plan_body(pairs, count, stored, tiles, lists, sizes, sems):
    copies = bring(0, 128, stored, tiles, sems)
    col, row = places()

    def put(base, which, entry, counts):
        at = (counts >> (which * 8)) & 255
        lists[(base + which) * ROOM + at] = entry
        return counts + (jnp.int32(1) << (which * 8))

    def sort(i, carry):
        d = pairs[0, i]
        s = pairs[1, i]
        c = s >> 2
        q = d >> 2
        sib = (c ^ col) & 1
        source = place_of(c, col, 3, 1) * 4 + (s & 3)
        target = place_of(q, row, 0, 1) * 4 + (d & 3)
        far = (source >= 4 * NEAR).astype(jnp.int32)
        entry = i | (target << 8) | ((source - far * 4 * NEAR) << 16)
        ahead = put(0, far * 2 + sib, entry, carry[0])
        far = (target >= 4 * NEAR).astype(jnp.int32)
        entry = i | ((target - far * 4 * NEAR) << 8) | (source << 16)
        back = put(4, far * 2 + sib, entry, carry[1])
        return ahead, back

    counts = lax.fori_loop(0, count[0], sort, (jnp.int32(0), jnp.int32(0)))
    for k in range(8):
        at = (counts[k // 4] >> (8 * (k % 4))) & 255
        sizes[k] = at
        for j in range(GROUP - 1):
            lists[k * ROOM + at + j] = 32 << 8 if k < 4 else 32 << 16
    for copy in copies:
        copy.wait()


def over_list(which, lists, sizes, product, total, to_target):
    def step(g, carry):
        news = []
        for j in range(GROUP):
            entry = lists[which * ROOM + g * GROUP + j]
            i = entry & 255
            d = (entry >> 8) & 255
            s = entry >> 16
            news.append((d if to_target else s, product(i, d, s)))
        for at, new in news:
            total[at] += new
        return carry

    lax.fori_loop(0, (sizes[which] + GROUP - 1) // GROUP, step, 0)


def pack_body(n, *rest):
    for k in range(n):
        rest[n][4 * k : 4 * k + 4] = rest[k][...].reshape(4, TILE, 128)
    for out in rest[n + 1 :]:
        out[...] = rest[PAIR][...]


def forward_step(lists, sizes, tiles, which, blocks, total):
    def product(i, d, s):
        return jnp.dot(tiles[i], blocks[s], preferred_element_type=F32)

    over_list(which, lists, sizes, product, total, True)


def forward_near_body(lists, sizes, tiles, mine, sib, total):
    total[...] = jnp.zeros_like(total)
    forward_step(lists, sizes, tiles, 0, mine, total)
    forward_step(lists, sizes, tiles, 1, sib, total)


def forward_far_body(lists, sizes, tiles, mine, before, total):
    forward_step(lists, sizes, tiles, 2, mine, total)


def forward_last_body(lists, sizes, tiles, sib, before, total, *outs):
    forward_step(lists, sizes, tiles, 3, sib, total)
    for k in range(8):
        outs[k][...] = total[4 * k : 4 * k + 4].reshape(1024, 128).astype(outs[k].dtype)


def hold_dz(parts, held):
    for k, ref in enumerate(parts):
        for b in range(4):
            held[4 * k + b] = ref[0:128, b * TILE : (b + 1) * TILE]


def backward_step(lists, sizes, tiles, which, held, total):
    def product(i, d, s):
        return jnp.dot(held[d], tiles[i], preferred_element_type=F32)

    over_list(which, lists, sizes, product, total, False)


def backward_near_body(lists, sizes, tiles, *rest):
    parts, (mine, sib, held) = rest[:NEAR], rest[NEAR:]
    hold_dz(parts, held)
    mine[...] = jnp.zeros_like(mine)
    sib[...] = jnp.zeros_like(sib)
    backward_step(lists, sizes, tiles, 5, held, sib)
    backward_step(lists, sizes, tiles, 4, held, mine)


def write_places(total, first, outs):
    for k, ref in enumerate(outs):
        for b in range(4):
            new = total[4 * (first + k) + b].astype(ref.dtype)
            ref[0:128, b * TILE : (b + 1) * TILE] = new


def backward_sib_body(lists, sizes, tiles, *rest):
    parts, (quarter, other, before, sib, far, quarter_out, held) = rest[:3], rest[3:]
    hold_dz(parts, held)
    backward_step(lists, sizes, tiles, 7, held, sib)
    write_places(sib, PAIR_LEFT, [far.at[pl.ds(128 * k, 128)] for k in range(3)])
    total = read_fine(quarter, 0) + read_fine(other, 0)
    quarter_out[...] = fine(total)
    write_fine(far, 384, total)


def backward_mine_body(lists, sizes, tiles, *rest):
    parts, (before, mine, held) = rest[:3], rest[3:]
    hold_dz(parts, held)
    backward_step(lists, sizes, tiles, 6, held, mine)


def add_sib_far_body(mine, sib, got, quarter, *rest):
    outs, (quarter_out, near, extra) = rest[:3], rest[3:]
    total = quarter[...] + read_fine(got, 384)
    quarter_out[...] = rounded(total)
    for k, ref in enumerate(outs):
        for b in range(4):
            nodes = slice(b * TILE, (b + 1) * TILE)
            new = mine[4 * (PAIR_LEFT + k) + b] + got[128 * k : 128 * k + 128, nodes].astype(F32)
            ref[0:128, nodes] = new.astype(BF16)
    for ref, row in ((outs[0], 128), (outs[1], 128), (extra, 0)):
        write_extra(ref, row, total)
    write_places(sib, OWN, [near.at[k] for k in range(5)])


def add_round_body(pair, opposite, from_right, from_left, from_pair, pair_out, opposite_out):
    new = pair[...] + (from_right[...].astype(F32) + from_left[...].astype(F32))
    pair_out[...] = new.astype(BF16)
    opposite_out[...] = (opposite[...] + from_pair[...].astype(F32)).astype(BF16)


def add_sides_body(mine, got, left, right):
    for place, ref in ((LEFT, left), (RIGHT, right)):
        for b in range(4):
            nodes = slice(b * TILE, (b + 1) * TILE)
            new = mine[4 * place + b] + got[place, :, nodes].astype(F32)
            ref[:, nodes] = new.astype(BF16)


def add_near_body(mine, got, from_right, from_left, from_pair, *outs):
    more = {PAIR: [from_right, from_left], OPPOSITE: [from_pair]}
    for place, ref in zip((OWN, PAIR, OPPOSITE), outs):
        for b in range(4):
            nodes = slice(b * TILE, (b + 1) * TILE)
            new = mine[4 * place + b] + got[place, :, nodes].astype(F32)
            for came in more.get(place, []):
                new = new + came[0:128, nodes].astype(F32)
            ref[:, nodes] = new.astype(ref.dtype)


def ring_x_body(quarter, from_right, from_left, from_opposite, out, parts):
    x = (lax.axis_index("col") >> 1) & 3
    parts[x] = quarter[...]
    parts[(x + 3) & 3] = read_extra(from_left, 128)
    parts[(x + 1) & 3] = read_extra(from_right, 128)
    parts[(x + 2) & 3] = read_extra(from_opposite, 0)
    write_fine(out, 0, ((parts[0] + parts[1]) + parts[2]) + parts[3])


def first_sums(parts, step, swap):
    return step(parts[0], -1), step(parts[1], 1), swap(parts[2])


def second_sums(own, left, right, pair, opposite, step, swap):
    return [own, step(left, -1), step(right, 1), step(opposite, 2), swap(pair)]


def dense_body(bias, feats, upstream, w_self, w_neigh, *rest):
    sums = rest[:5]
    hidden, dpre_out, dz_out, *dz_to, quarter, agg_out, grads = rest[5:]
    for b in range(4):
        rows = slice(b * TILE, (b + 1) * TILE)
        agg = sums[0][rows]
        for ref in sums[1:]:
            agg = agg + ref[rows].astype(F32)
        agg = agg.astype(BF16)
        agg_out[rows] = agg
        pre = jnp.dot(feats[rows], w_self[...], preferred_element_type=F32)
        pre = pre + jnp.dot(agg, w_neigh[...], preferred_element_type=F32) + bias[...]
        sig = jax.nn.sigmoid(pre)
        hidden[rows] = (pre * sig).astype(BF16)
        slope = sig * (1.0 + pre * (1.0 - sig))
        dpre = (upstream[rows].astype(F32) * slope).astype(BF16)
        dpre_out[rows] = dpre
        dz = lax.dot_general(
            w_neigh[...], dpre, (((1,), (1,)), ((), ())), preferred_element_type=F32
        ).astype(BF16)
        for ref in [dz_out, *dz_to]:
            ref[0:128, rows] = dz
    over_nodes = (((0,), (0,)), ((), ()))
    grads[0:128] = lax.dot_general(
        feats[...], dpre_out[...], over_nodes, preferred_element_type=F32
    )
    grads[128:256] = lax.dot_general(
        agg_out[...], dpre_out[...], over_nodes, preferred_element_type=F32
    )
    z = lax.axis_index("row") >> 1

    def piece(k):
        return grads[pl.ds(pl.multiple_of(((z + k) & 3) * 64, 64), 64), :]

    quarter[...] = piece(0)
    for ref, k in zip(dz_to, (1, 3, 2)):
        write_extra(ref, 128, piece(k))


def ring_sum_body(quarter, opposite, left, right, out):
    total = quarter[...] + read_extra(left, 128)
    write_fine(out, 0, total + (read_extra(right, 128) + read_extra(opposite, 128)))


def own_grad_body(dpre, w_self, own_grad):
    own_grad[...] = lax.dot_general(
        w_self[...], dpre[...], (((1,), (1,)), ((), ())), preferred_element_type=F32
    )


def finish_body(own_grad, *rest):
    out = rest[-1]
    for b in range(4):
        nodes = slice(b * TILE, (b + 1) * TILE)
        total = own_grad[:, nodes]
        for ref in rest[:-1]:
            total = total + ref[0:128, nodes].astype(F32)
        out[nodes] = total.T.astype(BF16)


def weight_sum_body(ring, pair, out):
    out[...] = read_fine(ring, 0) + read_fine(pair, 0)


def weight_join_body(scale, own, *rest):
    others, (grad_self, grad_neigh, held) = rest[:3], rest[3:]
    z = lax.axis_index("row") >> 1
    for k, ref in enumerate([own, *others]):
        at = pl.multiple_of(((z + k) & 3) * 64, 64)
        held[pl.ds(at, 64), :] = ref[...] * scale
    grad_self[...] = held[0:128]
    grad_neigh[...] = held[128:256]


def shards(
    features, weight_self, weight_neigh, bias_term, upstream, tile_values, block_pairs, tile_counts
):
    nodes = 131072
    tile_bytes = 128 * TILE * TILE * 2
    share = 32 * 2 * TILE * TILE * 128
    in_hbm = pltpu.with_memory_space_constraint(tile_values.reshape(128, TILE, TILE), pltpu.HBM)
    with jax.named_scope("plan"):
        tiles, lists, sizes = pl.pallas_call(
            plan_body,
            out_shape=[
                VMEM((128, TILE, TILE), BF16),
                pltpu.SMEM((8 * ROOM,), jnp.int32),
                pltpu.SMEM((8,), jnp.int32),
            ],
            in_specs=[pl.BlockSpec(memory_space=pltpu.SMEM)] * 2
            + [pl.BlockSpec(memory_space=pl.ANY)],
            out_specs=[pl.BlockSpec(memory_space=VMEM)]
            + [pl.BlockSpec(memory_space=pltpu.SMEM)] * 2,
            scratch_shapes=[pltpu.SemaphoreType.DMA((16,))],
            compiler_params=pltpu.CompilerParams(vmem_limit_bytes=LIMIT),
            cost_estimate=pl.CostEstimate(flops=0, bytes_accessed=tile_bytes, transcendentals=0),
        )(block_pairs[0, 0].T, tile_counts.reshape(-1), in_hbm)
    by_list = [lists, sizes]

    with jax.named_scope("gather_features"):
        step, swap = (lambda v, d: hop_col(v, 0, d)), (lambda v: hop_col(v, 1, 0))
        near_blocks, far_blocks = VMEM((4 * NEAR, TILE, 128), BF16), VMEM((12, TILE, 128), BF16)
        near = first_round(features, step, swap)
        near_mine, near[PAIR] = call(
            functools.partial(pack_body, NEAR),
            [near_blocks, VMEM((1024, 128), BF16)],
            near,
            after=[sizes],
        )
        far = second_round(near, step, swap)
        near_sib = hop_col(near_mine, 0, 0, 1)
    with jax.named_scope("forward_tiles"):
        total = VMEM((33, TILE, 128), F32)
        sums = call(
            forward_near_body,
            total,
            [tiles, near_mine, near_sib],
            by_list,
        )
        far_mine = call(functools.partial(pack_body, 3), far_blocks, far, after=[sums])
        far_sib = hop_col(far_mine, 0, 0, 1)
        sums = call(
            forward_far_body,
            total,
            [tiles, far_mine, sums],
            by_list,
            alias={4: 0},
            flops=share,
            nbytes=tile_bytes // 4,
        )
        f32, bf16 = VMEM((1024, 128), F32), VMEM((1024, 128), BF16)
        _, *partial = call(
            forward_last_body,
            [total, f32, bf16, bf16, f32, f32, bf16, bf16, bf16],
            [tiles, far_sib, sums],
            by_list,
            alias={4: 0},
            flops=share,
            nbytes=tile_bytes // 4,
        )
    with jax.named_scope("sum_aggregates"):
        step, swap = (lambda v, d: hop_row(v, 0, d)), (lambda v: hop_row(v, 1, 0))
        own, left, right, pair, opposite, *far = partial
        pair, opposite = call(
            add_round_body,
            [bf16, bf16],
            [pair, opposite, *first_sums(far, step, swap)],
            nbytes=4 << 20,
        )
        sums = second_sums(own, left, right, pair, opposite, step, swap)
    with jax.named_scope("dense"):
        longer = VMEM((144, 1024), BF16)
        block = VMEM((64, 256), F32)
        hidden, dpre, dz, *dz_to, quarter = call(
            dense_body,
            [
                jax.ShapeDtypeStruct((1024, 256), BF16),
                VMEM((1024, 256), BF16),
                VMEM((128, 1024), BF16),
                longer,
                longer,
                longer,
                block,
            ],
            [bias_term.reshape(1, 256), features, upstream, weight_self, weight_neigh, *sums],
            scratch=[VMEM((1024, 128), BF16), VMEM((256, 256), F32)],
            flops=5 * 2 * 1024 * 128 * 256,
            nbytes=6 << 20,
        )
    with jax.named_scope("gather_dz"):
        near = first_round(dz, step, swap, dz_to)
        quarter = call(
            ring_sum_body,
            VMEM((32, 1024), BF16),
            [quarter, near[OPPOSITE], near[LEFT], near[RIGHT]],
        )
        quarter_pair = swap(quarter)
        far = second_round(near, step, swap)
    with jax.named_scope("own_grad"):
        own_grad = call(
            own_grad_body,
            VMEM((128, 1024), F32),
            [dpre, weight_self],
            flops=2 * 1024 * 128 * 256,
            nbytes=2 << 20,
        )
    with jax.named_scope("backward_tiles"):
        total = VMEM((33, 128, TILE), F32)
        held = [VMEM((4 * NEAR, 128, TILE), BF16)]
        mine, sib = call(
            backward_near_body,
            [total, total],
            [tiles, *near],
            by_list,
            after=[own_grad],
            scratch=held,
            flops=2 * share,
            nbytes=tile_bytes // 2,
        )
        sib, sib_far, quarter = call(
            backward_sib_body,
            [total, VMEM((416, 1024), BF16), block],
            [tiles, *far, quarter, quarter_pair, sib],
            by_list,
            alias={8: 0},
            scratch=held,
            flops=share,
            nbytes=tile_bytes // 4,
        )
        mine = call(
            backward_mine_body,
            total,
            [tiles, *far, mine],
            by_list,
            scratch=held,
            alias={6: 0},
            flops=share,
            nbytes=tile_bytes // 4,
        )
    with jax.named_scope("sum_grads"):
        step, swap = (lambda v, d: hop_col(v, 0, d)), (lambda v: hop_col(v, 1, 0))
        f32, bf16 = VMEM((128, 1024), F32), VMEM((128, 1024), BF16)
        *far, quarter, sib_near, extra = call(
            add_sib_far_body,
            [longer, longer, bf16, block, VMEM((5, 128, 1024), BF16), VMEM((16, 1024), BF16)],
            [mine, sib, hop_col(sib_far, 0, 0, 1), quarter],
            nbytes=3 << 20,
        )
        from_right, from_left, from_pair = first_sums(far, step, swap)
        sib_near = hop_col(sib_near, 0, 0, 1)
        left, right = call(add_sides_body, [bf16, bf16], [mine, sib_near], nbytes=2 << 20)
        left, right = step(left, -1), step(right, 1)
        ring = call(
            ring_x_body,
            VMEM((32, 1024), BF16),
            [quarter, from_right, from_left, step(extra, 2)],
            scratch=[VMEM((4, 64, 256), F32)],
        )
        pair_ring = swap(ring)
        own, pair, opposite = call(
            add_near_body,
            [f32, bf16, bf16],
            [mine, sib_near, from_right, from_left, from_pair],
            after=[pair_ring],
            nbytes=5 << 20,
        )
        sums = [own, left, right, step(opposite, 2), swap(pair)]
    with jax.named_scope("sum_weights"):
        quarter = call(weight_sum_body, block, [ring, pair_ring], after=[left, right])
        shape = jax.ShapeDtypeStruct((128, 256), F32)
        grad_self, grad_neigh = call(
            functools.partial(weight_join_body, float(nodes) ** -0.5),
            [shape, shape],
            [quarter, *[hop_row(quarter, 0, -k) for k in (1, 2, 3)]],
            scratch=[VMEM((256, 256), F32)],
            nbytes=1 << 20,
        )
    with jax.named_scope("finish"):
        grad_features = call(
            finish_body,
            jax.ShapeDtypeStruct((1024, 128), BF16),
            [own_grad, *sums],
            nbytes=4 << 20,
        )
    return hidden, grad_features, grad_self, grad_neigh


def solution(mesh):
    placed = (
        P(("row", "col"), None),
        P(),
        P(),
        P(),
        P(("row", "col"), None),
        P("row", "col", None, None, None),
        P("row", "col", None, None),
        P("row", "col"),
    )
    return jax.shard_map(
        shards,
        mesh=mesh,
        in_specs=placed,
        out_specs=(P(("row", "col"), None), P(("row", "col"), None), P(), P()),
        check_vma=False,
    )
```

```python
import functools

import jax
import jax.numpy as jnp
from jax import lax
from jax.experimental import pallas as pl
from jax.experimental.pallas import tpu as pltpu
from jax.sharding import PartitionSpec as P

TILE = 256
VMEM = pltpu.VMEM
BF16 = jnp.bfloat16
F32 = jnp.float32
LIMIT = 12 * 1024 * 1024
GROUP = 16
ROOM = 144

NEAR = 5
ORDER = [(0, 0), (0, 3), (0, 1), (1, 0), (0, 2), (1, 3), (1, 1), (1, 2)]
OWN, LEFT, RIGHT, PAIR, OPPOSITE, PAIR_LEFT, PAIR_RIGHT, PAIR_OPPOSITE = range(8)
PLACE = sum(ORDER.index((k // 4, k % 4)) << (4 * k) for k in range(8))


def hop_col(value, dy, dx, dc=0):
    pairs = []
    for y in range(2):
        for x in range(4):
            for c in range(2):
                to = (((y + dy) % 2) * 4 + (x + dx) % 4) * 2 + (c + dc) % 2
                pairs.append(((y * 4 + x) * 2 + c, to))
    return lax.ppermute(value, "col", pairs)


def hop_row(value, dy, dz):
    pairs = []
    for z in range(4):
        for y in range(2):
            pairs.append((z * 2 + y, ((z + dz) % 4) * 2 + (y + dy) % 2))
    return lax.ppermute(value, "row", pairs)


def in_vmem(*values):
    return [pltpu.with_memory_space_constraint(v, VMEM) for v in values]


def vmem_specs(n):
    return [pl.BlockSpec(memory_space=VMEM)] * n


def call(
    body,
    outs,
    vmem_args,
    smem_args=(),
    after=(),
    scratch=(),
    alias=None,
    flops=0,
    nbytes=0,
):
    single = not isinstance(outs, (list, tuple))
    skip = len(smem_args) + len(vmem_args)

    def run(*refs):
        body(*refs[:skip], *refs[skip + len(after) :])

    return pl.pallas_call(
        run,
        out_shape=outs,
        in_specs=[pl.BlockSpec(memory_space=pltpu.SMEM)] * len(smem_args)
        + vmem_specs(len(vmem_args))
        + [pl.BlockSpec(memory_space=pl.ANY)] * len(after),
        out_specs=pl.BlockSpec(memory_space=VMEM) if single else vmem_specs(len(outs)),
        scratch_shapes=list(scratch),
        input_output_aliases=alias or {},
        compiler_params=pltpu.CompilerParams(vmem_limit_bytes=LIMIT),
        cost_estimate=pl.CostEstimate(flops=flops, bytes_accessed=nbytes, transcendentals=0),
    )(*smem_args, *in_vmem(*vmem_args), *after)


def write_extra(ref, row, value):
    for j in range(4):
        ref[row : row + 16, j * 256 : (j + 1) * 256] = value[16 * j : 16 * j + 16].astype(BF16)


def read_extra(ref, row):
    return jnp.concatenate(
        [ref[row : row + 16, j * 256 : (j + 1) * 256].astype(F32) for j in range(4)], axis=0
    )


def rounded(value):
    return value.astype(BF16).astype(F32)


def write_fine(ref, row, value):
    write_extra(ref, row, value)
    write_extra(ref, row + 16, value - rounded(value))


def read_fine(ref, row):
    return read_extra(ref, row) + read_extra(ref, row + 16)


def fine(value):
    high = rounded(value)
    return high + rounded(value - high)


def places():
    return lax.axis_index("col"), lax.axis_index("row")


def first_round(value, step, swap, to=None):
    to = to or [value] * 3
    return [value, step(to[0], 1), step(to[1], -1), swap(value), step(to[2], 2)]


def second_round(near, step, swap):
    return [step(near[PAIR], 1), step(near[PAIR], -1), swap(near[OPPOSITE])]


def place_of(index, me, other_bit, ring_shift):
    other = ((index ^ me) >> other_bit) & 1
    offset = ((index >> ring_shift) - (me >> ring_shift)) & 3
    return (PLACE >> ((other * 4 + offset) * 4)) & 15


def bring(first, last, stored, tiles, sems):
    copies = []
    for k, at in enumerate(range(first, last, 8)):
        part = pl.ds(at, 8)
        copies.append(pltpu.make_async_copy(stored.at[part], tiles.at[part], sems.at[k]))
        copies[-1].start()
    return copies


def plan_body(pairs, count, stored, tiles, lists, sizes, sems):
    copies = bring(0, 128, stored, tiles, sems)
    col, row = places()

    def put(base, which, entry, counts):
        at = (counts >> (which * 8)) & 255
        lists[(base + which) * ROOM + at] = entry
        return counts + (jnp.int32(1) << (which * 8))

    def sort(i, carry):
        d = pairs[0, i]
        s = pairs[1, i]
        c = s >> 2
        q = d >> 2
        sib = (c ^ col) & 1
        source = place_of(c, col, 3, 1) * 4 + (s & 3)
        target = place_of(q, row, 0, 1) * 4 + (d & 3)
        far = (source >= 4 * NEAR).astype(jnp.int32)
        entry = i | (target << 8) | ((source - far * 4 * NEAR) << 16)
        ahead = put(0, far * 2 + sib, entry, carry[0])
        far = (target >= 4 * NEAR).astype(jnp.int32)
        entry = i | ((target - far * 4 * NEAR) << 8) | (source << 16)
        back = put(4, far * 2 + sib, entry, carry[1])
        return ahead, back

    counts = lax.fori_loop(0, count[0], sort, (jnp.int32(0), jnp.int32(0)))
    for k in range(8):
        at = (counts[k // 4] >> (8 * (k % 4))) & 255
        sizes[k] = at
        for j in range(GROUP - 1):
            lists[k * ROOM + at + j] = 32 << 8 if k < 4 else 32 << 16
    for copy in copies:
        copy.wait()


def over_list(which, lists, sizes, product, total, to_target):
    def step(g, carry):
        news = []
        for j in range(GROUP):
            entry = lists[which * ROOM + g * GROUP + j]
            i = entry & 255
            d = (entry >> 8) & 255
            s = entry >> 16
            news.append((d if to_target else s, product(i, d, s)))
        for at, new in news:
            total[at] += new
        return carry

    lax.fori_loop(0, (sizes[which] + GROUP - 1) // GROUP, step, 0)


def pack_body(n, *rest):
    for k in range(n):
        rest[n][4 * k : 4 * k + 4] = rest[k][...].reshape(4, TILE, 128)
    for out in rest[n + 1 :]:
        out[...] = rest[PAIR][...]


def forward_step(lists, sizes, tiles, which, blocks, total):
    def product(i, d, s):
        return jnp.dot(tiles[i], blocks[s], preferred_element_type=F32)

    over_list(which, lists, sizes, product, total, True)


def forward_near_body(lists, sizes, tiles, mine, sib, total):
    total[...] = jnp.zeros_like(total)
    forward_step(lists, sizes, tiles, 0, mine, total)
    forward_step(lists, sizes, tiles, 1, sib, total)


def forward_far_body(lists, sizes, tiles, mine, before, total):
    forward_step(lists, sizes, tiles, 2, mine, total)


def forward_last_body(lists, sizes, tiles, sib, before, total, *outs):
    forward_step(lists, sizes, tiles, 3, sib, total)
    for k in range(8):
        outs[k][...] = total[4 * k : 4 * k + 4].reshape(1024, 128).astype(outs[k].dtype)


def hold_dz(parts, held):
    for k, ref in enumerate(parts):
        for b in range(4):
            held[4 * k + b] = ref[0:128, b * TILE : (b + 1) * TILE]


def backward_step(lists, sizes, tiles, which, held, total):
    def product(i, d, s):
        return jnp.dot(held[d], tiles[i], preferred_element_type=F32)

    over_list(which, lists, sizes, product, total, False)


def backward_near_body(lists, sizes, tiles, *rest):
    parts, (mine, sib, held) = rest[:NEAR], rest[NEAR:]
    hold_dz(parts, held)
    mine[...] = jnp.zeros_like(mine)
    sib[...] = jnp.zeros_like(sib)
    backward_step(lists, sizes, tiles, 5, held, sib)
    backward_step(lists, sizes, tiles, 4, held, mine)


def write_places(total, first, outs):
    for k, ref in enumerate(outs):
        for b in range(4):
            new = total[4 * (first + k) + b].astype(ref.dtype)
            ref[0:128, b * TILE : (b + 1) * TILE] = new


def backward_sib_body(lists, sizes, tiles, *rest):
    parts, (quarter, other, before, sib, far, quarter_out, held) = rest[:3], rest[3:]
    hold_dz(parts, held)
    backward_step(lists, sizes, tiles, 7, held, sib)
    write_places(sib, PAIR_LEFT, [far.at[pl.ds(128 * k, 128)] for k in range(3)])
    total = read_fine(quarter, 0) + read_fine(other, 0)
    quarter_out[...] = fine(total)
    write_fine(far, 384, total)


def backward_mine_body(lists, sizes, tiles, *rest):
    parts, (before, mine, held) = rest[:3], rest[3:]
    hold_dz(parts, held)
    backward_step(lists, sizes, tiles, 6, held, mine)


def add_sib_far_body(mine, sib, got, quarter, *rest):
    outs, quarter_out, near = rest[:3], rest[3], rest[4]
    total = quarter[...] + read_fine(got, 384)
    quarter_out[...] = rounded(total)
    for k, ref in enumerate(outs):
        for b in range(4):
            nodes = slice(b * TILE, (b + 1) * TILE)
            new = mine[4 * (PAIR_LEFT + k) + b] + got[128 * k : 128 * k + 128, nodes].astype(F32)
            ref[0:128, nodes] = new.astype(BF16)
        write_extra(ref, 128, total)
    write_places(sib, OWN, [near.at[k] for k in range(5)])


def add_round_body(pair, opposite, from_right, from_left, from_pair, pair_out, opposite_out):
    new = pair[...] + (from_right[...].astype(F32) + from_left[...].astype(F32))
    pair_out[...] = new.astype(BF16)
    opposite_out[...] = (opposite[...] + from_pair[...].astype(F32)).astype(BF16)


def add_sides_body(mine, got, left, right):
    for place, ref in ((LEFT, left), (RIGHT, right)):
        for b in range(4):
            nodes = slice(b * TILE, (b + 1) * TILE)
            new = mine[4 * place + b] + got[place, :, nodes].astype(F32)
            ref[:, nodes] = new.astype(BF16)


def add_near_body(mine, got, from_right, from_left, from_pair, *outs):
    more = {PAIR: [from_right, from_left], OPPOSITE: [from_pair]}
    for place, ref in zip((OWN, PAIR, OPPOSITE), outs):
        for b in range(4):
            nodes = slice(b * TILE, (b + 1) * TILE)
            new = mine[4 * place + b] + got[place, :, nodes].astype(F32)
            for came in more.get(place, []):
                new = new + came[0:128, nodes].astype(F32)
            ref[:, nodes] = new.astype(ref.dtype)


def extras_body(quarter, from_right, from_left, from_pair, pair, opposite):
    write_extra(opposite, 0, quarter[...])
    opposite[16:32] = from_pair[128:144]
    pair[0:16] = from_left[128:144]
    pair[16:32] = from_right[128:144]


def first_sums(parts, step, swap):
    return step(parts[0], -1), step(parts[1], 1), swap(parts[2])


def second_sums(own, left, right, pair, opposite, step, swap):
    return [own, step(left, -1), step(right, 1), step(opposite, 2), swap(pair)]


def dense_body(bias, feats, upstream, w_self, w_neigh, *rest):
    sums = rest[:5]
    hidden, dpre_out, dz_out, *dz_to, quarter, agg_out, grads = rest[5:]
    for b in range(4):
        rows = slice(b * TILE, (b + 1) * TILE)
        agg = sums[0][rows]
        for ref in sums[1:]:
            agg = agg + ref[rows].astype(F32)
        agg = agg.astype(BF16)
        agg_out[rows] = agg
        pre = jnp.dot(feats[rows], w_self[...], preferred_element_type=F32)
        pre = pre + jnp.dot(agg, w_neigh[...], preferred_element_type=F32) + bias[...]
        sig = jax.nn.sigmoid(pre)
        hidden[rows] = (pre * sig).astype(BF16)
        slope = sig * (1.0 + pre * (1.0 - sig))
        dpre = (upstream[rows].astype(F32) * slope).astype(BF16)
        dpre_out[rows] = dpre
        dz = lax.dot_general(
            w_neigh[...], dpre, (((1,), (1,)), ((), ())), preferred_element_type=F32
        ).astype(BF16)
        for ref in [dz_out, *dz_to]:
            ref[0:128, rows] = dz
    over_nodes = (((0,), (0,)), ((), ()))
    grads[0:128] = lax.dot_general(
        feats[...], dpre_out[...], over_nodes, preferred_element_type=F32
    )
    grads[128:256] = lax.dot_general(
        agg_out[...], dpre_out[...], over_nodes, preferred_element_type=F32
    )
    z = lax.axis_index("row") >> 1

    def piece(k):
        return grads[pl.ds(pl.multiple_of(((z + k) & 3) * 64, 64), 64), :]

    quarter[...] = piece(0)
    for ref, k in zip(dz_to, (1, 3, 2)):
        write_extra(ref, 128, piece(k))


def ring_sum_body(quarter, opposite, left, right, out):
    total = quarter[...] + read_extra(left, 128)
    write_fine(out, 0, total + (read_extra(right, 128) + read_extra(opposite, 128)))


def own_grad_body(dpre, w_self, own_grad):
    own_grad[...] = lax.dot_general(
        w_self[...], dpre[...], (((1,), (1,)), ((), ())), preferred_element_type=F32
    )


def finish_body(own_grad, *rest):
    out = rest[-1]
    for b in range(4):
        nodes = slice(b * TILE, (b + 1) * TILE)
        total = own_grad[:, nodes]
        for ref in rest[:-1]:
            total = total + ref[0:128, nodes].astype(F32)
        out[nodes] = total.T.astype(BF16)


def weight_sum_body(own, left, right, pair, from_opposite, from_pair, out, parts):
    col, _ = places()
    y, x = col >> 3, (col >> 1) & 3
    parts[y * 4 + x] = own[...]
    parts[y * 4 + ((x + 3) & 3)] = read_extra(left, 128)
    parts[y * 4 + ((x + 1) & 3)] = read_extra(right, 128)
    parts[(1 - y) * 4 + x] = read_extra(pair, 128)
    parts[y * 4 + ((x + 2) & 3)] = read_extra(from_opposite, 0)
    parts[(1 - y) * 4 + ((x + 2) & 3)] = read_extra(from_opposite, 16)
    parts[(1 - y) * 4 + ((x + 3) & 3)] = read_extra(from_pair, 0)
    parts[(1 - y) * 4 + ((x + 1) & 3)] = read_extra(from_pair, 16)
    total = parts[0]
    for k in range(1, 8):
        total = total + parts[k]
    out[...] = total


def weight_join_body(scale, own, *rest):
    others, (grad_self, grad_neigh, held) = rest[:3], rest[3:]
    z = lax.axis_index("row") >> 1
    for k, ref in enumerate([own, *others]):
        at = pl.multiple_of(((z + k) & 3) * 64, 64)
        held[pl.ds(at, 64), :] = ref[...] * scale
    grad_self[...] = held[0:128]
    grad_neigh[...] = held[128:256]


def shards(
    features, weight_self, weight_neigh, bias_term, upstream, tile_values, block_pairs, tile_counts
):
    nodes = 131072
    tile_bytes = 128 * TILE * TILE * 2
    share = 32 * 2 * TILE * TILE * 128
    in_hbm = pltpu.with_memory_space_constraint(tile_values.reshape(128, TILE, TILE), pltpu.HBM)
    with jax.named_scope("plan"):
        tiles, lists, sizes = pl.pallas_call(
            plan_body,
            out_shape=[
                VMEM((128, TILE, TILE), BF16),
                pltpu.SMEM((8 * ROOM,), jnp.int32),
                pltpu.SMEM((8,), jnp.int32),
            ],
            in_specs=[pl.BlockSpec(memory_space=pltpu.SMEM)] * 2
            + [pl.BlockSpec(memory_space=pl.ANY)],
            out_specs=[pl.BlockSpec(memory_space=VMEM)]
            + [pl.BlockSpec(memory_space=pltpu.SMEM)] * 2,
            scratch_shapes=[pltpu.SemaphoreType.DMA((16,))],
            compiler_params=pltpu.CompilerParams(vmem_limit_bytes=LIMIT),
            cost_estimate=pl.CostEstimate(flops=0, bytes_accessed=tile_bytes, transcendentals=0),
        )(block_pairs[0, 0].T, tile_counts.reshape(-1), in_hbm)
    by_list = [lists, sizes]

    with jax.named_scope("gather_features"):
        step, swap = (lambda v, d: hop_col(v, 0, d)), (lambda v: hop_col(v, 1, 0))
        near_blocks, far_blocks = VMEM((4 * NEAR, TILE, 128), BF16), VMEM((12, TILE, 128), BF16)
        near = first_round(features, step, swap)
        near_mine, near[PAIR] = call(
            functools.partial(pack_body, NEAR),
            [near_blocks, VMEM((1024, 128), BF16)],
            near,
            after=[sizes],
        )
        far = second_round(near, step, swap)
        near_sib = hop_col(near_mine, 0, 0, 1)
    with jax.named_scope("forward_tiles"):
        total = VMEM((33, TILE, 128), F32)
        sums = call(
            forward_near_body,
            total,
            [tiles, near_mine, near_sib],
            by_list,
        )
        far_mine = call(functools.partial(pack_body, 3), far_blocks, far, after=[sums])
        far_sib = hop_col(far_mine, 0, 0, 1)
        sums = call(
            forward_far_body,
            total,
            [tiles, far_mine, sums],
            by_list,
            alias={4: 0},
            flops=share,
            nbytes=tile_bytes // 4,
        )
        f32, bf16 = VMEM((1024, 128), F32), VMEM((1024, 128), BF16)
        _, *partial = call(
            forward_last_body,
            [total, f32, bf16, bf16, f32, f32, bf16, bf16, bf16],
            [tiles, far_sib, sums],
            by_list,
            alias={4: 0},
            flops=share,
            nbytes=tile_bytes // 4,
        )
    with jax.named_scope("sum_aggregates"):
        step, swap = (lambda v, d: hop_row(v, 0, d)), (lambda v: hop_row(v, 1, 0))
        own, left, right, pair, opposite, *far = partial
        pair, opposite = call(
            add_round_body,
            [bf16, bf16],
            [pair, opposite, *first_sums(far, step, swap)],
            nbytes=4 << 20,
        )
        sums = second_sums(own, left, right, pair, opposite, step, swap)
    with jax.named_scope("dense"):
        longer = VMEM((144, 1024), BF16)
        block = VMEM((64, 256), F32)
        hidden, dpre, dz, *dz_to, quarter = call(
            dense_body,
            [
                jax.ShapeDtypeStruct((1024, 256), BF16),
                VMEM((1024, 256), BF16),
                VMEM((128, 1024), BF16),
                longer,
                longer,
                longer,
                block,
            ],
            [bias_term.reshape(1, 256), features, upstream, weight_self, weight_neigh, *sums],
            scratch=[VMEM((1024, 128), BF16), VMEM((256, 256), F32)],
            flops=5 * 2 * 1024 * 128 * 256,
            nbytes=6 << 20,
        )
    with jax.named_scope("gather_dz"):
        near = first_round(dz, step, swap, dz_to)
        quarter = call(
            ring_sum_body,
            VMEM((32, 1024), BF16),
            [quarter, near[OPPOSITE], near[LEFT], near[RIGHT]],
        )
        quarter_pair = swap(quarter)
        far = second_round(near, step, swap)
    with jax.named_scope("own_grad"):
        own_grad = call(
            own_grad_body,
            VMEM((128, 1024), F32),
            [dpre, weight_self],
            flops=2 * 1024 * 128 * 256,
            nbytes=2 << 20,
        )
    with jax.named_scope("backward_tiles"):
        total = VMEM((33, 128, TILE), F32)
        held = [VMEM((4 * NEAR, 128, TILE), BF16)]
        mine, sib = call(
            backward_near_body,
            [total, total],
            [tiles, *near],
            by_list,
            after=[own_grad],
            scratch=held,
            flops=2 * share,
            nbytes=tile_bytes // 2,
        )
        sib, sib_far, quarter = call(
            backward_sib_body,
            [total, VMEM((416, 1024), BF16), block],
            [tiles, *far, quarter, quarter_pair, sib],
            by_list,
            alias={8: 0},
            scratch=held,
            flops=share,
            nbytes=tile_bytes // 4,
        )
        mine = call(
            backward_mine_body,
            total,
            [tiles, *far, mine],
            by_list,
            scratch=held,
            alias={6: 0},
            flops=share,
            nbytes=tile_bytes // 4,
        )
    with jax.named_scope("sum_grads"):
        step, swap = (lambda v, d: hop_col(v, 0, d)), (lambda v: hop_col(v, 1, 0))
        f32, bf16 = VMEM((128, 1024), F32), VMEM((128, 1024), BF16)
        *far, quarter, sib_near = call(
            add_sib_far_body,
            [longer, longer, longer, block, VMEM((5, 128, 1024), BF16)],
            [mine, sib, hop_col(sib_far, 0, 0, 1), quarter],
            nbytes=3 << 20,
        )
        from_right, from_left, from_pair = first_sums(far, step, swap)
        sib_near = hop_col(sib_near, 0, 0, 1)
        left, right = call(add_sides_body, [bf16, bf16], [mine, sib_near], nbytes=2 << 20)
        left, right = step(left, -1), step(right, 1)
        extra = VMEM((32, 1024), BF16)
        pair_extra, opposite_extra = call(
            extras_body, [extra, extra], [quarter, from_right, from_left, from_pair]
        )
        came = [from_left, from_right, from_pair, step(opposite_extra, 2), swap(pair_extra)]
        own, pair, opposite = call(
            add_near_body,
            [f32, bf16, bf16],
            [mine, sib_near, from_right, from_left, from_pair],
            after=[*came[3:], left, right],
            nbytes=5 << 20,
        )
        sums = [own, left, right, step(opposite, 2), swap(pair)]
    with jax.named_scope("sum_weights"):
        quarter = call(
            weight_sum_body,
            block,
            [quarter, *came],
            scratch=[VMEM((8, 64, 256), F32)],
            nbytes=1 << 20,
        )
        shape = jax.ShapeDtypeStruct((128, 256), F32)
        grad_self, grad_neigh = call(
            functools.partial(weight_join_body, float(nodes) ** -0.5),
            [shape, shape],
            [quarter, *[hop_row(quarter, 0, -k) for k in (1, 2, 3)]],
            scratch=[VMEM((256, 256), F32)],
            nbytes=1 << 20,
        )
    with jax.named_scope("finish"):
        grad_features = call(
            finish_body,
            jax.ShapeDtypeStruct((1024, 128), BF16),
            [own_grad, *sums],
            nbytes=4 << 20,
        )
    return hidden, grad_features, grad_self, grad_neigh


def solution(mesh):
    placed = (
        P(("row", "col"), None),
        P(),
        P(),
        P(),
        P(("row", "col"), None),
        P("row", "col", None, None, None),
        P("row", "col", None, None),
        P("row", "col"),
    )
    return jax.shard_map(
        shards,
        mesh=mesh,
        in_specs=placed,
        out_specs=(P(("row", "col"), None), P(("row", "col"), None), P(), P()),
        check_vma=False,
    )
```

```python
import functools

import jax
import jax.numpy as jnp
from jax import lax
from jax.experimental import pallas as pl
from jax.experimental.pallas import tpu as pltpu
from jax.sharding import PartitionSpec as P

TILE = 256
VMEM = pltpu.VMEM
BF16 = jnp.bfloat16
F32 = jnp.float32
LIMIT = 12 * 1024 * 1024
GROUP = 16
ROOM = 144

NEAR = 5
ORDER = [(0, 0), (0, 3), (0, 1), (1, 0), (0, 2), (1, 3), (1, 1), (1, 2)]
OWN, LEFT, RIGHT, PAIR, OPPOSITE, PAIR_LEFT, PAIR_RIGHT, PAIR_OPPOSITE = range(8)
PLACE = sum(ORDER.index((k // 4, k % 4)) << (4 * k) for k in range(8))


def hop_col(value, dy, dx, dc=0):
    pairs = []
    for y in range(2):
        for x in range(4):
            for c in range(2):
                to = (((y + dy) % 2) * 4 + (x + dx) % 4) * 2 + (c + dc) % 2
                pairs.append(((y * 4 + x) * 2 + c, to))
    return lax.ppermute(value, "col", pairs)


def hop_row(value, dy, dz):
    pairs = []
    for z in range(4):
        for y in range(2):
            pairs.append((z * 2 + y, ((z + dz) % 4) * 2 + (y + dy) % 2))
    return lax.ppermute(value, "row", pairs)


def in_vmem(*values):
    return [pltpu.with_memory_space_constraint(v, VMEM) for v in values]


def vmem_specs(n):
    return [pl.BlockSpec(memory_space=VMEM)] * n


def call(
    body,
    outs,
    vmem_args,
    smem_args=(),
    after=(),
    scratch=(),
    alias=None,
    flops=0,
    nbytes=0,
):
    single = not isinstance(outs, (list, tuple))
    skip = len(smem_args) + len(vmem_args)

    def run(*refs):
        body(*refs[:skip], *refs[skip + len(after) :])

    return pl.pallas_call(
        run,
        out_shape=outs,
        in_specs=[pl.BlockSpec(memory_space=pltpu.SMEM)] * len(smem_args)
        + vmem_specs(len(vmem_args))
        + [pl.BlockSpec(memory_space=pl.ANY)] * len(after),
        out_specs=pl.BlockSpec(memory_space=VMEM) if single else vmem_specs(len(outs)),
        scratch_shapes=list(scratch),
        input_output_aliases=alias or {},
        compiler_params=pltpu.CompilerParams(vmem_limit_bytes=LIMIT),
        cost_estimate=pl.CostEstimate(flops=flops, bytes_accessed=nbytes, transcendentals=0),
    )(*smem_args, *in_vmem(*vmem_args), *after)


def write_extra(ref, row, value):
    for j in range(4):
        ref[row : row + 16, j * 256 : (j + 1) * 256] = value[16 * j : 16 * j + 16].astype(BF16)


def read_extra(ref, row):
    return jnp.concatenate(
        [ref[row : row + 16, j * 256 : (j + 1) * 256].astype(F32) for j in range(4)], axis=0
    )


def rounded(value):
    return value.astype(BF16).astype(F32)


def write_fine(ref, row, value):
    write_extra(ref, row, value)
    write_extra(ref, row + 16, value - rounded(value))


def read_fine(ref, row):
    return read_extra(ref, row) + read_extra(ref, row + 16)


def fine(value):
    high = rounded(value)
    return high + rounded(value - high)


def places():
    return lax.axis_index("col"), lax.axis_index("row")


def first_round(value, step, swap, to=None):
    to = to or [value] * 3
    return [value, step(to[0], 1), step(to[1], -1), swap(value), step(to[2], 2)]


def second_round(near, step, swap):
    return [step(near[PAIR], 1), step(near[PAIR], -1), swap(near[OPPOSITE])]


def place_of(index, me, other_bit, ring_shift):
    other = ((index ^ me) >> other_bit) & 1
    offset = ((index >> ring_shift) - (me >> ring_shift)) & 3
    return (PLACE >> ((other * 4 + offset) * 4)) & 15


def bring(first, last, stored, tiles, sems):
    copies = []
    for k, at in enumerate(range(first, last, 8)):
        part = pl.ds(at, 8)
        copies.append(pltpu.make_async_copy(stored.at[part], tiles.at[part], sems.at[k]))
        copies[-1].start()
    return copies


def plan_body(pairs, count, stored, tiles, lists, sizes, sems):
    copies = bring(0, 128, stored, tiles, sems)
    col, row = places()

    def put(base, which, entry, counts):
        at = (counts >> (which * 8)) & 255
        lists[(base + which) * ROOM + at] = entry
        return counts + (jnp.int32(1) << (which * 8))

    def sort(i, carry):
        d = pairs[0, i]
        s = pairs[1, i]
        c = s >> 2
        q = d >> 2
        sib = (c ^ col) & 1
        source = place_of(c, col, 3, 1) * 4 + (s & 3)
        target = place_of(q, row, 0, 1) * 4 + (d & 3)
        far = (source >= 4 * NEAR).astype(jnp.int32)
        entry = i | (target << 8) | ((source - far * 4 * NEAR) << 16)
        ahead = put(0, far * 2 + sib, entry, carry[0])
        far = (target >= 4 * NEAR).astype(jnp.int32)
        entry = i | ((target - far * 4 * NEAR) << 8) | (source << 16)
        back = put(4, far * 2 + sib, entry, carry[1])
        return ahead, back

    counts = lax.fori_loop(0, count[0], sort, (jnp.int32(0), jnp.int32(0)))
    for k in range(8):
        at = (counts[k // 4] >> (8 * (k % 4))) & 255
        sizes[k] = at
        for j in range(GROUP - 1):
            lists[k * ROOM + at + j] = 32 << 8 if k < 4 else 32 << 16
    for copy in copies:
        copy.wait()


def over_list(which, lists, sizes, product, total, to_target):
    def step(g, carry):
        news = []
        for j in range(GROUP):
            entry = lists[which * ROOM + g * GROUP + j]
            i = entry & 255
            d = (entry >> 8) & 255
            s = entry >> 16
            news.append((d if to_target else s, product(i, d, s)))
        for at, new in news:
            total[at] += new
        return carry

    lax.fori_loop(0, (sizes[which] + GROUP - 1) // GROUP, step, 0)


def pack_body(n, *rest):
    for k in range(n):
        rest[n][4 * k : 4 * k + 4] = rest[k][...].reshape(4, TILE, 128)
    for out in rest[n + 1 :]:
        out[...] = rest[PAIR][...]


def forward_step(lists, sizes, tiles, which, blocks, total):
    def product(i, d, s):
        return jnp.dot(tiles[i], blocks[s], preferred_element_type=F32)

    over_list(which, lists, sizes, product, total, True)


def forward_near_body(lists, sizes, tiles, mine, sib, total):
    total[...] = jnp.zeros_like(total)
    forward_step(lists, sizes, tiles, 0, mine, total)
    forward_step(lists, sizes, tiles, 1, sib, total)


def forward_far_body(lists, sizes, tiles, mine, before, total):
    forward_step(lists, sizes, tiles, 2, mine, total)


def forward_last_body(lists, sizes, tiles, sib, before, total, *outs):
    forward_step(lists, sizes, tiles, 3, sib, total)
    for k in range(8):
        outs[k][...] = total[4 * k : 4 * k + 4].reshape(1024, 128).astype(outs[k].dtype)


def hold_dz(parts, held):
    for k, ref in enumerate(parts):
        for b in range(4):
            held[4 * k + b] = ref[0:128, b * TILE : (b + 1) * TILE]


def backward_step(lists, sizes, tiles, which, held, total):
    def product(i, d, s):
        return jnp.dot(held[d], tiles[i], preferred_element_type=F32)

    over_list(which, lists, sizes, product, total, False)


def backward_near_body(lists, sizes, tiles, *rest):
    parts, (mine, sib, held) = rest[:NEAR], rest[NEAR:]
    hold_dz(parts, held)
    mine[...] = jnp.zeros_like(mine)
    sib[...] = jnp.zeros_like(sib)
    backward_step(lists, sizes, tiles, 5, held, sib)
    backward_step(lists, sizes, tiles, 4, held, mine)


def write_places(total, first, outs):
    for k, ref in enumerate(outs):
        for b in range(4):
            new = total[4 * (first + k) + b].astype(ref.dtype)
            ref[0:128, b * TILE : (b + 1) * TILE] = new


def backward_sib_body(lists, sizes, tiles, *rest):
    parts, (quarter, other, before, sib, far, quarter_out, held) = rest[:3], rest[3:]
    hold_dz(parts, held)
    backward_step(lists, sizes, tiles, 7, held, sib)
    write_places(sib, PAIR_LEFT, [far.at[pl.ds(128 * k, 128)] for k in range(3)])
    total = read_fine(quarter, 0) + read_fine(other, 0)
    quarter_out[...] = fine(total)
    write_fine(far, 384, total)


def backward_mine_body(lists, sizes, tiles, *rest):
    parts, (before, mine, held) = rest[:3], rest[3:]
    hold_dz(parts, held)
    backward_step(lists, sizes, tiles, 6, held, mine)


def add_sib_far_body(mine, sib, got, quarter, *rest):
    outs, (quarter_out, near, extra) = rest[:3], rest[3:]
    total = quarter[...] + read_fine(got, 384)
    quarter_out[...] = rounded(total)
    for k, ref in enumerate(outs):
        for b in range(4):
            nodes = slice(b * TILE, (b + 1) * TILE)
            new = mine[4 * (PAIR_LEFT + k) + b] + got[128 * k : 128 * k + 128, nodes].astype(F32)
            ref[0:128, nodes] = new.astype(BF16)
    for ref, row in ((outs[0], 128), (outs[1], 128), (extra, 0)):
        write_extra(ref, row, total)
    write_places(sib, OWN, [near.at[k] for k in range(5)])


def add_round_body(pair, opposite, from_right, from_left, from_pair, pair_out, opposite_out):
    new = pair[...] + (from_right[...].astype(F32) + from_left[...].astype(F32))
    pair_out[...] = new.astype(BF16)
    opposite_out[...] = (opposite[...] + from_pair[...].astype(F32)).astype(BF16)


def add_sides_body(mine, got, left, right):
    for place, ref in ((LEFT, left), (RIGHT, right)):
        for b in range(4):
            nodes = slice(b * TILE, (b + 1) * TILE)
            new = mine[4 * place + b] + got[place, :, nodes].astype(F32)
            ref[:, nodes] = new.astype(BF16)


def add_near_body(mine, got, from_right, from_left, from_pair, *outs):
    more = {PAIR: [from_right, from_left], OPPOSITE: [from_pair]}
    for place, ref in zip((OWN, PAIR, OPPOSITE), outs):
        for b in range(4):
            nodes = slice(b * TILE, (b + 1) * TILE)
            new = mine[4 * place + b] + got[place, :, nodes].astype(F32)
            for came in more.get(place, []):
                new = new + came[0:128, nodes].astype(F32)
            ref[:, nodes] = new.astype(ref.dtype)


def ring_x_body(quarter, from_right, from_left, from_opposite, out, parts):
    x = (lax.axis_index("col") >> 1) & 3
    parts[x] = quarter[...]
    parts[(x + 3) & 3] = read_extra(from_left, 128)
    parts[(x + 1) & 3] = read_extra(from_right, 128)
    parts[(x + 2) & 3] = read_extra(from_opposite, 0)
    write_fine(out, 0, ((parts[0] + parts[1]) + parts[2]) + parts[3])


def first_sums(parts, step, swap):
    return step(parts[0], -1), step(parts[1], 1), swap(parts[2])


def second_sums(own, left, right, pair, opposite, step, swap):
    return [own, step(left, -1), step(right, 1), step(opposite, 2), swap(pair)]


def dense_body(bias, feats, upstream, w_self, w_neigh, *rest):
    sums = rest[:5]
    hidden, dpre_out, dz_out, *dz_to, quarter, agg_out, grads = rest[5:]
    for b in range(4):
        rows = slice(b * TILE, (b + 1) * TILE)
        agg = sums[0][rows]
        for ref in sums[1:]:
            agg = agg + ref[rows].astype(F32)
        agg = agg.astype(BF16)
        agg_out[rows] = agg
        pre = jnp.dot(feats[rows], w_self[...], preferred_element_type=F32)
        pre = pre + jnp.dot(agg, w_neigh[...], preferred_element_type=F32) + bias[...]
        sig = jax.nn.sigmoid(pre)
        hidden[rows] = (pre * sig).astype(BF16)
        slope = sig * (1.0 + pre * (1.0 - sig))
        dpre = (upstream[rows].astype(F32) * slope).astype(BF16)
        dpre_out[rows] = dpre
        dz = lax.dot_general(
            w_neigh[...], dpre, (((1,), (1,)), ((), ())), preferred_element_type=F32
        ).astype(BF16)
        for ref in [dz_out, *dz_to]:
            ref[0:128, rows] = dz
    over_nodes = (((0,), (0,)), ((), ()))
    grads[0:128] = lax.dot_general(
        feats[...], dpre_out[...], over_nodes, preferred_element_type=F32
    )
    grads[128:256] = lax.dot_general(
        agg_out[...], dpre_out[...], over_nodes, preferred_element_type=F32
    )
    z = lax.axis_index("row") >> 1

    def piece(k):
        return grads[pl.ds(pl.multiple_of(((z + k) & 3) * 64, 64), 64), :]

    quarter[...] = piece(0)
    for ref, k in zip(dz_to, (1, 3, 2)):
        write_extra(ref, 128, piece(k))


def ring_sum_body(quarter, opposite, left, right, out):
    total = quarter[...] + read_extra(left, 128)
    write_fine(out, 0, total + (read_extra(right, 128) + read_extra(opposite, 128)))


def own_grad_body(dpre, w_self, own_grad):
    own_grad[...] = lax.dot_general(
        w_self[...], dpre[...], (((1,), (1,)), ((), ())), preferred_element_type=F32
    )


def finish_body(own_grad, *rest):
    out = rest[-1]
    for b in range(4):
        nodes = slice(b * TILE, (b + 1) * TILE)
        total = own_grad[:, nodes]
        for ref in rest[:-1]:
            total = total + ref[0:128, nodes].astype(F32)
        out[nodes] = total.T.astype(BF16)


def weight_sum_body(ring, pair, out):
    out[...] = read_fine(ring, 0) + read_fine(pair, 0)


def weight_join_body(scale, own, *rest):
    others, (grad_self, grad_neigh, held) = rest[:3], rest[3:]
    z = lax.axis_index("row") >> 1
    for k, ref in enumerate([own, *others]):
        at = pl.multiple_of(((z + k) & 3) * 64, 64)
        held[pl.ds(at, 64), :] = ref[...] * scale
    grad_self[...] = held[0:128]
    grad_neigh[...] = held[128:256]


def shards(
    features, weight_self, weight_neigh, bias_term, upstream, tile_values, block_pairs, tile_counts
):
    nodes = 131072
    tile_bytes = 128 * TILE * TILE * 2
    share = 32 * 2 * TILE * TILE * 128
    in_hbm = pltpu.with_memory_space_constraint(tile_values.reshape(128, TILE, TILE), pltpu.HBM)
    with jax.named_scope("plan"):
        tiles, lists, sizes = pl.pallas_call(
            plan_body,
            out_shape=[
                VMEM((128, TILE, TILE), BF16),
                pltpu.SMEM((8 * ROOM,), jnp.int32),
                pltpu.SMEM((8,), jnp.int32),
            ],
            in_specs=[pl.BlockSpec(memory_space=pltpu.SMEM)] * 2
            + [pl.BlockSpec(memory_space=pl.ANY)],
            out_specs=[pl.BlockSpec(memory_space=VMEM)]
            + [pl.BlockSpec(memory_space=pltpu.SMEM)] * 2,
            scratch_shapes=[pltpu.SemaphoreType.DMA((16,))],
            compiler_params=pltpu.CompilerParams(vmem_limit_bytes=LIMIT),
            cost_estimate=pl.CostEstimate(flops=0, bytes_accessed=tile_bytes, transcendentals=0),
        )(block_pairs[0, 0].T, tile_counts.reshape(-1), in_hbm)
    by_list = [lists, sizes]

    with jax.named_scope("gather_features"):
        step, swap = (lambda v, d: hop_col(v, 0, d)), (lambda v: hop_col(v, 1, 0))
        near_blocks, far_blocks = VMEM((4 * NEAR, TILE, 128), BF16), VMEM((12, TILE, 128), BF16)
        near = first_round(features, step, swap)
        near_mine, near[PAIR] = call(
            functools.partial(pack_body, NEAR),
            [near_blocks, VMEM((1024, 128), BF16)],
            near,
            after=[sizes],
        )
        far = second_round(near, step, swap)
        near_sib = hop_col(near_mine, 0, 0, 1)
    with jax.named_scope("forward_tiles"):
        total = VMEM((33, TILE, 128), F32)
        sums = call(
            forward_near_body,
            total,
            [tiles, near_mine, near_sib],
            by_list,
        )
        far_mine = call(functools.partial(pack_body, 3), far_blocks, far, after=[sums])
        far_sib = hop_col(far_mine, 0, 0, 1)
        sums = call(
            forward_far_body,
            total,
            [tiles, far_mine, sums],
            by_list,
            alias={4: 0},
            flops=share,
            nbytes=tile_bytes // 4,
        )
        f32, bf16 = VMEM((1024, 128), F32), VMEM((1024, 128), BF16)
        _, *partial = call(
            forward_last_body,
            [total, f32, bf16, bf16, f32, f32, bf16, bf16, bf16],
            [tiles, far_sib, sums],
            by_list,
            alias={4: 0},
            flops=share,
            nbytes=tile_bytes // 4,
        )
    with jax.named_scope("sum_aggregates"):
        step, swap = (lambda v, d: hop_row(v, 0, d)), (lambda v: hop_row(v, 1, 0))
        own, left, right, pair, opposite, *far = partial
        pair, opposite = call(
            add_round_body,
            [bf16, bf16],
            [pair, opposite, *first_sums(far, step, swap)],
            nbytes=4 << 20,
        )
        sums = second_sums(own, left, right, pair, opposite, step, swap)
    with jax.named_scope("dense"):
        longer = VMEM((144, 1024), BF16)
        block = VMEM((64, 256), F32)
        hidden, dpre, dz, *dz_to, quarter = call(
            dense_body,
            [
                jax.ShapeDtypeStruct((1024, 256), BF16),
                VMEM((1024, 256), BF16),
                VMEM((128, 1024), BF16),
                longer,
                longer,
                longer,
                block,
            ],
            [bias_term.reshape(1, 256), features, upstream, weight_self, weight_neigh, *sums],
            scratch=[VMEM((1024, 128), BF16), VMEM((256, 256), F32)],
            flops=5 * 2 * 1024 * 128 * 256,
            nbytes=6 << 20,
        )
    with jax.named_scope("gather_dz"):
        near = first_round(dz, step, swap, dz_to)
        quarter = call(
            ring_sum_body,
            VMEM((32, 1024), BF16),
            [quarter, near[OPPOSITE], near[LEFT], near[RIGHT]],
        )
        quarter_pair = swap(quarter)
        far = second_round(near, step, swap)
    with jax.named_scope("own_grad"):
        own_grad = call(
            own_grad_body,
            VMEM((128, 1024), F32),
            [dpre, weight_self],
            flops=2 * 1024 * 128 * 256,
            nbytes=2 << 20,
        )
    with jax.named_scope("backward_tiles"):
        total = VMEM((33, 128, TILE), F32)
        held = [VMEM((4 * NEAR, 128, TILE), BF16)]
        mine, sib = call(
            backward_near_body,
            [total, total],
            [tiles, *near],
            by_list,
            after=[own_grad],
            scratch=held,
            flops=2 * share,
            nbytes=tile_bytes // 2,
        )
        sib, sib_far, quarter = call(
            backward_sib_body,
            [total, VMEM((416, 1024), BF16), block],
            [tiles, *far, quarter, quarter_pair, sib],
            by_list,
            alias={8: 0},
            scratch=held,
            flops=share,
            nbytes=tile_bytes // 4,
        )
        mine = call(
            backward_mine_body,
            total,
            [tiles, *far, mine],
            by_list,
            scratch=held,
            alias={6: 0},
            flops=share,
            nbytes=tile_bytes // 4,
        )
    with jax.named_scope("sum_grads"):
        step, swap = (lambda v, d: hop_col(v, 0, d)), (lambda v: hop_col(v, 1, 0))
        f32, bf16 = VMEM((128, 1024), F32), VMEM((128, 1024), BF16)
        *far, quarter, sib_near, extra = call(
            add_sib_far_body,
            [longer, longer, bf16, block, VMEM((5, 128, 1024), BF16), VMEM((16, 1024), BF16)],
            [mine, sib, hop_col(sib_far, 0, 0, 1), quarter],
            nbytes=3 << 20,
        )
        from_right, from_left, from_pair = first_sums(far, step, swap)
        sib_near = hop_col(sib_near, 0, 0, 1)
        left, right = call(add_sides_body, [bf16, bf16], [mine, sib_near], nbytes=2 << 20)
        left, right = step(left, -1), step(right, 1)
        ring = call(
            ring_x_body,
            VMEM((32, 1024), BF16),
            [quarter, from_right, from_left, step(extra, 2)],
            scratch=[VMEM((4, 64, 256), F32)],
        )
        pair_ring = swap(ring)
        own, pair, opposite = call(
            add_near_body,
            [f32, bf16, bf16],
            [mine, sib_near, from_right, from_left, from_pair],
            after=[pair_ring, left, right],
            nbytes=5 << 20,
        )
        sums = [own, left, right, step(opposite, 2), swap(pair)]
    with jax.named_scope("sum_weights"):
        quarter = call(weight_sum_body, block, [ring, pair_ring])
        shape = jax.ShapeDtypeStruct((128, 256), F32)
        grad_self, grad_neigh = call(
            functools.partial(weight_join_body, float(nodes) ** -0.5),
            [shape, shape],
            [quarter, *[hop_row(quarter, 0, -k) for k in (1, 2, 3)]],
            scratch=[VMEM((256, 256), F32)],
            nbytes=1 << 20,
        )
    with jax.named_scope("finish"):
        grad_features = call(
            finish_body,
            jax.ShapeDtypeStruct((1024, 128), BF16),
            [own_grad, *sums],
            nbytes=4 << 20,
        )
    return hidden, grad_features, grad_self, grad_neigh


def solution(mesh):
    placed = (
        P(("row", "col"), None),
        P(),
        P(),
        P(),
        P(("row", "col"), None),
        P("row", "col", None, None, None),
        P("row", "col", None, None),
        P("row", "col"),
    )
    return jax.shard_map(
        shards,
        mesh=mesh,
        in_specs=placed,
        out_specs=(P(("row", "col"), None), P(("row", "col"), None), P(), P()),
        check_vma=False,
    )
```
